32 devices in a mesh: rows: 4 (over x, core), feat: 8 (over z, y).
Axes of the slice: x: 2, y: 2, z: 4, core: 2. Of those that a mesh axis runs over, the one named last changes fastest.
Arguments:
- design: bfloat16 [3072, 65536], P('rows', 'feat'), may hold values from -0.0234375 to 0.0234375
- labels: int32 [64, 3072], P(None, 'rows'), may hold values from -1 to 1, as said below
- local_x: float32 [4, 64, 65536], P('rows', None, 'feat'), may hold values from -6 to 6
- dual_u: float32 [4, 64, 65536], P('rows', None, 'feat'), may hold values from -3 to 3
- consensus_z: float32 [64, 65536], P(None, 'feat'), may hold values from -6 to 6
- step_size: float32 [64], replicated, may hold values from 0.5 to 1
- rho: float32 [64], replicated, may hold values from 0.5 to 1.5
- penalty: float32 [64], replicated, may hold values from 0.5 to 4
Outputs:
- new_x: float32 [4, 64, 65536], P('rows', None, 'feat')
- new_z: float32 [64, 65536], P(None, 'feat')
- new_u: float32 [4, 64, 65536], P('rows', None, 'feat')
The draws below stay inside these ranges and needn't reach their ends.
Inputs may be any that keep to these rules, and one draw needn't show every extreme that they name: `labels`: each entry is -1 or 1.
All inputs are finite; a program needn't handle non-finite values.
Results may differ from the reference program's by a relative error of at most 0.0023.
Values may be sent and summed in bfloat16 or wider, within the bound.
No kernel may reach another device: no remote copies, remote signals or barrier semaphores. Data moves between devices by JAX's collectives and lax.ppermute only.
A program may use at most 64 MiB of HBM per device.

```python
import math
import jax
import jax.numpy as jnp
from jax import lax

F = 65536
K = 64
S_DEV = 768
SAMPLES = 3072
BLOCKS = 4
N_ROWS = 4


def draw_labels(key, part):
    return (2 * jax.random.randint(key, (K, SAMPLES), 0, 2) - 1).astype(jnp.int32)


def block_levels(stream_key, dims, pieces, smallest, largest):
    def one(position, parts):
        heights = jax.random.uniform(jax.random.fold_in(jax.random.fold_in(stream_key, 6), position), (parts,), jnp.float32, smallest / len(pieces), largest / len(pieces))
        return jnp.repeat(jnp.exp(heights), dims[position] // parts).reshape((-1,) + (1,) * (len(dims) - position - 1))

    factor_of = one(*pieces[0])
    for cut in pieces[1:]:
        factor_of = factor_of * one(*cut)
    return factor_of


def gaussian(key, shape, spread, bound, pieces=(), dtype=jnp.bfloat16):
    level = block_levels(key, shape, pieces, -0.22, 0.18) if pieces else 1.0
    values = jax.random.normal(key, shape, jnp.float32) * spread * level
    return jnp.minimum(jnp.maximum(values, -bound), bound).astype(dtype)


def setup_inputs(seed: int = 0) -> dict:
    seeds = jax.random.split(jax.random.key(seed), 9)
    return {
        "design": gaussian(seeds[0], (SAMPLES, F), (F ** -0.5), 0.0234375, ((0, 4), (1, 8))),
        "labels": draw_labels(jax.random.fold_in(seeds[8], 71), 0),
        "local_x": gaussian(seeds[2], (BLOCKS, K, F), 1.0, 6.0, ((0, 4), (2, 8)), jnp.float32),
        "dual_u": gaussian(seeds[3], (BLOCKS, K, F), 0.5, 3.0, ((0, 4), (2, 8)), jnp.float32),
        "consensus_z": gaussian(seeds[4], (K, F), 1.0, 6.0, ((1, 8),), jnp.float32),
        "step_size": jnp.clip(jnp.exp(jax.random.uniform(seeds[5], (K,), jnp.float32, math.log(0.5), math.log(1.0))), 0.5, 1.0),
        "rho": jnp.clip(jnp.exp(jax.random.uniform(seeds[6], (K,), jnp.float32, math.log(0.5), math.log(1.5))), 0.5, 1.5),
        "penalty": jnp.clip(jnp.exp(jax.random.uniform(seeds[7], (K,), jnp.float32, math.log(0.5), math.log(4.0))), 0.5, 4.0),
    }


def reference(design, labels, local_x, dual_u, consensus_z, step_size, rho, penalty):
    blocks = design.reshape(N_ROWS, S_DEV, F)
    signs = labels.reshape(K, N_ROWS, S_DEV).transpose(1, 0, 2).astype(jnp.float32)
    eta = step_size[:, None]
    weight = rho[:, None]

    def solve(item):
        rows_block, sign, x, u = item
        for turn in range(2):
            xb = x.astype(jnp.bfloat16)
            margin = lax.dot_general(xb, rows_block, (((1,), (1,)), ((), ())), preferred_element_type=jnp.float32)
            resid = (sign * jax.nn.sigmoid(-sign * margin)).astype(jnp.bfloat16)
            grad = jnp.dot(resid, rows_block, preferred_element_type=jnp.float32)
            x = x - eta * (weight * (x - consensus_z + u) - grad)
        return x

    new_x = lax.map(solve, (blocks, signs, local_x, dual_u))
    mean = jnp.sum(new_x + dual_u, axis=0) / N_ROWS
    limit = (penalty / (rho * N_ROWS))[:, None]
    new_z = mean - jnp.clip(mean, -limit, limit)
    new_u = dual_u + new_x - new_z[None]
    return new_x, new_z, new_u
```

```python
import jax
import jax.numpy as jnp
from jax import lax
from jax.sharding import PartitionSpec as P

CHUNKS = 4


def exchange(value, axis, mask):
    n = lax.axis_size(axis)
    return lax.ppermute(value, axis, [(i, i ^ mask) for i in range(n)])


def sum_over_rows(value, wire):
    n = lax.axis_size("rows")
    if n & (n - 1):
        return lax.psum(value, "rows")
    half = value.shape[1] // 2
    odd = (lax.axis_index("rows") & 1) == 1
    low, high = value[:, :half], value[:, half:]
    mine = jnp.where(odd, high, low)
    other = jnp.where(odd, low, high)
    mine = mine + exchange(other.astype(wire), "rows", 1).astype(jnp.float32)
    mask = 2
    while mask < n:
        sent = mine.astype(wire)
        mine = sent.astype(jnp.float32) + exchange(sent, "rows", mask).astype(jnp.float32)
        mask *= 2
    sent = mine.astype(wire)
    theirs = exchange(sent, "rows", 1).astype(jnp.float32)
    mine = sent.astype(jnp.float32)
    return jnp.concatenate(
        [jnp.where(odd, theirs, mine), jnp.where(odd, mine, theirs)], axis=1
    )


def per_device(design, labels, local_x, dual_u, consensus_z, step_size, rho, penalty):
    x0 = local_x[0]
    dual = dual_u[0]
    z = consensus_z
    tasks, width = x0.shape
    samples = design.shape[0]
    shards = lax.axis_size("feat")
    blocks_count = lax.axis_size("rows")
    part = tasks // shards
    sign = lax.dynamic_slice_in_dim(
        labels, lax.axis_index("feat") * part, part, 0
    ).astype(jnp.float32)
    eta = step_size[:, None]
    pull = eta * rho[:, None]
    keep = 1.0 - pull

    def residual(xb):
        partial = lax.dot_general(
            xb, design, (((1,), (1,)), ((), ())), preferred_element_type=jnp.float32
        )
        got = lax.all_to_all(partial.reshape(shards, part, samples), "feat", 0, 0)
        margin = jnp.sum(got, axis=0)
        resid = (sign * jax.nn.sigmoid(-sign * margin)).astype(jnp.bfloat16)
        spread = jnp.broadcast_to(resid[None], (shards, part, samples))
        return lax.all_to_all(spread, "feat", 0, 0).reshape(tasks, samples)

    start = sum_over_rows(x0 + dual, jnp.float32) / blocks_count

    resid1 = residual(x0.astype(jnp.bfloat16))
    grad1 = jnp.dot(resid1, design, preferred_element_type=jnp.float32)
    x1 = x0 - pull * (x0 - z + dual) + eta * grad1
    resid2 = residual(x1.astype(jnp.bfloat16))

    limit = (penalty / (rho * blocks_count))[:, None]
    step = width // CHUNKS
    xs, zs, us = [], [], []
    for c in range(CHUNKS):
        cut = slice(c * step, (c + 1) * step)
        grad2 = jnp.dot(resid2, design[:, cut], preferred_element_type=jnp.float32)
        x2 = x1[:, cut] - pull * (x1[:, cut] - z[:, cut] + dual[:, cut]) + eta * grad2
        pushed = sum_over_rows(eta * (keep * grad1[:, cut] + grad2), jnp.bfloat16) / blocks_count
        mean = keep * keep * start[:, cut] + pull * (1.0 + keep) * z[:, cut] + pushed
        new_z = mean - jnp.clip(mean, -limit, limit)
        xs.append(x2)
        zs.append(new_z)
        us.append(dual[:, cut] + x2 - new_z)
    cat = lambda parts: jnp.concatenate(parts, axis=1)
    return (cat(xs)[None], cat(zs), cat(us)[None])


def solution(mesh):
    in_specs = (
        P("rows", "feat"),
        P(None, "rows"),
        P("rows", None, "feat"),
        P("rows", None, "feat"),
        P(None, "feat"),
        P(),
        P(),
        P(),
    )
    out_specs = (P("rows", None, "feat"), P(None, "feat"), P("rows", None, "feat"))
    return jax.shard_map(
        per_device, mesh=mesh, in_specs=in_specs, out_specs=out_specs, check_vma=False
    )
```

```python
import functools

import jax
import jax.numpy as jnp
from jax import lax
from jax.experimental import pallas as pl
from jax.experimental.pallas import tpu as pltpu
from jax.sharding import PartitionSpec as P

BF16 = jnp.bfloat16
F32 = jnp.float32
CHUNKS = 4
PARAMS = pltpu.CompilerParams(vmem_limit_bytes=32 * 1024 * 1024)


def exchange(value, axis, mask):
    n = lax.axis_size(axis)
    return lax.ppermute(value, axis, [(i, i ^ mask) for i in range(n)])


def sum_over(value, axis, first=1):
    n = lax.axis_size(axis)
    mask = first
    total = value.astype(F32)
    while mask < n:
        sent = total.astype(value.dtype)
        total = sent.astype(F32) + exchange(sent, axis, mask).astype(F32)
        mask *= 2
    return total


def nt(a, b):
    return lax.dot_general(a, b, (((1,), (1,)), ((), ())), preferred_element_type=F32)


def cost(flops, nbytes):
    return pl.CostEstimate(flops=flops // 64, bytes_accessed=nbytes // 64, transcendentals=0)


def margin_kernel(x_ref, a_ref, out_ref, acc_ref):
    @pl.when(pl.program_id(0) == 0)
    def _():
        acc_ref[...] = jnp.zeros_like(acc_ref)

    acc_ref[...] += nt(x_ref[...].astype(BF16), a_ref[...])

    @pl.when(pl.program_id(0) == pl.num_programs(0) - 1)
    def _():
        out_ref[...] = acc_ref[...].astype(BF16)


def margins(x, design, block):
    tasks, width = x.shape
    samples = design.shape[0]
    return pl.pallas_call(
        margin_kernel,
        grid=(width // block,),
        in_specs=[
            pl.BlockSpec((tasks, block), lambda i: (0, i)),
            pl.BlockSpec((samples, block), lambda i: (0, i)),
        ],
        out_specs=pl.BlockSpec((tasks, samples), lambda i: (0, 0)),
        out_shape=jax.ShapeDtypeStruct((tasks, samples), BF16),
        scratch_shapes=[pltpu.VMEM((tasks, samples), F32)],
        compiler_params=PARAMS,
        cost_estimate=cost(2 * tasks * samples * width, 2 * samples * width + 4 * tasks * width),
        name="margins",
    )(x, design)


def turn_kernel(r_ref, eta_ref, pull_ref, x_ref, u_ref, z_ref, a_ref, q_ref, out_ref, acc_ref):
    @pl.when(pl.program_id(0) == 0)
    def _():
        acc_ref[...] = jnp.zeros_like(acc_ref)

    pull = pull_ref[...]
    push = eta_ref[...] * jnp.dot(r_ref[...], a_ref[...], preferred_element_type=F32)
    x = x_ref[...]
    x = x - pull * (x - z_ref[...] + u_ref[...]) + push
    q_ref[...] = (1.0 - pull) * push
    acc_ref[...] += nt(x.astype(BF16), a_ref[...])

    @pl.when(pl.program_id(0) == pl.num_programs(0) - 1)
    def _():
        out_ref[...] = acc_ref[...].astype(BF16)


def turn(resid, eta, pull, x, u, z, design, block):
    tasks, width = x.shape
    samples = design.shape[0]
    column = pl.BlockSpec((tasks, block), lambda i: (0, i))
    scale = pl.BlockSpec((tasks, 1), lambda i: (0, 0))
    whole = pl.BlockSpec((tasks, samples), lambda i: (0, 0))
    return pl.pallas_call(
        turn_kernel,
        grid=(width // block,),
        in_specs=[whole, scale, scale, column, column, column, pl.BlockSpec((samples, block), lambda i: (0, i))],
        out_specs=(column, whole),
        out_shape=(jax.ShapeDtypeStruct((tasks, width), F32), jax.ShapeDtypeStruct((tasks, samples), BF16)),
        scratch_shapes=[pltpu.VMEM((tasks, samples), F32)],
        compiler_params=PARAMS,
        cost_estimate=cost(4 * tasks * samples * width, 2 * samples * width + 16 * tasks * width),
        name="turn",
    )(resid, eta, pull, x, u, z, design)


def push_kernel(has_buffer, has_sum, *refs):
    refs = list(refs[1:])
    if has_buffer:
        refs.pop(0)
    r_ref, eta_ref, pull_ref, x_ref, u_ref, z_ref, q_ref, a_ref = refs[:8]
    rest = refs[8:]
    x_out, h_out = rest[-2:]
    keep = 1.0 - pull_ref[...]
    push = q_ref[...] + eta_ref[...] * jnp.dot(r_ref[...], a_ref[...], preferred_element_type=F32)
    u, z = u_ref[...], z_ref[...]
    x_out[...] = z - u + keep * keep * (x_ref[...] - z + u) + push
    if has_sum:
        push = push + rest[0][...].astype(F32)
    h_out[...] = push.astype(BF16)


def push(parity, buffer, resid, eta, pull, x, u, z, q, design, received, mine, chunk, count, block):
    tasks, width = x.shape
    samples = design.shape[0]
    chunk_width = width // 2 // count
    steps = chunk_width // block
    half_blocks = width // 2 // block

    def place(i, p):
        side = p[0] if mine else 1 - p[0]
        return (0, side * half_blocks + chunk * steps + i)

    column = pl.BlockSpec((tasks, block), place)
    local = pl.BlockSpec((tasks, block), lambda i, p: (0, i))
    scale = pl.BlockSpec((tasks, 1), lambda i, p: (0, 0))
    whole = pl.BlockSpec((tasks, samples), lambda i, p: (0, 0))
    in_specs = [whole, scale, scale, column, column, column, column, pl.BlockSpec((samples, block), place)]
    args = [resid, eta, pull, x, u, z, q, design]
    aliases = {}
    if buffer is not None:
        in_specs.insert(0, pl.BlockSpec(memory_space=pl.ANY))
        args.insert(0, buffer)
        aliases = {1: 0}
    if received is not None:
        in_specs.append(local)
        args.append(received)
    return pl.pallas_call(
        functools.partial(push_kernel, buffer is not None, received is not None),
        grid_spec=pltpu.PrefetchScalarGridSpec(
            num_scalar_prefetch=1,
            grid=(steps,),
            in_specs=in_specs,
            out_specs=(column, local),
        ),
        out_shape=(jax.ShapeDtypeStruct((tasks, width), F32), jax.ShapeDtypeStruct((tasks, chunk_width), BF16)),
        input_output_aliases=aliases,
        compiler_params=PARAMS,
        cost_estimate=cost(2 * tasks * samples * chunk_width, 2 * samples * chunk_width + 24 * tasks * chunk_width),
        name="push",
    )(parity, *args)


def final_kernel(blocks_count, has_buffers, *refs):
    refs = list(refs[1:])
    if has_buffers:
        refs = refs[2:]
    pull_ref, limit_ref, x_ref, u_ref, z_ref, s_mine, s_theirs, h_mine, h_theirs, z_out, u_out = refs
    pull, limit = pull_ref[...], limit_ref[...]
    keep = 1.0 - pull
    first = pl.program_id(0) == 0
    start = jnp.where(first, s_mine[...], s_theirs[...])
    pushed = jnp.where(first, h_mine[...].astype(F32), h_theirs[...].astype(F32))
    mean = (keep * keep * start + pushed) * (1.0 / blocks_count) + pull * (1.0 + keep) * z_ref[...]
    new_z = mean - jnp.clip(mean, -limit, limit)
    z_out[...] = new_z
    u_out[...] = u_ref[...] + x_ref[...] - new_z


def final(parity, buffers, pull, limit, x, u, z, starts, pushes, chunk, count, blocks_count):
    tasks, width = x.shape
    block = width // 2 // count
    half_blocks = count

    def place(i, p):
        return (0, (p[0] + i - 2 * p[0] * i) * half_blocks + chunk)

    column = pl.BlockSpec((tasks, block), place)
    half = pl.BlockSpec((tasks, block), lambda i, p: (0, chunk))
    local = pl.BlockSpec((tasks, block), lambda i, p: (0, 0))
    scale = pl.BlockSpec((tasks, 1), lambda i, p: (0, 0))
    in_specs = [scale, scale, column, column, column, half, half, local, local]
    args = [pull, limit, x, u, z, *starts, *pushes]
    aliases = {}
    if buffers is not None:
        in_specs = [pl.BlockSpec(memory_space=pl.ANY)] * 2 + in_specs
        args = list(buffers) + args
        aliases = {1: 0, 2: 1}
    out = jax.ShapeDtypeStruct((tasks, width), F32)
    return pl.pallas_call(
        functools.partial(final_kernel, blocks_count, buffers is not None),
        grid_spec=pltpu.PrefetchScalarGridSpec(
            num_scalar_prefetch=1, grid=(2,), in_specs=in_specs, out_specs=(column, column)
        ),
        out_shape=(out, out),
        input_output_aliases=aliases,
        compiler_params=PARAMS,
        cost_estimate=cost(20 * tasks * block, 60 * tasks * block),
        name="final",
    )(parity, *args)


def per_device(design, labels, local_x, dual_u, consensus_z, step_size, rho, penalty):
    x0 = local_x[0]
    dual = dual_u[0]
    z = consensus_z
    tasks, width = x0.shape
    half = width // 2
    blocks_count = lax.axis_size("rows")
    side = lax.axis_index("rows") & 1
    parity = side.astype(jnp.int32)[None]
    sign = labels.astype(F32)
    eta = step_size[:, None]
    pull = eta * rho[:, None]
    limit = (penalty / (rho * blocks_count))[:, None]

    def residual(margin):
        return (sign * jax.nn.sigmoid(-sign * margin)).astype(BF16)

    def side_of(which):
        cut = lambda v: lax.dynamic_slice_in_dim(v, which * half, half, 1)
        return cut(x0) + cut(dual)

    margin1 = margins(x0, design, 1024)
    margin1, here = lax.optimization_barrier((margin1, side))
    start_mine = side_of(here) + exchange(side_of(1 - here), "rows", 1)
    resid1 = residual(sum_over(margin1, "feat"))
    resid1, start_mine = lax.optimization_barrier((resid1, start_mine))

    carried, margin2 = turn(resid1, eta, pull, x0, dual, z, design, 1024)
    start_mine = sum_over(start_mine, "rows", 2)
    resid2 = residual(sum_over(margin2, "feat"))
    resid2, start_mine = lax.optimization_barrier((resid2, start_mine))
    start_theirs = exchange(start_mine, "rows", 1)

    new_x = None
    args = (resid2, eta, pull, x0, dual, z, carried, design)
    block = min(1024, half // CHUNKS)
    received = []
    pieces = []
    for c in range(CHUNKS + 1):
        if c < CHUNKS:
            new_x, other = push(parity, new_x, *args, None, False, c, CHUNKS, block)
            received.append(exchange(other, "rows", 1))
        if c > 0:
            new_x, mine = push(parity, new_x, *args, received[c - 1], True, c - 1, CHUNKS, block)
            pieces.append(sum_over(mine, "rows", 2).astype(BF16))
    results = None
    for c in range(CHUNKS):
        piece = pieces[c]
        if results is not None:
            piece, results = lax.optimization_barrier((piece, results))
        pushes = (piece, exchange(piece, "rows", 1))
        results = final(
            parity, results, pull, limit, new_x, dual, z, (start_mine, start_theirs), pushes, c, CHUNKS, blocks_count
        )
    new_z, new_u = results
    return (new_x[None], new_z, new_u[None])


def solution(mesh):
    in_specs = (
        P("rows", "feat"),
        P(None, "rows"),
        P("rows", None, "feat"),
        P("rows", None, "feat"),
        P(None, "feat"),
        P(),
        P(),
        P(),
    )
    out_specs = (P("rows", None, "feat"), P(None, "feat"), P("rows", None, "feat"))
    return jax.shard_map(
        per_device, mesh=mesh, in_specs=in_specs, out_specs=out_specs, check_vma=False
    )
```

```python
import functools

import jax
import jax.numpy as jnp
from jax import lax
from jax.experimental import pallas as pl
from jax.experimental.pallas import tpu as pltpu
from jax.sharding import PartitionSpec as P

BF16 = jnp.bfloat16
F32 = jnp.float32
CHUNKS = 4
STEP = 1024
HBM = pl.BlockSpec(memory_space=pltpu.HBM)
VMEM = pl.BlockSpec(memory_space=pltpu.VMEM)
SMEM = pl.BlockSpec(memory_space=pltpu.SMEM)


def exchange(value, axis, mask):
    n = lax.axis_size(axis)
    return lax.ppermute(value, axis, [(i, i ^ mask) for i in range(n)])


def doubling(value, axis, first=1):
    n = lax.axis_size(axis)
    mask = first
    other = exchange(value, axis, mask)
    while 2 * mask < n:
        mask *= 2
        value = (value.astype(F32) + other.astype(F32)).astype(value.dtype)
        other = exchange(value, axis, mask)
    return value, other


def nt(a, b):
    return lax.dot_general(a, b, (((1,), (1,)), ((), ())), preferred_element_type=F32)


def call(kernel, name, in_specs, out_shape, out_specs, scratch=(), aliases=None, limit=16, work=1000):
    return pl.pallas_call(
        kernel,
        in_specs=in_specs,
        out_shape=out_shape,
        out_specs=out_specs,
        scratch_shapes=list(scratch),
        input_output_aliases=aliases or {},
        compiler_params=pltpu.CompilerParams(vmem_limit_bytes=limit * 1024 * 1024),
        cost_estimate=pl.CostEstimate(flops=work, bytes_accessed=work, transcendentals=0),
        name=name,
    )


def pin(space, *values):
    return [pltpu.with_memory_space_constraint(v, space) for v in values]


def columns(start, size):
    return pl.ds(pl.multiple_of(start, 128), size)


def load_kernel(side, x_hbm, u_hbm, z_hbm, a_hbm, m_out, a_out, x_out, u_out, z_out, mine_out, other_out, acc, sems):
    width = x_hbm.shape[1]
    steps = width // STEP

    def pair(j):
        cut = columns(j * STEP, STEP)
        return (
            pltpu.make_async_copy(x_hbm.at[:, cut], x_out.at[:, cut], sems.at[0, j]),
            pltpu.make_async_copy(a_hbm.at[:, cut], a_out.at[:, cut], sems.at[1, j]),
        )

    rest = (
        pltpu.make_async_copy(u_hbm, u_out, sems.at[2, 0]),
        pltpu.make_async_copy(z_hbm, z_out, sems.at[2, 1]),
    )
    for j in range(steps):
        for copy in pair(j):
            copy.start()
    for copy in rest:
        copy.start()
    acc[...] = jnp.zeros_like(acc)

    @pl.loop(0, steps)
    def _(j):
        for copy in pair(j):
            copy.wait()
        cut = columns(j * STEP, STEP)
        acc[...] += nt(x_out[:, cut].astype(BF16), a_out[:, cut])

    m_out[...] = acc[...].astype(BF16)
    for copy in rest:
        copy.wait()
    half = width // 2
    mine = columns(side[0] * half, half)
    other = columns((1 - side[0]) * half, half)
    mine_out[...] = x_out[:, mine] + u_out[:, mine]
    other_out[...] = x_out[:, other] + u_out[:, other]


def load(side, x, u, z, design):
    tasks, width = x.shape
    samples = design.shape[0]
    steps = width // STEP
    full = pltpu.VMEM((tasks, width), F32)
    half = pltpu.VMEM((tasks, width // 2), F32)
    return call(
        load_kernel,
        "load_and_margins",
        [SMEM] + [HBM] * 4,
        (pltpu.VMEM((tasks, samples), BF16), pltpu.VMEM(design.shape, BF16), full, full, full, half, half),
        [VMEM] * 7,
        [pltpu.VMEM((tasks, samples), F32), pltpu.SemaphoreType.DMA((3, max(steps, 2)))],
    )(side, *pin(pltpu.HBM, x, u, z, design))


def residual(sign, own, other):
    margin = own.astype(F32) + other.astype(F32)
    sign = sign.astype(F32)
    return (sign * jax.nn.sigmoid(-sign * margin)).astype(BF16)


def turn_kernel(sign, own, other, scale, x_ref, u_ref, z_ref, a_ref, q_out, m_out, resid, acc):
    resid[...] = residual(sign[...], own[...], other[...])
    acc[...] = jnp.zeros_like(acc)
    eta, pull = scale[:, 0:1], scale[:, 1:2]

    @pl.loop(0, x_ref.shape[1] // STEP)
    def _(j):
        cut = columns(j * STEP, STEP)
        push = eta * jnp.dot(resid[...], a_ref[:, cut], preferred_element_type=F32)
        x = x_ref[:, cut]
        x = x - pull * (x - z_ref[:, cut] + u_ref[:, cut]) + push
        q_out[:, cut] = (1.0 - pull) * push
        acc[...] += nt(x.astype(BF16), a_ref[:, cut])

    m_out[...] = acc[...].astype(BF16)


def turn(sign, pair, scale, x, u, z, design):
    tasks, width = x.shape
    samples = design.shape[0]
    return call(
        turn_kernel,
        "turn",
        [VMEM] * 8,
        (pltpu.VMEM((tasks, width), F32), pltpu.VMEM((tasks, samples), BF16)),
        [VMEM] * 2,
        [pltpu.VMEM((tasks, samples), BF16), pltpu.VMEM((tasks, samples), F32)],
    )(*pin(pltpu.VMEM, sign, *pair, scale, x, u, z, design))


def push_kernel(mine, chunk, size, side, sign, own, other, scale, q_ref, a_ref, *rest):
    received = rest[0] if mine else None
    h_out, sent_out = rest[-2:]
    half = q_ref.shape[1] // 2
    eta = scale[:, 0:1]
    resid = residual(sign[...], own[...], other[...])
    base = (side[0] if mine else 1 - side[0]) * half + chunk * size
    step = min(STEP, size)
    for j in range(size // step):
        cut = columns(base + j * step, step)
        here = pl.ds(j * step, step)
        push = q_ref[:, cut] + eta * jnp.dot(resid, a_ref[:, cut], preferred_element_type=F32)
        h_out[:, here] = push
        if mine:
            push = push + received[:, here].astype(F32)
        sent_out[:, here] = push.astype(BF16)


def push(side, sign, pair, scale, q, design, received, chunk, size):
    tasks = q.shape[0]
    mine = received is not None
    args = [sign, *pair, scale, q, design] + ([received] if mine else [])
    return call(
        functools.partial(push_kernel, mine, chunk, size),
        "push_mine" if mine else "push_other",
        [SMEM] + [VMEM] * len(args),
        (pltpu.VMEM((tasks, size), F32), pltpu.VMEM((tasks, size), BF16)),
        [VMEM] * 2,
    )(side, *pin(pltpu.VMEM, *args))


def final_kernel(blocks_count, chunk, size, buffered, side, scale, x_ref, u_ref, z_ref, *rest):
    starts, hs, pushes = rest[0:2], rest[2:4], rest[4:6]
    outs = rest[6 + 3 * buffered : 9 + 3 * buffered]
    stage, sems = rest[-2:]
    half = x_ref.shape[1] // 2
    pull, limit = scale[:, 1:2], scale[:, 2:3]
    keep = 1.0 - pull
    copies = []
    for k in range(2):
        base = (side[0] if k == 0 else 1 - side[0]) * half + chunk * size
        cut = columns(base, size)
        u, z = u_ref[:, cut], z_ref[:, cut]
        new_x = z - u + keep * keep * (x_ref[:, cut] - z + u) + hs[k][...]
        start = starts[k][:, pl.ds(chunk * size, size)]
        mean = (keep * keep * start + pushes[k][...].astype(F32)) * (1.0 / blocks_count) + pull * (1.0 + keep) * z
        new_z = mean - jnp.clip(mean, -limit, limit)
        for o, value in enumerate((new_x, new_z, u + new_x - new_z)):
            stage[k, o] = value
            copy = pltpu.make_async_copy(stage.at[k, o], outs[o].at[:, cut], sems.at[k, o])
            copy.start()
            copies.append(copy)
    for copy in copies:
        copy.wait()


def final(side, scale, x, u, z, starts, hs, pushes, buffers, chunk, size, blocks_count):
    tasks, width = x.shape
    buffered = buffers is not None
    args = pin(pltpu.VMEM, scale, x, u, z, *starts, *hs, *pushes)
    out = pltpu.HBM((tasks, width), F32)
    aliases = {}
    if buffered:
        aliases = {1 + len(args) + o: o for o in range(3)}
        args += pin(pltpu.HBM, *buffers)
    return call(
        functools.partial(final_kernel, blocks_count, chunk, size, buffered),
        "final",
        [SMEM] + [VMEM] * 10 + [HBM] * (3 * buffered),
        (out, out, out),
        [HBM] * 3,
        [pltpu.VMEM((2, 3, tasks, size), F32), pltpu.SemaphoreType.DMA((2, 3))],
        aliases,
    )(side, *args)


def per_device(design, labels, local_x, dual_u, consensus_z, step_size, rho, penalty):
    tasks, width = consensus_z.shape
    blocks_count = lax.axis_size("rows")
    side = (lax.axis_index("rows") & 1).astype(jnp.int32)[None]
    scale = jnp.stack([step_size, step_size * rho, penalty / (rho * blocks_count)], axis=1)

    margin1, design, x0, dual, z, start_mine, start_other = load(side, local_x[0], dual_u[0], consensus_z, design)
    start_mine = start_mine + exchange(start_other, "rows", 1)
    pair = doubling(margin1, "feat")
    pair, start_mine = lax.optimization_barrier((pair, start_mine))

    carried, margin2 = turn(labels, pair, scale, x0, dual, z, design)
    pair = doubling(margin2, "feat")
    mask = 2
    while mask < blocks_count:
        start_mine = start_mine + exchange(start_mine, "rows", mask)
        mask *= 2
    pair, start_mine = lax.optimization_barrier((pair, start_mine))
    start_theirs = exchange(start_mine, "rows", 1)

    size = width // 2 // CHUNKS
    args = (side, labels, pair, scale, carried, design)
    others, mines, received, pieces = [], [], [], []
    for c in range(CHUNKS + 1):
        if c < CHUNKS:
            value, other = push(*args, None, c, size)
            others.append(value)
            received.append(exchange(other, "rows", 1))
        if c > 0:
            value, mine = push(*args, received[c - 1], c - 1, size)
            mines.append(value)
            a, b = doubling(mine, "rows", 2)
            pieces.append((a.astype(F32) + b.astype(F32)).astype(BF16))
    results = None
    for c in range(CHUNKS):
        piece = pieces[c]
        if results is not None:
            piece, results = lax.optimization_barrier((piece, results))
        pushes = (piece, exchange(piece, "rows", 1))
        results = final(
            side, scale, x0, dual, z, (start_mine, start_theirs), (mines[c], others[c]), pushes, results, c, size, blocks_count
        )
    new_x, new_z, new_u = results
    return (new_x[None], new_z, new_u[None])


def solution(mesh):
    in_specs = (
        P("rows", "feat"),
        P(None, "rows"),
        P("rows", None, "feat"),
        P("rows", None, "feat"),
        P(None, "feat"),
        P(),
        P(),
        P(),
    )
    out_specs = (P("rows", None, "feat"), P(None, "feat"), P("rows", None, "feat"))
    return jax.shard_map(
        per_device, mesh=mesh, in_specs=in_specs, out_specs=out_specs, check_vma=False
    )
```

```python
import functools
import math

import jax
import jax.numpy as jnp
from jax import lax
from jax.experimental import pallas as pl
from jax.experimental.pallas import tpu as pltpu
from jax.sharding import PartitionSpec as P

BF16 = jnp.bfloat16
F32 = jnp.float32
EIGHTHS = (3, 3, 2)
STEP = 1024
AHEAD = 3
HBM = pl.BlockSpec(memory_space=pltpu.HBM)
VMEM = pl.BlockSpec(memory_space=pltpu.VMEM)
SMEM = pl.BlockSpec(memory_space=pltpu.SMEM)


def exchange(value, axis, mask):
    n = lax.axis_size(axis)
    return lax.ppermute(value, axis, [(i, i ^ mask) for i in range(n)])


def doubling(value, axis, first=1, other=None):
    n = lax.axis_size(axis)
    mask = first
    if other is None:
        other = exchange(value, axis, mask)
    while 2 * mask < n:
        mask *= 2
        value = (value.astype(F32) + other.astype(F32)).astype(value.dtype)
        other = exchange(value, axis, mask)
    return value, other


def nt(a, b):
    return lax.dot_general(a, b, (((1,), (1,)), ((), ())), preferred_element_type=F32)


def call(kernel, name, in_specs, out_shape, out_specs, scratch=(), aliases=None, limit=16, work=1000):
    return pl.pallas_call(
        kernel,
        in_specs=in_specs,
        out_shape=out_shape,
        out_specs=out_specs,
        scratch_shapes=list(scratch),
        input_output_aliases=aliases or {},
        compiler_params=pltpu.CompilerParams(vmem_limit_bytes=limit * 1024 * 1024),
        cost_estimate=pl.CostEstimate(flops=work, bytes_accessed=work, transcendentals=0),
        name=name,
    )


def pin(space, *values):
    return [pltpu.with_memory_space_constraint(v, space) for v in values]


def columns(start, size):
    return pl.ds(pl.multiple_of(start, 128), size)


def load_kernel(side, x_hbm, u_hbm, a_hbm, m_out, a_out, x_out, u_out, mine_out, other_out, acc, sems):
    width = x_hbm.shape[1]
    steps = width // STEP

    def pair(j):
        cut = columns(j * STEP, STEP)
        return (
            pltpu.make_async_copy(x_hbm.at[:, cut], x_out.at[:, cut], sems.at[0, j]),
            pltpu.make_async_copy(a_hbm.at[:, cut], a_out.at[:, cut], sems.at[1, j]),
        )

    def begin(j):
        for copy in pair(j):
            copy.start()

    dual = pltpu.make_async_copy(u_hbm, u_out, sems.at[2, 0])
    for j in range(min(AHEAD, steps)):
        begin(j)
    acc[...] = jnp.zeros_like(acc)

    @pl.loop(0, steps)
    def _(j):
        for copy in pair(j):
            copy.wait()

        @pl.when(j + AHEAD < steps)
        def _():
            begin(j + AHEAD)

        @pl.when(j == max(steps - AHEAD, 0))
        def _():
            dual.start()

        cut = columns(j * STEP, STEP)
        acc[...] += nt(x_out[:, cut].astype(BF16), a_out[:, cut])

    m_out[...] = acc[...].astype(BF16)
    dual.wait()
    half = width // 2
    mine = columns(side[0] * half, half)
    other = columns((1 - side[0]) * half, half)
    mine_out[...] = x_out[:, mine] + u_out[:, mine]
    other_out[...] = x_out[:, other] + u_out[:, other]


def load(side, x, u, design):
    tasks, width = x.shape
    samples = design.shape[0]
    full = pltpu.VMEM((tasks, width), F32)
    half = pltpu.VMEM((tasks, width // 2), F32)
    return call(
        load_kernel,
        "load_and_margins",
        [SMEM] + [HBM] * 3,
        (pltpu.VMEM((tasks, samples), BF16), pltpu.VMEM(design.shape, BF16), full, full, half, half),
        [VMEM] * 6,
        [pltpu.VMEM((tasks, samples), F32), pltpu.SemaphoreType.DMA((3, width // STEP))],
    )(side, *pin(pltpu.HBM, x, u, design))


def rest_kernel(blocks_count, z_hbm, sign_hbm, eta_hbm, rho_hbm, lam_hbm, *refs):
    z_out, sign_out, scale_out, eta_row, rho_row, lam_row, sems = refs
    pairs = ((eta_hbm, eta_row), (rho_hbm, rho_row), (lam_hbm, lam_row), (z_hbm, z_out), (sign_hbm, sign_out))
    copies = [pltpu.make_async_copy(a, b, sems.at[k]) for k, (a, b) in enumerate(pairs)]
    for copy in copies:
        copy.start()
    for copy in copies[:3]:
        copy.wait()
    tasks = z_out.shape[0]
    one = lax.broadcasted_iota(jnp.int32, (tasks, tasks), 0) == lax.broadcasted_iota(jnp.int32, (tasks, tasks), 1)
    eta, rho, lam = eta_row[...], rho_row[...], lam_row[...]
    for k, row in enumerate((eta, eta * rho, lam / (rho * blocks_count))):
        upright = jnp.where(one, jnp.broadcast_to(row, (tasks, tasks)), 0.0)
        scale_out[:, k : k + 1] = jnp.sum(upright, axis=1, keepdims=True)
    for copy in copies[3:]:
        copy.wait()


def load_rest(z, sign, step_size, rho, penalty, blocks_count):
    tasks, width = z.shape
    rows = [v.reshape(1, tasks) for v in (step_size, rho, penalty)]
    return call(
        functools.partial(rest_kernel, blocks_count),
        "load_rest",
        [HBM] * 5,
        (pltpu.VMEM((tasks, width), F32), pltpu.VMEM(sign.shape, jnp.int32), pltpu.VMEM((tasks, 128), F32)),
        [VMEM] * 3,
        [pltpu.VMEM((1, tasks), F32)] * 3 + [pltpu.SemaphoreType.DMA((5,))],
    )(*pin(pltpu.HBM, z, sign, *rows))


def residual(sign, own, other):
    margin = own.astype(F32) + other.astype(F32)
    sign = sign.astype(F32)
    return (sign * jax.nn.sigmoid(-sign * margin)).astype(BF16)


def turn_kernel(sign, own, other, scale, x_ref, u_ref, z_ref, a_ref, q_out, m_out, resid, acc):
    resid[...] = residual(sign[...], own[...], other[...])
    acc[...] = jnp.zeros_like(acc)
    eta, pull = scale[:, 0:1], scale[:, 1:2]

    @pl.loop(0, x_ref.shape[1] // STEP)
    def _(j):
        cut = columns(j * STEP, STEP)
        push = eta * jnp.dot(resid[...], a_ref[:, cut], preferred_element_type=F32)
        x = x_ref[:, cut]
        x = x - pull * (x - z_ref[:, cut] + u_ref[:, cut]) + push
        q_out[:, cut] = (1.0 - pull) * push
        acc[...] += nt(x.astype(BF16), a_ref[:, cut])

    m_out[...] = acc[...].astype(BF16)


def turn(sign, pair, scale, x, u, z, design):
    tasks, width = x.shape
    samples = design.shape[0]
    return call(
        turn_kernel,
        "turn",
        [VMEM] * 8,
        (pltpu.VMEM((tasks, width), F32), pltpu.VMEM((tasks, samples), BF16)),
        [VMEM] * 2,
        [pltpu.VMEM((tasks, samples), BF16), pltpu.VMEM((tasks, samples), F32)],
    )(*pin(pltpu.VMEM, sign, *pair, scale, x, u, z, design))


def push_kernel(mine, begin, size, side, sign, own, other, scale, q_ref, a_ref, *rest):
    received = rest[0] if mine else None
    h_out, sent_out = rest[-2:]
    half = q_ref.shape[1] // 2
    eta = scale[:, 0:1]
    resid = residual(sign[...], own[...], other[...])
    base = (side[0] if mine else 1 - side[0]) * half + begin
    step = math.gcd(512, size)
    for j in range(size // step):
        cut = columns(base + j * step, step)
        here = pl.ds(j * step, step)
        push = q_ref[:, cut] + eta * jnp.dot(resid, a_ref[:, cut], preferred_element_type=F32)
        h_out[:, here] = push
        if mine:
            push = push + received[:, here].astype(F32)
        sent_out[:, here] = push.astype(BF16)


def push(side, sign, pair, scale, q, design, received, begin, size):
    tasks = q.shape[0]
    mine = received is not None
    args = [sign, *pair, scale, q, design] + ([received] if mine else [])
    return call(
        functools.partial(push_kernel, mine, begin, size),
        "push_mine" if mine else "push_other",
        [SMEM] + [VMEM] * len(args),
        (pltpu.VMEM((tasks, size), F32), pltpu.VMEM((tasks, size), BF16)),
        [VMEM] * 2,
    )(side, *pin(pltpu.VMEM, *args))


def store_kernel(sizes, side, scale, x_ref, u_ref, z_ref, *rest):
    count = len(sizes)
    hs = (rest[:count], rest[count : 2 * count])
    x_out, stage, sems = rest[2 * count :]
    half = x_ref.shape[1] // 2
    keep = 1.0 - scale[:, 1:2]
    copies = []
    for k in range(2):
        begin = 0
        for c, size in enumerate(sizes):
            cut = columns((side[0] if k == 0 else 1 - side[0]) * half + begin, size)
            u, z = u_ref[:, cut], z_ref[:, cut]
            stage[:, cut] = z - u + keep * keep * (x_ref[:, cut] - z + u) + hs[k][c][...]
            copy = pltpu.make_async_copy(stage.at[:, cut], x_out.at[:, cut], sems.at[k, c])
            copy.start()
            copies.append(copy)
            begin += size
    for copy in copies:
        copy.wait()


def store_x(side, scale, x, u, z, mines, others, sizes):
    tasks, width = x.shape
    return call(
        functools.partial(store_kernel, sizes),
        "store_x",
        [SMEM] + [VMEM] * (4 + 2 * len(sizes)),
        pltpu.HBM((tasks, width), F32),
        HBM,
        [pltpu.VMEM((tasks, width), F32), pltpu.SemaphoreType.DMA((2, len(sizes)))],
    )(side, *pin(pltpu.VMEM, scale, x, u, z, *mines, *others))


def final_kernel(blocks_count, begin, size, buffered, side, scale, x_ref, u_ref, z_ref, *rest):
    starts, hs, pushes = rest[0:2], rest[2:4], rest[4:6]
    outs = rest[6 + 2 * buffered : 8 + 2 * buffered]
    stage, sems = rest[-2:]
    half = x_ref.shape[1] // 2
    pull, limit = scale[:, 1:2], scale[:, 2:3]
    keep = 1.0 - pull
    copies = []
    for k in range(2):
        cut = columns((side[0] if k == 0 else 1 - side[0]) * half + begin, size)
        z = z_ref[:, cut]
        start = starts[k][:, pl.ds(begin, size)]
        mean = (keep * keep * start + pushes[k][...].astype(F32)) * (1.0 / blocks_count) + pull * (1.0 + keep) * z
        new_z = mean - jnp.clip(mean, -limit, limit)
        moved = z + keep * keep * (x_ref[:, cut] - z + u_ref[:, cut]) + hs[k][...]
        for o, value in enumerate((new_z, moved - new_z)):
            stage[k, o] = value
            copy = pltpu.make_async_copy(stage.at[k, o], outs[o].at[:, cut], sems.at[k, o])
            copy.start()
            copies.append(copy)
    for copy in copies:
        copy.wait()


def final(side, scale, x, u, z, starts, hs, pushes, buffers, begin, size, blocks_count):
    tasks, width = x.shape
    buffered = buffers is not None
    args = pin(pltpu.VMEM, scale, x, u, z, *starts, *hs, *pushes)
    out = pltpu.HBM((tasks, width), F32)
    aliases = {}
    if buffered:
        aliases = {1 + len(args) + o: o for o in range(2)}
        args += pin(pltpu.HBM, *buffers)
    return call(
        functools.partial(final_kernel, blocks_count, begin, size, buffered),
        "final",
        [SMEM] + [VMEM] * 10 + [HBM] * (2 * buffered),
        (out, out),
        [HBM] * 2,
        [pltpu.VMEM((2, 2, tasks, size), F32), pltpu.SemaphoreType.DMA((2, 2))],
        aliases,
    )(side, *args)


def tie(value, *after):
    return lax.optimization_barrier((value, after))[0]


def per_device(design, labels, local_x, dual_u, consensus_z, step_size, rho, penalty):
    tasks, width = consensus_z.shape
    half = width // 2
    blocks_count = lax.axis_size("rows")
    side = (lax.axis_index("rows") & 1).astype(jnp.int32)[None]

    margin1, design, x0, dual, start_mine, start_other = load(side, local_x[0], dual_u[0], design)
    start_mine = start_mine + exchange(start_other, "rows", 1)
    other = exchange(margin1, "feat", 1)
    z, sign, scale = load_rest(consensus_z, labels, tie(step_size, other), rho, penalty, blocks_count)
    pair = doubling(margin1, "feat", 1, other)
    pair = tie(pair, start_mine)

    carried, margin2 = turn(sign, pair, scale, x0, dual, z, design)
    pair = doubling(margin2, "feat")
    mask = 2
    while mask < blocks_count:
        start_mine = start_mine + exchange(start_mine, "rows", mask)
        mask *= 2
    pair = tie(pair, start_mine)
    start_theirs = exchange(start_mine, "rows", 1)

    sizes = [half * part // sum(EIGHTHS) for part in EIGHTHS]
    begins = [sum(sizes[:c]) for c in range(len(sizes))]
    count = len(sizes)
    args = (sign, pair, scale, carried, design)
    others, mines, received, sums = [], [], [], []
    token = side
    for c in range(count + 1):
        if c < count:
            value, other = push(token, *args, None, begins[c], sizes[c])
            others.append(value)
            received.append(exchange(other, "rows", 1))
        if c > 0:
            value, sent = push(token, *args, received[c - 1], begins[c - 1], sizes[c - 1])
            mines.append(value)
            sums.append(doubling(sent, "rows", 2))
            token = tie(side, sent)
    new_x = store_x(side, scale, x0, dual, z, mines, others, sizes)

    results, pushes = None, []
    for c in range(count + 1):
        if c < count:
            a, b = sums[c]
            if c == 0:
                b = tie(b, new_x)
            if c > 1:
                b = tie(b, results)
            piece = (a.astype(F32) + b.astype(F32)).astype(BF16)
            pushes.append((piece, exchange(piece, "rows", 1)))
        if c > 0:
            results = final(
                side, scale, x0, dual, z, (start_mine, start_theirs), (mines[c - 1], others[c - 1]), pushes[c - 1],
                results, begins[c - 1], sizes[c - 1], blocks_count,
            )
    new_z, new_u = results
    return (new_x[None], new_z, new_u[None])


def solution(mesh):
    in_specs = (
        P("rows", "feat"),
        P(None, "rows"),
        P("rows", None, "feat"),
        P("rows", None, "feat"),
        P(None, "feat"),
        P(),
        P(),
        P(),
    )
    out_specs = (P("rows", None, "feat"), P(None, "feat"), P("rows", None, "feat"))
    return jax.shard_map(
        per_device, mesh=mesh, in_specs=in_specs, out_specs=out_specs, check_vma=False
    )
```

```python
import functools
import math

import jax
import jax.numpy as jnp
from jax import lax
from jax.experimental import pallas as pl
from jax.experimental.pallas import tpu as pltpu
from jax.sharding import PartitionSpec as P

BF16 = jnp.bfloat16
F32 = jnp.float32
EIGHTHS = (2, 4, 2)
STEP = 1024
AHEAD = 4
NARROW = 256
HBM = pl.BlockSpec(memory_space=pltpu.HBM)
VMEM = pl.BlockSpec(memory_space=pltpu.VMEM)
SMEM = pl.BlockSpec(memory_space=pltpu.SMEM)


def exchange(value, axis, mask):
    n = lax.axis_size(axis)
    return lax.ppermute(value, axis, [(i, i ^ mask) for i in range(n)])


def doubling(value, axis, first=1):
    n = lax.axis_size(axis)
    mask = first
    other = exchange(value, axis, mask)
    while 2 * mask < n:
        mask *= 2
        value = (value.astype(F32) + other.astype(F32)).astype(value.dtype)
        other = exchange(value, axis, mask)
    return value, other


def feat_orders():
    n = lax.axis_size("feat")
    masks = [1 << k for k in range(n.bit_length() - 1)]
    return list(zip(masks[:1] + masks[:0:-1], masks[1:2] + masks[:1] + masks[2:]))


def feat_exchange(value, pair):
    n = lax.axis_size("feat")
    moves = [(r * n + f, r * n + (f ^ pair[r & 1])) for r in range(lax.axis_size("rows")) for f in range(n)]
    return lax.ppermute(value, ("rows", "feat"), moves)


def feat_doubling(value, other=None):
    pairs = feat_orders()
    for k, pair in enumerate(pairs):
        if k > 0:
            value = (value.astype(F32) + other.astype(F32)).astype(value.dtype)
        if k > 0 or other is None:
            other = feat_exchange(value, pair)
    return value, other


def nt(a, b):
    return lax.dot_general(a, b, (((1,), (1,)), ((), ())), preferred_element_type=F32)


def call(kernel, name, in_specs, out_shape, out_specs, scratch=(), aliases=None, limit=16, work=1000):
    return pl.pallas_call(
        kernel,
        in_specs=in_specs,
        out_shape=out_shape,
        out_specs=out_specs,
        scratch_shapes=list(scratch),
        input_output_aliases=aliases or {},
        compiler_params=pltpu.CompilerParams(vmem_limit_bytes=limit * 1024 * 1024),
        cost_estimate=pl.CostEstimate(flops=work, bytes_accessed=work, transcendentals=0),
        name=name,
    )


def pin(space, *values):
    return [pltpu.with_memory_space_constraint(v, space) for v in values]


def columns(start, size):
    return pl.ds(pl.multiple_of(start, 128), size)


def load_kernel(side, x_hbm, u_hbm, a_hbm, m_out, a_out, x_out, u_out, mine_out, other_out, acc, sems):
    width = x_hbm.shape[1]
    steps = width // STEP

    def pair(j):
        cut = columns(j * STEP, STEP)
        return (
            pltpu.make_async_copy(x_hbm.at[:, cut], x_out.at[:, cut], sems.at[0, j]),
            pltpu.make_async_copy(a_hbm.at[:, cut], a_out.at[:, cut], sems.at[1, j]),
        )

    def begin(j):
        for copy in pair(j):
            copy.start()

    dual = pltpu.make_async_copy(u_hbm, u_out, sems.at[2, 0])
    for j in range(min(AHEAD, steps)):
        begin(j)
    acc[...] = jnp.zeros_like(acc)

    @pl.loop(0, steps)
    def _(j):
        for copy in pair(j):
            copy.wait()

        @pl.when(j + AHEAD < steps)
        def _():
            begin(j + AHEAD)

        @pl.when(j == max(steps - AHEAD, 0))
        def _():
            dual.start()

        cut = columns(j * STEP, STEP)
        acc[...] += nt(x_out[:, cut].astype(BF16), a_out[:, cut])

    m_out[...] = acc[...].astype(BF16)
    dual.wait()
    half = width // 2
    mine = columns(side[0] * half, half)
    other = columns((1 - side[0]) * half, half)
    mine_out[...] = x_out[:, mine] + u_out[:, mine]
    other_out[...] = x_out[:, other] + u_out[:, other]


def load(side, x, u, design):
    tasks, width = x.shape
    samples = design.shape[0]
    full = pltpu.VMEM((tasks, width), F32)
    half = pltpu.VMEM((tasks, width // 2), F32)
    return call(
        load_kernel,
        "load_and_margins",
        [SMEM] + [HBM] * 3,
        (pltpu.VMEM((tasks, samples), BF16), pltpu.VMEM(design.shape, BF16), full, full, half, half),
        [VMEM] * 6,
        [pltpu.VMEM((tasks, samples), F32), pltpu.SemaphoreType.DMA((3, width // STEP))],
    )(side, *pin(pltpu.HBM, x, u, design))


def rest_kernel(blocks_count, z_hbm, sign_hbm, eta_hbm, rho_hbm, lam_hbm, *refs):
    z_out, sign_out, scale_out, eta_row, rho_row, lam_row, sems = refs
    pairs = ((eta_hbm, eta_row), (rho_hbm, rho_row), (lam_hbm, lam_row), (z_hbm, z_out), (sign_hbm, sign_out))
    copies = [pltpu.make_async_copy(a, b, sems.at[k]) for k, (a, b) in enumerate(pairs)]
    for copy in copies:
        copy.start()
    for copy in copies[:3]:
        copy.wait()
    tasks = z_out.shape[0]
    one = lax.broadcasted_iota(jnp.int32, (tasks, tasks), 0) == lax.broadcasted_iota(jnp.int32, (tasks, tasks), 1)
    eta, rho, lam = eta_row[...], rho_row[...], lam_row[...]
    for k, row in enumerate((eta, eta * rho, lam / (rho * blocks_count))):
        upright = jnp.where(one, jnp.broadcast_to(row, (tasks, tasks)), 0.0)
        scale_out[:, k : k + 1] = jnp.sum(upright, axis=1, keepdims=True)
    for copy in copies[3:]:
        copy.wait()


def load_rest(z, sign, step_size, rho, penalty, blocks_count):
    tasks, width = z.shape
    rows = [v.reshape(1, tasks) for v in (step_size, rho, penalty)]
    return call(
        functools.partial(rest_kernel, blocks_count),
        "load_rest",
        [HBM] * 5,
        (pltpu.VMEM((tasks, width), F32), pltpu.VMEM(sign.shape, jnp.int32), pltpu.VMEM((tasks, 128), F32)),
        [VMEM] * 3,
        [pltpu.VMEM((1, tasks), F32)] * 3 + [pltpu.SemaphoreType.DMA((5,))],
    )(*pin(pltpu.HBM, z, sign, *rows))


def residual(sign, own, other):
    margin = own.astype(F32) + other.astype(F32)
    sign = sign.astype(F32)
    return (sign * jax.nn.sigmoid(-sign * margin)).astype(BF16)


def turn_kernel(sign, own, other, scale, x_ref, u_ref, z_ref, a_ref, q_out, m_out, resid, acc):
    resid[...] = residual(sign[...], own[...], other[...])
    acc[...] = jnp.zeros_like(acc)
    eta, pull = scale[:, 0:1], scale[:, 1:2]

    @pl.loop(0, x_ref.shape[1] // 512)
    def _(j):
        cut = columns(j * 512, 512)
        push = eta * jnp.dot(resid[...], a_ref[:, cut], preferred_element_type=F32)
        x = x_ref[:, cut]
        x = x - pull * (x - z_ref[:, cut] + u_ref[:, cut]) + push
        q_out[:, cut] = (1.0 - pull) * push
        acc[...] += nt(x.astype(BF16), a_ref[:, cut])

    m_out[...] = acc[...].astype(BF16)


def turn(sign, pair, scale, x, u, z, design):
    tasks, width = x.shape
    samples = design.shape[0]
    return call(
        turn_kernel,
        "turn",
        [VMEM] * 8,
        (pltpu.VMEM((tasks, width), F32), pltpu.VMEM((tasks, samples), BF16)),
        [VMEM] * 2,
        [pltpu.VMEM((tasks, samples), BF16), pltpu.VMEM((tasks, samples), F32)],
    )(*pin(pltpu.VMEM, sign, *pair, scale, x, u, z, design))


def push_kernel(mine, begin, size, side, *refs):
    if mine is None:
        sign, own, other, scale, q_ref, a_ref, h_out, sent_out, resid = refs
        resid[...] = residual(sign[...], own[...], other[...])
    else:
        resid, scale, q_ref, a_ref, *received, h_out, sent_out = refs
    half = q_ref.shape[1] // 2
    eta = scale[:, 0:1]
    base = (side[0] if mine else 1 - side[0]) * half + begin
    step = math.gcd(512, size)
    for j in range(size // step):
        cut = columns(base + j * step, step)
        here = pl.ds(j * step, step)
        push = q_ref[:, cut] + eta * jnp.dot(resid[...], a_ref[:, cut], preferred_element_type=F32)
        h_out[:, here] = push
        if mine:
            push = push + received[0][:, here].astype(F32)
        sent_out[:, here] = push.astype(BF16)


def push(side, resid, scale, q, design, received, begin, size):
    tasks = q.shape[0]
    mine = received is not None
    first = isinstance(resid, tuple)
    args = [*(resid if first else [resid]), scale, q, design] + ([received] if mine else [])
    out = [pltpu.VMEM((tasks, size), F32), pltpu.VMEM((tasks, size), BF16)]
    if first:
        out.append(pltpu.VMEM((tasks, design.shape[0]), BF16))
    return call(
        functools.partial(push_kernel, None if first else mine, begin, size),
        "push_mine" if mine else "push_other",
        [SMEM] + [VMEM] * len(args),
        tuple(out),
        [VMEM] * len(out),
    )(side, *pin(pltpu.VMEM, *args))


def store_kernel(sizes, side, scale, x_ref, u_ref, z_ref, *rest):
    count = len(sizes)
    hs = (rest[:count], rest[count : 2 * count])
    x_out, stage, sems = rest[2 * count :]
    half = x_ref.shape[1] // 2
    keep = 1.0 - scale[:, 1:2]
    copies = []
    for k in range(2):
        begin = 0
        for c, size in enumerate(sizes):
            base = (side[0] if k == 0 else 1 - side[0]) * half + begin
            for j in range(0, size, NARROW):
                cut = columns(base + j, NARROW)
                u, z = u_ref[:, cut], z_ref[:, cut]
                h = hs[k][c][:, pl.ds(j, NARROW)]
                stage[:, cut] = z - u + keep * keep * (x_ref[:, cut] - z + u) + h
            cut = columns(base, size)
            copy = pltpu.make_async_copy(stage.at[:, cut], x_out.at[:, cut], sems.at[k, c])
            copy.start()
            copies.append(copy)
            begin += size
    for copy in copies:
        copy.wait()


def store_x(side, scale, x, u, z, mines, others, sizes):
    tasks, width = x.shape
    return call(
        functools.partial(store_kernel, sizes),
        "store_x",
        [SMEM] + [VMEM] * (4 + 2 * len(sizes)),
        pltpu.HBM((tasks, width), F32),
        HBM,
        [pltpu.VMEM((tasks, width), F32), pltpu.SemaphoreType.DMA((2, len(sizes)))],
    )(side, *pin(pltpu.VMEM, scale, x, u, z, *mines, *others))


def final_kernel(blocks_count, begin, size, buffered, side, scale, x_ref, u_ref, z_ref, *rest):
    starts, hs, pushes = rest[0:2], rest[2:4], rest[4:6]
    outs = rest[6 + 2 * buffered : 8 + 2 * buffered]
    stage, sems = rest[-2:]
    half = x_ref.shape[1] // 2
    pull, limit = scale[:, 1:2], scale[:, 2:3]
    keep = 1.0 - pull
    copies = []
    for k in range(2):
        base = (side[0] if k == 0 else 1 - side[0]) * half + begin
        for j in range(0, size, NARROW):
            cut, here = columns(base + j, NARROW), pl.ds(j, NARROW)
            z = z_ref[:, cut]
            start = starts[k][:, pl.ds(begin + j, NARROW)]
            mean = (keep * keep * start + pushes[k][:, here].astype(F32)) * (1.0 / blocks_count) + pull * (1.0 + keep) * z
            new_z = mean - jnp.clip(mean, -limit, limit)
            moved = z + keep * keep * (x_ref[:, cut] - z + u_ref[:, cut]) + hs[k][:, here]
            stage[k, 0, :, here] = new_z
            stage[k, 1, :, here] = moved - new_z
        cut = columns(base, size)
        for o in range(2):
            copy = pltpu.make_async_copy(stage.at[k, o], outs[o].at[:, cut], sems.at[k, o])
            copy.start()
            copies.append(copy)
    for copy in copies:
        copy.wait()


def final(side, scale, x, u, z, starts, hs, pushes, buffers, begin, size, blocks_count):
    tasks, width = x.shape
    buffered = buffers is not None
    args = pin(pltpu.VMEM, scale, x, u, z, *starts, *hs, *pushes)
    out = pltpu.HBM((tasks, width), F32)
    aliases = {}
    if buffered:
        aliases = {1 + len(args) + o: o for o in range(2)}
        args += pin(pltpu.HBM, *buffers)
    return call(
        functools.partial(final_kernel, blocks_count, begin, size, buffered),
        "final",
        [SMEM] + [VMEM] * 10 + [HBM] * (2 * buffered),
        (out, out),
        [HBM] * 2,
        [pltpu.VMEM((2, 2, tasks, size), F32), pltpu.SemaphoreType.DMA((2, 2))],
        aliases,
    )(side, *args)


def tie(value, *after):
    return lax.optimization_barrier((value, after))[0]


def per_device(design, labels, local_x, dual_u, consensus_z, step_size, rho, penalty):
    tasks, width = consensus_z.shape
    half = width // 2
    blocks_count = lax.axis_size("rows")
    side = (lax.axis_index("rows") & 1).astype(jnp.int32)[None]

    margin1, design, x0, dual, start_mine, start_other = load(side, local_x[0], dual_u[0], design)
    start_mine = start_mine + exchange(start_other, "rows", 1)
    other = feat_exchange(margin1, feat_orders()[0])
    z, sign, scale = load_rest(consensus_z, labels, tie(step_size, other), rho, penalty, blocks_count)
    pair = feat_doubling(margin1, other)
    pair = tie(pair, start_mine)

    carried, margin2 = turn(sign, pair, scale, x0, dual, z, design)
    pair = feat_doubling(margin2)
    mask = 2
    while mask < blocks_count:
        start_mine = start_mine + exchange(start_mine, "rows", mask)
        mask *= 2
    pair = tie(pair, start_mine)
    start_theirs = exchange(start_mine, "rows", 1)

    sizes = [half * part // sum(EIGHTHS) for part in EIGHTHS]
    begins = [sum(sizes[:c]) for c in range(len(sizes))]
    count = len(sizes)
    others, mines, received, sums = [], [], [], []
    resid, token = (sign, *pair), side
    for c in range(count + 1):
        if c < count:
            value, other, *made = push(token, resid, scale, carried, design, None, begins[c], sizes[c])
            if made:
                resid = made[0]
            others.append(value)
            received.append(exchange(other, "rows", 1))
        if c > 0:
            value, sent = push(token, resid, scale, carried, design, received[c - 1], begins[c - 1], sizes[c - 1])
            mines.append(value)
            sums.append(doubling(sent, "rows", 2))
            token = tie(side, sent)
    new_x = store_x(side, scale, x0, dual, z, mines, others, sizes)

    results, pushes = [None], []

    def finish(c):
        results.append(
            final(
                side, scale, x0, dual, z, (start_mine, start_theirs), (mines[c], others[c]), pushes[c],
                results[-1], begins[c], sizes[c], blocks_count,
            )
        )

    for c, (a, b) in enumerate(sums):
        if 0 < c < count - 1:
            finish(c - 1)
        b = tie(b, new_x, results[-1])
        piece = (a.astype(F32) + b.astype(F32)).astype(BF16)
        pushes.append((piece, exchange(piece, "rows", 1)))
    for c in range(len(results) - 1, count):
        finish(c)
    new_z, new_u = results[-1]
    return (new_x[None], new_z, new_u[None])


def solution(mesh):
    in_specs = (
        P("rows", "feat"),
        P(None, "rows"),
        P("rows", None, "feat"),
        P("rows", None, "feat"),
        P(None, "feat"),
        P(),
        P(),
        P(),
    )
    out_specs = (P("rows", None, "feat"), P(None, "feat"), P("rows", None, "feat"))
    return jax.shard_map(
        per_device, mesh=mesh, in_specs=in_specs, out_specs=out_specs, check_vma=False
    )
```

```python
import functools
import math

import jax
import jax.numpy as jnp
from jax import lax
from jax.experimental import pallas as pl
from jax.experimental.pallas import tpu as pltpu
from jax.sharding import PartitionSpec as P

BF16 = jnp.bfloat16
F32 = jnp.float32
MINE = (2, 3, 3)
OTHER = (2, 6)
STEP = 1024
WIDE = 2048
AHEAD = 4
NARROW = 256
HBM = pl.BlockSpec(memory_space=pltpu.HBM)
VMEM = pl.BlockSpec(memory_space=pltpu.VMEM)
SMEM = pl.BlockSpec(memory_space=pltpu.SMEM)


def exchange(value, axis, mask):
    n = lax.axis_size(axis)
    return lax.ppermute(value, axis, [(i, i ^ mask) for i in range(n)])


def doubling(value, axis, first=1):
    n = lax.axis_size(axis)
    mask = first
    other = exchange(value, axis, mask)
    while 2 * mask < n:
        mask *= 2
        value = (value.astype(F32) + other.astype(F32)).astype(value.dtype)
        other = exchange(value, axis, mask)
    return value, other


def two_doublings(first, second):
    n = lax.axis_size("feat")
    values, gots, begun = [first, second], [None, None], [None, None]
    mask = 1
    while mask < n:
        for k in range(2):
            if mask > 1:
                got = gots[k] if k == 0 else tie(gots[k], values[0])
                values[k] = (values[k].astype(F32) + got.astype(F32)).astype(BF16)
            gots[k] = exchange(values[k], "feat", mask)
            if mask == 1:
                begun[k] = gots[k]
        mask *= 2
    return tuple(((v, g), b) for v, g, b in zip(values, gots, begun))


def nt(a, b):
    return lax.dot_general(a, b, (((1,), (1,)), ((), ())), preferred_element_type=F32)


def call(kernel, name, in_specs, out_shape, out_specs, scratch=(), aliases=None, limit=16, work=1000):
    return pl.pallas_call(
        kernel,
        in_specs=in_specs,
        out_shape=out_shape,
        out_specs=out_specs,
        scratch_shapes=list(scratch),
        input_output_aliases=aliases or {},
        compiler_params=pltpu.CompilerParams(vmem_limit_bytes=limit * 1024 * 1024),
        cost_estimate=pl.CostEstimate(flops=work, bytes_accessed=work, transcendentals=0),
        name=name,
    )


def pin(space, *values):
    return [pltpu.with_memory_space_constraint(v, space) for v in values]


def columns(start, size):
    return pl.ds(pl.multiple_of(start, 128), size)


def parts(tasks, samples):
    cut = samples - samples // 3
    return pltpu.VMEM((tasks, cut), BF16), pltpu.VMEM((tasks, samples - cut), BF16)


def load_kernel(side, x_hbm, u_hbm, a_hbm, first_out, second_out, a_out, x_out, u_out, mine_out, other_out, acc, sems):
    width = x_hbm.shape[1]
    steps = width // STEP

    def pair(j):
        cut = columns(j * STEP, STEP)
        return (
            pltpu.make_async_copy(x_hbm.at[:, cut], x_out.at[:, cut], sems.at[0, j]),
            pltpu.make_async_copy(a_hbm.at[:, cut], a_out.at[:, cut], sems.at[1, j]),
        )

    def begin(j):
        for copy in pair(j):
            copy.start()

    dual = pltpu.make_async_copy(u_hbm, u_out, sems.at[2, 0])
    for j in range(min(AHEAD, steps)):
        begin(j)
    acc[...] = jnp.zeros_like(acc)

    @pl.loop(0, steps)
    def _(j):
        for copy in pair(j):
            copy.wait()

        @pl.when(j + AHEAD < steps)
        def _():
            begin(j + AHEAD)

        @pl.when(j == max(steps - AHEAD, 0))
        def _():
            dual.start()

        cut = columns(j * STEP, STEP)
        acc[...] += nt(x_out[:, cut].astype(BF16), a_out[:, cut])

    cut = first_out.shape[1]
    first_out[...] = acc[:, :cut].astype(BF16)
    second_out[...] = acc[:, cut:].astype(BF16)
    dual.wait()
    half = width // 2
    mine = columns(side[0] * half, half)
    other = columns((1 - side[0]) * half, half)
    mine_out[...] = x_out[:, mine] + u_out[:, mine]
    other_out[...] = x_out[:, other] + u_out[:, other]


def load(side, x, u, design):
    tasks, width = x.shape
    samples = design.shape[0]
    full = pltpu.VMEM((tasks, width), F32)
    half = pltpu.VMEM((tasks, width // 2), F32)
    return call(
        load_kernel,
        "load_and_margins",
        [SMEM] + [HBM] * 3,
        (*parts(tasks, samples), pltpu.VMEM(design.shape, BF16), full, full, half, half),
        [VMEM] * 7,
        [pltpu.VMEM((tasks, samples), F32), pltpu.SemaphoreType.DMA((3, width // STEP))],
    )(side, *pin(pltpu.HBM, x, u, design))


def rest_kernel(blocks_count, z_hbm, sign_hbm, eta_hbm, rho_hbm, lam_hbm, *refs):
    z_out, sign_out, scale_out, eta_row, rho_row, lam_row, sems = refs
    pairs = ((eta_hbm, eta_row), (rho_hbm, rho_row), (lam_hbm, lam_row), (z_hbm, z_out), (sign_hbm, sign_out))
    copies = [pltpu.make_async_copy(a, b, sems.at[k]) for k, (a, b) in enumerate(pairs)]
    for copy in copies:
        copy.start()
    for copy in copies[:3]:
        copy.wait()
    tasks = z_out.shape[0]
    one = lax.broadcasted_iota(jnp.int32, (tasks, tasks), 0) == lax.broadcasted_iota(jnp.int32, (tasks, tasks), 1)
    eta, rho, lam = eta_row[...], rho_row[...], lam_row[...]
    for k, row in enumerate((eta, eta * rho, lam / (rho * blocks_count))):
        upright = jnp.where(one, jnp.broadcast_to(row, (tasks, tasks)), 0.0)
        scale_out[:, k : k + 1] = jnp.sum(upright, axis=1, keepdims=True)
    for copy in copies[3:]:
        copy.wait()


def load_rest(z, sign, step_size, rho, penalty, blocks_count):
    tasks, width = z.shape
    rows = [v.reshape(1, tasks) for v in (step_size, rho, penalty)]
    return call(
        functools.partial(rest_kernel, blocks_count),
        "load_rest",
        [HBM] * 5,
        (pltpu.VMEM((tasks, width), F32), pltpu.VMEM(sign.shape, jnp.int32), pltpu.VMEM((tasks, 128), F32)),
        [VMEM] * 3,
        [pltpu.VMEM((1, tasks), F32)] * 3 + [pltpu.SemaphoreType.DMA((5,))],
    )(*pin(pltpu.HBM, z, sign, *rows))


def residual(sign, own, other):
    margin = own.astype(F32) + other.astype(F32)
    sign = sign.astype(F32)
    return (sign * jax.nn.sigmoid(-sign * margin)).astype(BF16)


def first_kernel(sign, own, other, scale, a_ref, *rest):
    before, out, resid = rest[:-2], rest[-2], rest[-1]
    cut = own.shape[1]
    eta = scale[:, 0:1]
    resid[...] = residual(sign[:, :cut], own[...], other[...])

    @pl.loop(0, out.shape[1] // STEP)
    def _(j):
        at = columns(j * STEP, STEP)
        push = eta * jnp.dot(resid[...], a_ref[:cut, at], preferred_element_type=F32)
        out[:, at] = push + before[0][:, at] if before else push


def first_push(sign, pair, scale, design, before=None):
    tasks = sign.shape[0]
    args = [sign, *pair, scale, design] + ([] if before is None else [before])
    return call(
        first_kernel,
        "first_push",
        [VMEM] * len(args),
        pltpu.VMEM((tasks, design.shape[1]), F32),
        VMEM,
        [pltpu.VMEM(pair[0].shape, BF16)],
    )(*pin(pltpu.VMEM, *args))


def margin_loop(x_ref, a_ref, rows, acc, out):
    width = x_ref.shape[1]
    wide = math.gcd(WIDE, width)
    for j in range(width // wide):
        at = pl.ds(j * wide, wide)
        product = nt(x_ref[:, at], a_ref[rows, at])
        if j == 0:
            acc[...] = product
        else:
            acc[...] += product
    out[...] = acc[...].astype(BF16)


def turn_kernel(sign, own, other, scale, x_ref, u_ref, z_ref, p_ref, a_ref, q_out, x_out, m_out, resid, acc):
    cut = m_out.shape[1]
    resid[...] = residual(sign[:, cut:], own[...], other[...])
    eta, pull = scale[:, 0:1], scale[:, 1:2]

    @pl.loop(0, x_ref.shape[1] // STEP)
    def _(j):
        at = columns(j * STEP, STEP)
        push = p_ref[:, at] + eta * jnp.dot(resid[...], a_ref[cut:, at], preferred_element_type=F32)
        x = x_ref[:, at]
        x_out[:, at] = (x - pull * (x - z_ref[:, at] + u_ref[:, at]) + push).astype(BF16)
        q_out[:, at] = (1.0 - pull) * push

    margin_loop(x_out, a_ref, pl.ds(0, cut), acc, m_out)


def turn(sign, pair, scale, x, u, z, pushed, design):
    tasks, width = x.shape
    first, second = parts(tasks, design.shape[0])
    return call(
        turn_kernel,
        "turn",
        [VMEM] * 9,
        (pltpu.VMEM((tasks, width), F32), pltpu.VMEM((tasks, width), BF16), first),
        [VMEM] * 3,
        [pltpu.VMEM(second.shape, BF16), pltpu.VMEM(first.shape, F32)],
    )(*pin(pltpu.VMEM, sign, *pair, scale, x, u, z, pushed, design))


def margin_kernel(x_ref, a_ref, out, acc):
    rows = out.shape[1]
    margin_loop(x_ref, a_ref, pl.ds(a_ref.shape[0] - rows, rows), acc, out)


def rest_margins(x, design):
    tasks = x.shape[0]
    _, second = parts(tasks, design.shape[0])
    return call(
        margin_kernel, "rest_margins", [VMEM] * 2, second, VMEM, [pltpu.VMEM(second.shape, F32)]
    )(*pin(pltpu.VMEM, x, design))


def push_kernel(first, mine, begin, offset, size, side, *refs):
    if first:
        sign, own, other, scale, q_ref, a_ref, h_out, sent_out, resid = refs
        resid[...] = residual(sign[:, sign.shape[1] - own.shape[1] :], own[...], other[...])
    else:
        resid, scale, q_ref, a_ref, *received, h_out, sent_out = refs
    half = q_ref.shape[1] // 2
    cut = a_ref.shape[0] - resid.shape[1]
    eta = scale[:, 0:1]
    base = (side[0] if mine else 1 - side[0]) * half + begin
    step = math.gcd(512, size)
    for j in range(size // step):
        at = columns(base + j * step, step)
        here = pl.ds(j * step, step)
        push = q_ref[:, at] + eta * jnp.dot(resid[...], a_ref[cut:, at], preferred_element_type=F32)
        h_out[:, here] = push
        if mine:
            push = push + received[0][:, pl.ds(offset + j * step, step)].astype(F32)
        sent_out[:, here] = push.astype(BF16)


def push(side, resid, scale, q, design, received, begin, offset, size):
    tasks = q.shape[0]
    mine = received is not None
    first = isinstance(resid, tuple)
    args = [*(resid if first else [resid]), scale, q, design] + ([received] if mine else [])
    out = [pltpu.VMEM((tasks, size), F32), pltpu.VMEM((tasks, size), BF16)]
    if first:
        out.append(parts(tasks, design.shape[0])[1])
    return call(
        functools.partial(push_kernel, first, mine, begin, offset, size),
        "push_mine" if mine else "push_other",
        [SMEM] + [VMEM] * len(args),
        tuple(out),
        [VMEM] * len(out),
    )(side, *pin(pltpu.VMEM, *args))


def store_kernel(side, scale, x_ref, u_ref, z_ref, *rest):
    *hs, x_out, stage, sems = rest
    half = x_ref.shape[1] // 2
    keep = 1.0 - scale[:, 1:2]
    copies = []
    done = 0
    for c, h_ref in enumerate(hs):
        size = h_ref.shape[1]
        base = (side[0] if done < half else 1 - side[0]) * half + done % half
        done += size
        for j in range(0, size, NARROW):
            at = columns(base + j, NARROW)
            u, z = u_ref[:, at], z_ref[:, at]
            stage[:, at] = z - u + keep * keep * (x_ref[:, at] - z + u) + h_ref[:, pl.ds(j, NARROW)]
        at = columns(base, size)
        copy = pltpu.make_async_copy(stage.at[:, at], x_out.at[:, at], sems.at[c])
        copy.start()
        copies.append(copy)
    for copy in copies:
        copy.wait()


def store_x(side, scale, x, u, z, mines, others):
    tasks, width = x.shape
    args = [scale, x, u, z, *mines, *others]
    return call(
        store_kernel,
        "store_x",
        [SMEM] + [VMEM] * len(args),
        pltpu.HBM((tasks, width), F32),
        HBM,
        [pltpu.VMEM((tasks, width), F32), pltpu.SemaphoreType.DMA((len(mines) + len(others),))],
    )(side, *pin(pltpu.VMEM, *args))


def final_kernel(blocks_count, mine, begin, offset, size, buffered, side, scale, x_ref, u_ref, z_ref, *rest):
    start, h, pushed = rest[:3]
    outs = rest[3 + 2 * buffered : 5 + 2 * buffered]
    stage, sems = rest[-2:]
    half = x_ref.shape[1] // 2
    pull, limit = scale[:, 1:2], scale[:, 2:3]
    keep = 1.0 - pull
    base = (side[0] if mine else 1 - side[0]) * half + begin
    for j in range(0, size, NARROW):
        cut, here = columns(base + j, NARROW), pl.ds(j, NARROW)
        z = z_ref[:, cut]
        total = keep * keep * start[:, pl.ds(begin + j, NARROW)] + pushed[:, here].astype(F32)
        mean = total * (1.0 / blocks_count) + pull * (1.0 + keep) * z
        new_z = mean - jnp.clip(mean, -limit, limit)
        moved = z + keep * keep * (x_ref[:, cut] - z + u_ref[:, cut]) + h[:, pl.ds(offset + j, NARROW)]
        stage[0, :, here] = new_z
        stage[1, :, here] = moved - new_z
    cut = columns(base, size)
    copies = [pltpu.make_async_copy(stage.at[o], outs[o].at[:, cut], sems.at[o]) for o in range(2)]
    for copy in copies:
        copy.start()
    for copy in copies:
        copy.wait()


def final(side, scale, x, u, z, start, h, pushed, buffers, mine, begin, offset, blocks_count):
    tasks, width = x.shape
    size = pushed.shape[1]
    buffered = buffers is not None
    args = pin(pltpu.VMEM, scale, x, u, z, start, h, pushed)
    out = pltpu.HBM((tasks, width), F32)
    aliases = {}
    if buffered:
        aliases = {1 + len(args) + o: o for o in range(2)}
        args += pin(pltpu.HBM, *buffers)
    return call(
        functools.partial(final_kernel, blocks_count, mine, begin, offset, size, buffered),
        "final_mine" if mine else "final_other",
        [SMEM] + [VMEM] * 7 + [HBM] * (2 * buffered),
        (out, out),
        [HBM] * 2,
        [pltpu.VMEM((2, tasks, size), F32), pltpu.SemaphoreType.DMA((2,))],
        aliases,
    )(side, *args)


def tie(value, *after):
    return lax.optimization_barrier((value, after))[0]


def per_device(design, labels, local_x, dual_u, consensus_z, step_size, rho, penalty):
    tasks, width = consensus_z.shape
    half = width // 2
    blocks_count = lax.axis_size("rows")
    side = (lax.axis_index("rows") & 1).astype(jnp.int32)[None]

    first, second, design, x0, dual, start_mine, start_other = load(side, local_x[0], dual_u[0], design)
    start_mine = start_mine + exchange(start_other, "rows", 1)
    (pair_first, other_first), (pair_second, _) = two_doublings(first, second)
    z, sign, scale = load_rest(consensus_z, labels, tie(step_size, other_first), rho, penalty, blocks_count)
    pushed = first_push(sign, pair_first, scale, design)
    pair_second = tie(pair_second, pushed, start_mine)

    carried, x1, first = turn(sign, pair_second, scale, x0, dual, z, pushed, design)
    second = rest_margins(x1, design)
    mask = 2
    while mask < blocks_count:
        start_mine = start_mine + exchange(start_mine, "rows", mask)
        mask *= 2
    (pair_first, _), (pair_second, _) = two_doublings(first, second)
    pushed = first_push(sign, pair_first, scale, design, carried)
    pair_second = tie(pair_second, pushed, start_mine)

    sizes = [half * part // sum(MINE) for part in MINE]
    begins = [sum(sizes[:c]) for c in range(len(sizes))]
    other_sizes = [half * part // sum(OTHER) for part in OTHER]
    other_begins = [sum(other_sizes[:c]) for c in range(len(other_sizes))]
    count = len(sizes)
    others, received = [], []
    resid = (sign, *pair_second)
    for begin, size in zip(other_begins, other_sizes):
        value, other, *made = push(side, resid, scale, pushed, design, None, begin, 0, size)
        resid = made[0] if made else resid
        others.append(value)
        received.append(exchange(other, "rows", 1))
    mines, sums, places = [], [], []
    token = tie(side, others[-1])
    for begin, size in zip(begins, sizes):
        source = max(k for k, b in enumerate(other_begins) if b <= begin)
        places.append((source, begin - other_begins[source]))
        value, sent = push(token, resid, scale, pushed, design, received[source], begin, places[-1][1], size)
        mines.append(value)
        sums.append(doubling(sent, "rows", 2))
        token = tie(side, sent)
    new_x = store_x(side, scale, x0, dual, z, mines, others)

    start_theirs = exchange(tie(start_mine, mines[0]), "rows", 1)

    pieces, results = [], None

    def finish(c, mine):
        source, offset = places[c]
        return final(
            side, scale, x0, dual, z, start_mine if mine else start_theirs, mines[c] if mine else others[source],
            pieces[c][0 if mine else 1], results, mine, begins[c], 0 if mine else offset, blocks_count,
        )

    for c, (a, b) in enumerate(sums):
        b = tie(b, new_x, results)
        piece = (a.astype(F32) + b.astype(F32)).astype(BF16)
        if c == count - 1:
            results = tie(results, piece)
            results = finish(c - 1, False)
        pieces.append((piece, exchange(piece, "rows", 1)))
        results = finish(c, True)
        if c != count - 2:
            results = finish(c, False)
    new_z, new_u = results
    return (new_x[None], new_z, new_u[None])


def solution(mesh):
    in_specs = (
        P("rows", "feat"),
        P(None, "rows"),
        P("rows", None, "feat"),
        P("rows", None, "feat"),
        P(None, "feat"),
        P(),
        P(),
        P(),
    )
    out_specs = (P("rows", None, "feat"), P(None, "feat"), P("rows", None, "feat"))
    return jax.shard_map(
        per_device, mesh=mesh, in_specs=in_specs, out_specs=out_specs, check_vma=False
    )
```

```python
import functools
import math

import jax
import jax.numpy as jnp
from jax import lax
from jax.experimental import pallas as pl
from jax.experimental.pallas import tpu as pltpu
from jax.sharding import PartitionSpec as P

BF16 = jnp.bfloat16
F32 = jnp.float32
MINE = (2, 3, 3)
OTHER = (2, 6)
STEP = 1024
WIDE = 2048
AHEAD = 4
NARROW = 256
TURN_BYTES = 150_000_000
HBM = pl.BlockSpec(memory_space=pltpu.HBM)
VMEM = pl.BlockSpec(memory_space=pltpu.VMEM)
SMEM = pl.BlockSpec(memory_space=pltpu.SMEM)


def exchange(value, axis, mask):
    n = lax.axis_size(axis)
    return lax.ppermute(value, axis, [(i, i ^ mask) for i in range(n)])


def doubling(value, axis, first=1):
    n = lax.axis_size(axis)
    mask = first
    other = exchange(value, axis, mask)
    while 2 * mask < n:
        mask *= 2
        value = (value.astype(F32) + other.astype(F32)).astype(value.dtype)
        other = exchange(value, axis, mask)
    return value, other


def square_sum(value, axis):
    n = lax.axis_size(axis)
    terms = [value]
    mask = 1
    while mask < n:
        if len(terms) > 1:
            terms = [sum(t.astype(F32) for t in terms).astype(value.dtype)]
        steps = [mask, 2 * mask, 3 * mask] if 2 * mask < n else [mask]
        terms += [exchange(terms[0], axis, step) for step in steps]
        mask *= 4
    return terms


def nt(a, b):
    return lax.dot_general(a, b, (((1,), (1,)), ((), ())), preferred_element_type=F32)


def call(kernel, name, in_specs, out_shape, out_specs, scratch=(), aliases=None, limit=16, work=1000):
    return pl.pallas_call(
        kernel,
        in_specs=in_specs,
        out_shape=out_shape,
        out_specs=out_specs,
        scratch_shapes=list(scratch),
        input_output_aliases=aliases or {},
        compiler_params=pltpu.CompilerParams(vmem_limit_bytes=limit * 1024 * 1024),
        cost_estimate=pl.CostEstimate(flops=1000, bytes_accessed=work, transcendentals=0),
        name=name,
    )


def pin(space, *values):
    return [pltpu.with_memory_space_constraint(v, space) for v in values]


def columns(start, size):
    return pl.ds(pl.multiple_of(start, 128), size)


def load_kernel(side, x_hbm, u_hbm, a_hbm, m_out, a_out, x_out, u_out, mine_out, other_out, acc, sems):
    width = x_hbm.shape[1]
    steps = width // STEP

    def pair(j):
        cut = columns(j * STEP, STEP)
        return (
            pltpu.make_async_copy(x_hbm.at[:, cut], x_out.at[:, cut], sems.at[0, j]),
            pltpu.make_async_copy(a_hbm.at[:, cut], a_out.at[:, cut], sems.at[1, j]),
        )

    def begin(j):
        for copy in pair(j):
            copy.start()

    dual = pltpu.make_async_copy(u_hbm, u_out, sems.at[2, 0])
    for j in range(min(AHEAD, steps)):
        begin(j)
    acc[...] = jnp.zeros_like(acc)

    @pl.loop(0, steps)
    def _(j):
        for copy in pair(j):
            copy.wait()

        @pl.when(j + AHEAD < steps)
        def _():
            begin(j + AHEAD)

        @pl.when(j == max(steps - AHEAD, 0))
        def _():
            dual.start()

        cut = columns(j * STEP, STEP)
        acc[...] += nt(x_out[:, cut].astype(BF16), a_out[:, cut])

    m_out[...] = acc[...].astype(BF16)
    dual.wait()
    half = width // 2
    mine = columns(side[0] * half, half)
    other = columns((1 - side[0]) * half, half)
    mine_out[...] = x_out[:, mine] + u_out[:, mine]
    other_out[...] = x_out[:, other] + u_out[:, other]


def load(side, x, u, design):
    tasks, width = x.shape
    samples = design.shape[0]
    full = pltpu.VMEM((tasks, width), F32)
    half = pltpu.VMEM((tasks, width // 2), F32)
    return call(
        load_kernel,
        "load_and_margins",
        [SMEM] + [HBM] * 3,
        (pltpu.VMEM((tasks, samples), BF16), pltpu.VMEM(design.shape, BF16), full, full, half, half),
        [VMEM] * 6,
        [pltpu.VMEM((tasks, samples), F32), pltpu.SemaphoreType.DMA((3, width // STEP))],
    )(side, *pin(pltpu.HBM, x, u, design))


def rest_kernel(blocks_count, z_hbm, sign_hbm, eta_hbm, rho_hbm, lam_hbm, *refs):
    z_out, sign_out, scale_out, eta_row, rho_row, lam_row, sems = refs
    pairs = ((eta_hbm, eta_row), (rho_hbm, rho_row), (lam_hbm, lam_row), (z_hbm, z_out), (sign_hbm, sign_out))
    copies = [pltpu.make_async_copy(a, b, sems.at[k]) for k, (a, b) in enumerate(pairs)]
    for copy in copies:
        copy.start()
    for copy in copies[:3]:
        copy.wait()
    tasks = z_out.shape[0]
    one = lax.broadcasted_iota(jnp.int32, (tasks, tasks), 0) == lax.broadcasted_iota(jnp.int32, (tasks, tasks), 1)
    eta, rho, lam = eta_row[...], rho_row[...], lam_row[...]
    for k, row in enumerate((eta, eta * rho, lam / (rho * blocks_count))):
        upright = jnp.where(one, jnp.broadcast_to(row, (tasks, tasks)), 0.0)
        scale_out[:, k : k + 1] = jnp.sum(upright, axis=1, keepdims=True)
    for copy in copies[3:]:
        copy.wait()


def load_rest(z, sign, step_size, rho, penalty, blocks_count):
    tasks, width = z.shape
    rows = [v.reshape(1, tasks) for v in (step_size, rho, penalty)]
    return call(
        functools.partial(rest_kernel, blocks_count),
        "load_rest",
        [HBM] * 5,
        (pltpu.VMEM((tasks, width), F32), pltpu.VMEM(sign.shape, jnp.int32), pltpu.VMEM((tasks, 128), F32)),
        [VMEM] * 3,
        [pltpu.VMEM((1, tasks), F32)] * 3 + [pltpu.SemaphoreType.DMA((5,))],
    )(*pin(pltpu.HBM, z, sign, *rows))


def residual(sign, *terms):
    margin = sum(t.astype(F32) for t in terms)
    sign = sign.astype(F32)
    return (sign * jax.nn.sigmoid(-sign * margin)).astype(BF16)


def turn_kernel(sign, scale, x_ref, u_ref, z_ref, a_ref, *refs):
    *terms, q_out, m_out, resid, new_x, acc = refs
    resid[...] = residual(sign[...], *(t[...] for t in terms))
    eta, pull = scale[:, 0:1], scale[:, 1:2]
    width = x_ref.shape[1]

    @pl.loop(0, width // STEP)
    def _(j):
        at = columns(j * STEP, STEP)
        push = eta * jnp.dot(resid[...], a_ref[:, at], preferred_element_type=F32)
        x = x_ref[:, at]
        new_x[:, at] = (x - pull * (x - z_ref[:, at] + u_ref[:, at]) + push).astype(BF16)
        q_out[:, at] = (1.0 - pull) * push

    wide = math.gcd(WIDE, width)
    for j in range(width // wide):
        at = pl.ds(j * wide, wide)
        product = nt(new_x[:, at], a_ref[:, at])
        acc[...] = product if j == 0 else acc[...] + product
    m_out[...] = acc[...].astype(BF16)


def turn(sign, terms, scale, x, u, z, design):
    tasks, width = x.shape
    samples = design.shape[0]
    return call(
        turn_kernel,
        "turn",
        [VMEM] * (6 + len(terms)),
        (pltpu.VMEM((tasks, width), F32), pltpu.VMEM((tasks, samples), BF16)),
        [VMEM] * 2,
        [pltpu.VMEM((tasks, samples), BF16), pltpu.VMEM((tasks, width), BF16), pltpu.VMEM((tasks, samples), F32)],
        work=TURN_BYTES,
    )(*pin(pltpu.VMEM, sign, scale, x, u, z, design, *terms))


def push_kernel(first, mine, begin, offset, size, side, *refs):
    if first:
        scale, q_ref, a_ref, sign, *terms, h_out, sent_out, resid = refs
        resid[...] = residual(sign[...], *(t[...] for t in terms))
    else:
        scale, q_ref, a_ref, resid, *received, h_out, sent_out = refs
    half = q_ref.shape[1] // 2
    eta = scale[:, 0:1]
    base = (side[0] if mine else 1 - side[0]) * half + begin
    step = math.gcd(512, size)
    for j in range(size // step):
        at = columns(base + j * step, step)
        here = pl.ds(j * step, step)
        push = q_ref[:, at] + eta * jnp.dot(resid[...], a_ref[:, at], preferred_element_type=F32)
        h_out[:, here] = push
        if mine:
            push = push + received[0][:, pl.ds(offset + j * step, step)].astype(F32)
        sent_out[:, here] = push.astype(BF16)


def push(side, resid, scale, q, design, received, begin, offset, size):
    tasks = q.shape[0]
    mine = received is not None
    first = isinstance(resid, tuple)
    args = [scale, q, design, *(resid if first else [resid])] + ([received] if mine else [])
    out = [pltpu.VMEM((tasks, size), F32), pltpu.VMEM((tasks, size), BF16)]
    if first:
        out.append(pltpu.VMEM((tasks, design.shape[0]), BF16))
    return call(
        functools.partial(push_kernel, first, mine, begin, offset, size),
        "push_mine" if mine else "push_other",
        [SMEM] + [VMEM] * len(args),
        tuple(out),
        [VMEM] * len(out),
    )(side, *pin(pltpu.VMEM, *args))


def store_kernel(side, scale, x_ref, u_ref, z_ref, *rest):
    *hs, x_out, stage, sems = rest
    half = x_ref.shape[1] // 2
    keep = 1.0 - scale[:, 1:2]
    copies = []
    done = 0
    for c, h_ref in enumerate(hs):
        size = h_ref.shape[1]
        base = (side[0] if done < half else 1 - side[0]) * half + done % half
        done += size
        for j in range(0, size, NARROW):
            at = columns(base + j, NARROW)
            u, z = u_ref[:, at], z_ref[:, at]
            stage[:, at] = z - u + keep * keep * (x_ref[:, at] - z + u) + h_ref[:, pl.ds(j, NARROW)]
        at = columns(base, size)
        copy = pltpu.make_async_copy(stage.at[:, at], x_out.at[:, at], sems.at[c])
        copy.start()
        copies.append(copy)
    for copy in copies:
        copy.wait()


def store_x(side, scale, x, u, z, mines, others):
    tasks, width = x.shape
    args = [scale, x, u, z, *mines, *others]
    return call(
        store_kernel,
        "store_x",
        [SMEM] + [VMEM] * len(args),
        pltpu.HBM((tasks, width), F32),
        HBM,
        [pltpu.VMEM((tasks, width), F32), pltpu.SemaphoreType.DMA((len(mines) + len(others),))],
    )(side, *pin(pltpu.VMEM, *args))


def final_kernel(blocks_count, pieces, buffered, side, scale, x_ref, u_ref, z_ref, *refs):
    outs = refs[3 * len(pieces) + 2 * buffered :][:2]
    stage, sems = refs[-2:]
    half = x_ref.shape[1] // 2
    pull, limit = scale[:, 1:2], scale[:, 2:3]
    keep = 1.0 - pull
    copies, filled = [], 0
    for k, (mine, begin, offset, size) in enumerate(pieces):
        start, h, pushed = refs[3 * k : 3 * k + 3]
        base = (side[0] if mine else 1 - side[0]) * half + begin
        for j in range(0, size, NARROW):
            cut, here = columns(base + j, NARROW), pl.ds(filled + j, NARROW)
            z = z_ref[:, cut]
            total = keep * keep * start[:, pl.ds(begin + j, NARROW)] + pushed[:, pl.ds(j, NARROW)].astype(F32)
            mean = total * (1.0 / blocks_count) + pull * (1.0 + keep) * z
            new_z = mean - jnp.clip(mean, -limit, limit)
            moved = z + keep * keep * (x_ref[:, cut] - z + u_ref[:, cut]) + h[:, pl.ds(offset + j, NARROW)]
            stage[0, :, here] = new_z
            stage[1, :, here] = moved - new_z
        cut, here = columns(base, size), pl.ds(filled, size)
        for o in range(2):
            copy = pltpu.make_async_copy(stage.at[o, :, here], outs[o].at[:, cut], sems.at[k, o])
            copy.start()
            copies.append(copy)
        filled += size
    for copy in copies:
        copy.wait()


def final(side, scale, x, u, z, pieces, buffers, blocks_count):
    tasks, width = x.shape
    buffered = buffers is not None
    args = pin(pltpu.VMEM, scale, x, u, z, *(v for piece in pieces for v in piece[3:]))
    vmem = len(args)
    places = [(*piece[:3], piece[5].shape[1]) for piece in pieces]
    out = pltpu.HBM((tasks, width), F32)
    aliases = {}
    if buffered:
        aliases = {1 + vmem + o: o for o in range(2)}
        args += pin(pltpu.HBM, *buffers)
    return call(
        functools.partial(final_kernel, blocks_count, places, buffered),
        "final",
        [SMEM] + [VMEM] * vmem + [HBM] * (2 * buffered),
        (out, out),
        [HBM] * 2,
        [pltpu.VMEM((2, tasks, sum(p[3] for p in places)), F32), pltpu.SemaphoreType.DMA((len(pieces), 2))],
        aliases,
    )(side, *args)


def tie(value, *after):
    return lax.optimization_barrier((value, after))[0]


def per_device(design, labels, local_x, dual_u, consensus_z, step_size, rho, penalty):
    tasks, width = consensus_z.shape
    half = width // 2
    blocks_count = lax.axis_size("rows")
    side = (lax.axis_index("rows") & 1).astype(jnp.int32)[None]

    margin1, design, x0, dual, start_mine, start_other = load(side, local_x[0], dual_u[0], design)
    terms = doubling(margin1, "feat")
    start_mine = start_mine + exchange(start_other, "rows", 1)
    z, sign, scale = load_rest(consensus_z, labels, tie(step_size, terms[0]), rho, penalty, blocks_count)
    terms = tie(terms, start_mine)

    carried, margin2 = turn(sign, terms, scale, x0, dual, z, design)
    terms = square_sum(margin2, "feat")
    mask = 2
    while mask < blocks_count:
        start_mine = start_mine + exchange(start_mine, "rows", mask)
        mask *= 2
    terms = tie(terms, start_mine)

    sizes = [half * part // sum(MINE) for part in MINE]
    begins = [sum(sizes[:c]) for c in range(len(sizes))]
    other_sizes = [half * part // sum(OTHER) for part in OTHER]
    other_begins = [sum(other_sizes[:c]) for c in range(len(other_sizes))]
    count = len(sizes)
    others, received = [], []
    resid = (sign, *terms)
    for begin, size in zip(other_begins, other_sizes):
        value, other, *made = push(side, resid, scale, carried, design, None, begin, 0, size)
        resid = made[0] if made else resid
        others.append(value)
        received.append(exchange(other, "rows", 1))
    mines, sums, places = [], [], []
    token = tie(side, others[-1])
    for begin, size in zip(begins, sizes):
        source = max(k for k, b in enumerate(other_begins) if b <= begin)
        places.append((source, begin - other_begins[source]))
        value, sent = push(token, resid, scale, carried, design, received[source], begin, places[-1][1], size)
        mines.append(value)
        sums.append(doubling(sent, "rows", 2))
        token = tie(side, sent)
    new_x = store_x(side, scale, x0, dual, z, mines, others)

    start_theirs = exchange(tie(start_mine, mines[0]), "rows", 1)

    waiting, results = [], None
    for c, (a, b) in enumerate(sums):
        b = tie(b, new_x, results)
        piece = (a.astype(F32) + b.astype(F32)).astype(BF16)
        source, offset = places[c]
        back = exchange(piece, "rows", 1)
        ready = waiting + [(True, begins[c], 0, start_mine, mines[c], piece)]
        results = final(side, scale, x0, dual, z, ready, results, blocks_count)
        waiting = [(False, begins[c], offset, start_theirs, others[source], back)]
    results = final(side, scale, x0, dual, z, waiting, results, blocks_count)
    new_z, new_u = results
    return (new_x[None], new_z, new_u[None])


def solution(mesh):
    in_specs = (
        P("rows", "feat"),
        P(None, "rows"),
        P("rows", None, "feat"),
        P("rows", None, "feat"),
        P(None, "feat"),
        P(),
        P(),
        P(),
    )
    out_specs = (P("rows", None, "feat"), P(None, "feat"), P("rows", None, "feat"))
    return jax.shard_map(
        per_device, mesh=mesh, in_specs=in_specs, out_specs=out_specs, check_vma=False
    )
```

```python
import functools
import math

import jax
import jax.numpy as jnp
from jax import lax
from jax.experimental import pallas as pl
from jax.experimental.pallas import tpu as pltpu
from jax.sharding import PartitionSpec as P

BF16 = jnp.bfloat16
F32 = jnp.float32
MINE = (2, 3, 3)
OTHER = (2, 6)
STEP = 1024
WIDE = 2048
AHEAD = 4
NARROW = 256
WAIT_BYTES = 10_000_000
HBM = pl.BlockSpec(memory_space=pltpu.HBM)
VMEM = pl.BlockSpec(memory_space=pltpu.VMEM)
SMEM = pl.BlockSpec(memory_space=pltpu.SMEM)


def exchange(value, axis, mask):
    n = lax.axis_size(axis)
    return lax.ppermute(value, axis, [(i, i ^ mask) for i in range(n)])


def doubling(value, axis, first=1):
    n = lax.axis_size(axis)
    mask = first
    other = exchange(value, axis, mask)
    while 2 * mask < n:
        mask *= 2
        value = (value.astype(F32) + other.astype(F32)).astype(value.dtype)
        other = exchange(value, axis, mask)
    return value, other


def square_sum(value, axis):
    n = lax.axis_size(axis)
    terms = [value]
    mask = 1
    while mask < n:
        if len(terms) > 1:
            terms = [sum(t.astype(F32) for t in terms).astype(value.dtype)]
        steps = [mask, 2 * mask, 3 * mask] if 2 * mask < n else [mask]
        terms += [exchange(terms[0], axis, step) for step in steps]
        mask *= 4
    return terms


def nt(a, b):
    return lax.dot_general(a, b, (((1,), (1,)), ((), ())), preferred_element_type=F32)


def call(kernel, name, in_specs, out_shape, out_specs, scratch=(), aliases=None, limit=16, work=1000):
    return pl.pallas_call(
        kernel,
        in_specs=in_specs,
        out_shape=out_shape,
        out_specs=out_specs,
        scratch_shapes=list(scratch),
        input_output_aliases=aliases or {},
        compiler_params=pltpu.CompilerParams(vmem_limit_bytes=limit * 1024 * 1024),
        cost_estimate=pl.CostEstimate(flops=1000, bytes_accessed=work, transcendentals=0),
        name=name,
    )


def pin(space, *values):
    return [pltpu.with_memory_space_constraint(v, space) for v in values]


def columns(start, size):
    return pl.ds(pl.multiple_of(start, 128), size)


def load_kernel(side, x_hbm, u_hbm, a_hbm, m_out, a_out, x_out, u_out, mine_out, other_out, acc, sems):
    width = x_hbm.shape[1]
    steps = width // STEP

    def pair(j):
        cut = columns(j * STEP, STEP)
        return (
            pltpu.make_async_copy(x_hbm.at[:, cut], x_out.at[:, cut], sems.at[0, j]),
            pltpu.make_async_copy(a_hbm.at[:, cut], a_out.at[:, cut], sems.at[1, j]),
        )

    def begin(j):
        for copy in pair(j):
            copy.start()

    dual = pltpu.make_async_copy(u_hbm, u_out, sems.at[2, 0])
    for j in range(min(AHEAD, steps)):
        begin(j)
    acc[...] = jnp.zeros_like(acc)

    @pl.loop(0, steps)
    def _(j):
        for copy in pair(j):
            copy.wait()

        @pl.when(j + AHEAD < steps)
        def _():
            begin(j + AHEAD)

        @pl.when(j == max(steps - AHEAD, 0))
        def _():
            dual.start()

        cut = columns(j * STEP, STEP)
        acc[...] += nt(x_out[:, cut].astype(BF16), a_out[:, cut])

    m_out[...] = acc[...].astype(BF16)
    dual.wait()
    half = width // 2
    mine = columns(side[0] * half, half)
    other = columns((1 - side[0]) * half, half)
    mine_out[...] = x_out[:, mine] + u_out[:, mine]
    other_out[...] = x_out[:, other] + u_out[:, other]


def load(side, x, u, design):
    tasks, width = x.shape
    samples = design.shape[0]
    full = pltpu.VMEM((tasks, width), F32)
    half = pltpu.VMEM((tasks, width // 2), F32)
    return call(
        load_kernel,
        "load_and_margins",
        [SMEM] + [HBM] * 3,
        (pltpu.VMEM((tasks, samples), BF16), pltpu.VMEM(design.shape, BF16), full, full, half, half),
        [VMEM] * 6,
        [pltpu.VMEM((tasks, samples), F32), pltpu.SemaphoreType.DMA((3, width // STEP))],
    )(side, *pin(pltpu.HBM, x, u, design))


def gram_block(a_ref, row, cols, size, acc, high, low):
    width = a_ref.shape[1]
    wide = math.gcd(WIDE, width)
    for j in range(width // wide):
        at = pl.ds(j * wide, wide)
        product = nt(a_ref[pl.ds(row, size), at], a_ref[pl.ds(0, cols), at])
        acc[:, :cols] = product if j == 0 else acc[:, :cols] + product
    whole = acc[:, :cols]
    top = whole.astype(BF16)
    high[...] = top
    low[...] = (whole - top.astype(F32)).astype(BF16)


def rest_kernel(blocks_count, a_ref, z_hbm, sign_hbm, eta_hbm, rho_hbm, lam_hbm, *refs):
    z_out, sign_out, scale_out, high, low, eta_row, rho_row, lam_row, acc, sems = refs
    pairs = ((eta_hbm, eta_row), (rho_hbm, rho_row), (lam_hbm, lam_row), (z_hbm, z_out), (sign_hbm, sign_out))
    copies = [pltpu.make_async_copy(a, b, sems.at[k]) for k, (a, b) in enumerate(pairs)]
    for copy in copies:
        copy.start()
    size, cols = high.shape
    gram_block(a_ref, cols - size, cols, size, acc, high, low)
    for copy in copies[:3]:
        copy.wait()
    tasks = z_out.shape[0]
    one = lax.broadcasted_iota(jnp.int32, (tasks, tasks), 0) == lax.broadcasted_iota(jnp.int32, (tasks, tasks), 1)
    eta, rho, lam = eta_row[...], rho_row[...], lam_row[...]
    for k, row in enumerate((eta, eta * rho, lam / (rho * blocks_count))):
        upright = jnp.where(one, jnp.broadcast_to(row, (tasks, tasks)), 0.0)
        scale_out[:, k : k + 1] = jnp.sum(upright, axis=1, keepdims=True)
    for copy in copies[3:]:
        copy.wait()


def gram_shapes(samples, row):
    size = samples // 3
    return [pltpu.VMEM((size, (row + 1) * size), BF16)] * 2


def load_rest(z, sign, step_size, rho, penalty, design, blocks_count):
    tasks, width = z.shape
    samples = design.shape[0]
    rows = [v.reshape(1, tasks) for v in (step_size, rho, penalty)]
    return call(
        functools.partial(rest_kernel, blocks_count),
        "load_and_gram",
        [VMEM] + [HBM] * 5,
        (
            pltpu.VMEM((tasks, width), F32), pltpu.VMEM(sign.shape, jnp.int32), pltpu.VMEM((tasks, 128), F32),
            *gram_shapes(samples, 2),
        ),
        [VMEM] * 5,
        [pltpu.VMEM((1, tasks), F32)] * 3 + [pltpu.VMEM((samples // 3, samples), F32), pltpu.SemaphoreType.DMA((5,))],
        work=WAIT_BYTES,
    )(*pin(pltpu.VMEM, design), *pin(pltpu.HBM, z, sign, *rows))


def gram_kernel(token, a_ref, *refs):
    *outs, acc = refs
    size = outs[0].shape[0]
    for row in range(2):
        gram_block(a_ref, row * size, (row + 1) * size, size, acc, outs[2 * row], outs[2 * row + 1])


def gram_rows(token, design):
    samples = design.shape[0]
    return call(
        gram_kernel,
        "gram",
        [SMEM, VMEM],
        (*gram_shapes(samples, 0), *gram_shapes(samples, 1)),
        [VMEM] * 4,
        [pltpu.VMEM((samples // 3, samples), F32)],
        work=WAIT_BYTES,
    )(token, *pin(pltpu.VMEM, design))


def pulled_kernel(token, scale, x_ref, u_ref, z_ref, a_ref, out, both, acc):
    pull = scale[:, 1:2]
    tasks, width = x_ref.shape
    wide = math.gcd(WIDE, width)
    for j in range(width // wide):
        for k in range(0, wide, 512):
            at, here = pl.ds(j * wide + k, 512), pl.ds(k, 512)
            x = x_ref[:, at]
            v = x - pull * (x - z_ref[:, at] + u_ref[:, at])
            top = v.astype(BF16)
            both[:tasks, here] = top
            both[tasks:, here] = (v - top.astype(F32)).astype(BF16)
        product = nt(both[...], a_ref[:, pl.ds(j * wide, wide)])
        acc[...] = product if j == 0 else acc[...] + product
    out[...] = acc[:tasks] + acc[tasks:]


def pulled_margins(token, scale, x, u, z, design):
    tasks, width = x.shape
    samples = design.shape[0]
    return call(
        pulled_kernel,
        "pulled_margins",
        [SMEM] + [VMEM] * 5,
        pltpu.VMEM((tasks, samples), F32),
        VMEM,
        [pltpu.VMEM((2 * tasks, math.gcd(WIDE, width)), BF16), pltpu.VMEM((2 * tasks, samples), F32)],
        work=WAIT_BYTES,
    )(token, *pin(pltpu.VMEM, scale, x, u, z, design))


def residual(sign, *terms):
    margin = sum(t.astype(F32) for t in terms)
    sign = sign.astype(F32)
    return (sign * jax.nn.sigmoid(-sign * margin)).astype(BF16)


def turn_kernel(sign, scale, pulled, *refs):
    *terms, resid, out = refs[6:]
    grams = refs[:6]
    size = grams[0].shape[0]
    resid[...] = residual(sign[...], *(t[...] for t in terms))
    eta = scale[:, 0:1]
    r = [resid[:, pl.ds(k * size, size)] for k in range(3)]
    for col in range(3):
        total = jnp.zeros((resid.shape[0], size), F32)
        for row in range(3):
            for part in range(2):
                if row >= col:
                    block = grams[2 * row + part][:, pl.ds(col * size, size)]
                    total += jnp.dot(r[row], block, preferred_element_type=F32)
                else:
                    total += nt(r[row], grams[2 * col + part][:, pl.ds(row * size, size)])
        here = pl.ds(col * size, size)
        out[:, here] = (pulled[:, here] + eta * total).astype(BF16)


def turn(sign, terms, scale, pulled, grams):
    tasks, samples = pulled.shape
    out = pltpu.VMEM((tasks, samples), BF16)
    args = [sign, scale, pulled, *grams, *terms]
    return call(turn_kernel, "turn", [VMEM] * len(args), (out, out), [VMEM] * 2)(*pin(pltpu.VMEM, *args))


def push_kernel(first, mine, begin, offset, size, side, *refs):
    tasks = refs[0].shape[0]
    if first:
        scale, a_ref, resid1, sign, *terms, h_out, sent_out, resid = refs
        resid[:tasks] = resid1[...]
        resid[tasks:] = residual(sign[...], *(t[...] for t in terms))
    else:
        scale, a_ref, resid, *received, h_out, sent_out = refs
    half = a_ref.shape[1] // 2
    eta = scale[:, 0:1]
    keep = 1.0 - scale[:, 1:2]
    base = (side[0] if mine else 1 - side[0]) * half + begin
    step = math.gcd(512, size)
    for j in range(size // step):
        at = columns(base + j * step, step)
        here = pl.ds(j * step, step)
        grads = jnp.dot(resid[...], a_ref[:, at], preferred_element_type=F32)
        push = eta * (keep * grads[:tasks] + grads[tasks:])
        h_out[:, here] = push
        if mine:
            push = push + received[0][:, pl.ds(offset + j * step, step)].astype(F32)
        sent_out[:, here] = push.astype(BF16)


def push(side, resid, scale, design, received, begin, offset, size):
    tasks = scale.shape[0]
    mine = received is not None
    first = isinstance(resid, tuple)
    args = [scale, design, *(resid if first else [resid])] + ([received] if mine else [])
    out = [pltpu.VMEM((tasks, size), F32), pltpu.VMEM((tasks, size), BF16)]
    if first:
        out.append(pltpu.VMEM((2 * tasks, design.shape[0]), BF16))
    return call(
        functools.partial(push_kernel, first, mine, begin, offset, size),
        "push_mine" if mine else "push_other",
        [SMEM] + [VMEM] * len(args),
        tuple(out),
        [VMEM] * len(out),
    )(side, *pin(pltpu.VMEM, *args))


def store_kernel(side, scale, x_ref, u_ref, z_ref, *rest):
    *hs, x_out, stage, sems = rest
    half = x_ref.shape[1] // 2
    keep = 1.0 - scale[:, 1:2]
    copies = []
    done = 0
    for c, h_ref in enumerate(hs):
        size = h_ref.shape[1]
        base = (side[0] if done < half else 1 - side[0]) * half + done % half
        done += size
        for j in range(0, size, NARROW):
            at = columns(base + j, NARROW)
            u, z = u_ref[:, at], z_ref[:, at]
            stage[:, at] = z - u + keep * keep * (x_ref[:, at] - z + u) + h_ref[:, pl.ds(j, NARROW)]
        at = columns(base, size)
        copy = pltpu.make_async_copy(stage.at[:, at], x_out.at[:, at], sems.at[c])
        copy.start()
        copies.append(copy)
    for copy in copies:
        copy.wait()


def store_x(side, scale, x, u, z, mines, others):
    tasks, width = x.shape
    args = [scale, x, u, z, *mines, *others]
    return call(
        store_kernel,
        "store_x",
        [SMEM] + [VMEM] * len(args),
        pltpu.HBM((tasks, width), F32),
        HBM,
        [pltpu.VMEM((tasks, width), F32), pltpu.SemaphoreType.DMA((len(mines) + len(others),))],
    )(side, *pin(pltpu.VMEM, *args))


def final_kernel(blocks_count, pieces, buffered, side, scale, x_ref, u_ref, z_ref, *refs):
    outs = refs[3 * len(pieces) + 2 * buffered :][:2]
    stage, sems = refs[-2:]
    half = x_ref.shape[1] // 2
    pull, limit = scale[:, 1:2], scale[:, 2:3]
    keep = 1.0 - pull
    copies, filled = [], 0
    for k, (mine, begin, offset, size) in enumerate(pieces):
        start, h, pushed = refs[3 * k : 3 * k + 3]
        base = (side[0] if mine else 1 - side[0]) * half + begin
        for j in range(0, size, NARROW):
            cut, here = columns(base + j, NARROW), pl.ds(filled + j, NARROW)
            z = z_ref[:, cut]
            total = keep * keep * start[:, pl.ds(begin + j, NARROW)] + pushed[:, pl.ds(j, NARROW)].astype(F32)
            mean = total * (1.0 / blocks_count) + pull * (1.0 + keep) * z
            new_z = mean - jnp.clip(mean, -limit, limit)
            moved = z + keep * keep * (x_ref[:, cut] - z + u_ref[:, cut]) + h[:, pl.ds(offset + j, NARROW)]
            stage[0, :, here] = new_z
            stage[1, :, here] = moved - new_z
        cut, here = columns(base, size), pl.ds(filled, size)
        for o in range(2):
            copy = pltpu.make_async_copy(stage.at[o, :, here], outs[o].at[:, cut], sems.at[k, o])
            copy.start()
            copies.append(copy)
        filled += size
    for copy in copies:
        copy.wait()


def final(side, scale, x, u, z, pieces, buffers, blocks_count):
    tasks, width = x.shape
    buffered = buffers is not None
    args = pin(pltpu.VMEM, scale, x, u, z, *(v for piece in pieces for v in piece[3:]))
    vmem = len(args)
    places = [(*piece[:3], piece[5].shape[1]) for piece in pieces]
    out = pltpu.HBM((tasks, width), F32)
    aliases = {}
    if buffered:
        aliases = {1 + vmem + o: o for o in range(2)}
        args += pin(pltpu.HBM, *buffers)
    return call(
        functools.partial(final_kernel, blocks_count, places, buffered),
        "final",
        [SMEM] + [VMEM] * vmem + [HBM] * (2 * buffered),
        (out, out),
        [HBM] * 2,
        [pltpu.VMEM((2, tasks, sum(p[3] for p in places)), F32), pltpu.SemaphoreType.DMA((len(pieces), 2))],
        aliases,
    )(side, *args)


def tie(value, *after):
    return lax.optimization_barrier((value, after))[0]


def per_device(design, labels, local_x, dual_u, consensus_z, step_size, rho, penalty):
    tasks, width = consensus_z.shape
    half = width // 2
    blocks_count = lax.axis_size("rows")
    side = (lax.axis_index("rows") & 1).astype(jnp.int32)[None]

    margin1, design, x0, dual, start_mine, start_other = load(side, local_x[0], dual_u[0], design)
    start_mine = start_mine + exchange(start_other, "rows", 1)

    z, sign, scale, *gram2 = load_rest(consensus_z, labels, step_size, rho, penalty, design, blocks_count)
    terms, grams, pulled = [margin1], None, None
    for step in range(lax.axis_size("feat").bit_length() - 1):
        if step > 0:
            terms = [sum(t.astype(F32) for t in terms).astype(BF16)]
        token = tie(side, terms[0])
        got = exchange(terms[0], "feat", 1 << step)
        if step == 0:
            got = tie(got, scale)
        if step == 1:
            grams = gram_rows(token, design)
            got = tie(got, grams[0])
        if step == 2:
            pulled = pulled_margins(token, scale, x0, dual, z, design)
        terms.append(got)
    if grams is None:
        grams = gram_rows(side, design)
    if pulled is None:
        pulled = pulled_margins(side, scale, x0, dual, z, design)
    terms = tie(terms, start_mine)

    resid1, margin2 = turn(sign, terms, scale, pulled, [*grams, *gram2])
    terms = square_sum(margin2, "feat")
    mask = 2
    while mask < blocks_count:
        start_mine = start_mine + exchange(start_mine, "rows", mask)
        mask *= 2
    terms = tie(terms, start_mine)

    sizes = [half * part // sum(MINE) for part in MINE]
    begins = [sum(sizes[:c]) for c in range(len(sizes))]
    other_sizes = [half * part // sum(OTHER) for part in OTHER]
    other_begins = [sum(other_sizes[:c]) for c in range(len(other_sizes))]
    count = len(sizes)
    others, received = [], []
    resid = (resid1, sign, *terms)
    for begin, size in zip(other_begins, other_sizes):
        value, other, *made = push(side, resid, scale, design, None, begin, 0, size)
        resid = made[0] if made else resid
        others.append(value)
        received.append(exchange(other, "rows", 1))
    mines, sums, places = [], [], []
    token = tie(side, others[-1])
    for begin, size in zip(begins, sizes):
        source = max(k for k, b in enumerate(other_begins) if b <= begin)
        places.append((source, begin - other_begins[source]))
        value, sent = push(token, resid, scale, design, received[source], begin, places[-1][1], size)
        mines.append(value)
        sums.append(doubling(sent, "rows", 2))
        token = tie(side, sent)
    new_x = store_x(side, scale, x0, dual, z, mines, others)

    start_theirs = exchange(tie(start_mine, mines[0]), "rows", 1)

    waiting, results = [], None
    for c, (a, b) in enumerate(sums):
        b = tie(b, new_x, results)
        piece = (a.astype(F32) + b.astype(F32)).astype(BF16)
        source, offset = places[c]
        back = exchange(piece, "rows", 1)
        ready = waiting + [(True, begins[c], 0, start_mine, mines[c], piece)]
        results = final(side, scale, x0, dual, z, ready, results, blocks_count)
        waiting = [(False, begins[c], offset, start_theirs, others[source], back)]
    results = final(side, scale, x0, dual, z, waiting, results, blocks_count)
    new_z, new_u = results
    return (new_x[None], new_z, new_u[None])


def solution(mesh):
    in_specs = (
        P("rows", "feat"),
        P(None, "rows"),
        P("rows", None, "feat"),
        P("rows", None, "feat"),
        P(None, "feat"),
        P(),
        P(),
        P(),
    )
    out_specs = (P("rows", None, "feat"), P(None, "feat"), P("rows", None, "feat"))
    return jax.shard_map(
        per_device, mesh=mesh, in_specs=in_specs, out_specs=out_specs, check_vma=False
    )
```

```python
import functools
import math

import jax
import jax.numpy as jnp
from jax import lax
from jax.experimental import pallas as pl
from jax.experimental.pallas import tpu as pltpu
from jax.sharding import PartitionSpec as P

BF16 = jnp.bfloat16
F32 = jnp.float32
MINE = (2, 3, 3)
OTHER = (2, 6)
STEP = 1024
WIDE = 2048
AHEAD = 4
NARROW = 256
WAIT_BYTES = 10_000_000
GRAM_ORDER = (0, 1, 2)
HBM = pl.BlockSpec(memory_space=pltpu.HBM)
VMEM = pl.BlockSpec(memory_space=pltpu.VMEM)
SMEM = pl.BlockSpec(memory_space=pltpu.SMEM)


def exchange(value, axis, mask):
    n = lax.axis_size(axis)
    return lax.ppermute(value, axis, [(i, i ^ mask) for i in range(n)])


def doubling(value, axis, first=1):
    n = lax.axis_size(axis)
    mask = first
    other = exchange(value, axis, mask)
    while 2 * mask < n:
        mask *= 2
        value = (value.astype(F32) + other.astype(F32)).astype(value.dtype)
        other = exchange(value, axis, mask)
    return value, other


def square_sum(value, axis):
    n = lax.axis_size(axis)
    terms = [value]
    mask = 1
    while mask < n:
        if len(terms) > 1:
            terms = [sum(t.astype(F32) for t in terms).astype(value.dtype)]
        steps = [mask, 2 * mask, 3 * mask] if 2 * mask < n else [mask]
        terms += [exchange(terms[0], axis, step) for step in steps]
        mask *= 4
    return terms


def nt(a, b):
    return lax.dot_general(a, b, (((1,), (1,)), ((), ())), preferred_element_type=F32)


def call(kernel, name, in_specs, out_shape, out_specs, scratch=(), aliases=None, limit=16, work=1000):
    return pl.pallas_call(
        kernel,
        in_specs=in_specs,
        out_shape=out_shape,
        out_specs=out_specs,
        scratch_shapes=list(scratch),
        input_output_aliases=aliases or {},
        compiler_params=pltpu.CompilerParams(vmem_limit_bytes=limit * 1024 * 1024),
        cost_estimate=pl.CostEstimate(flops=1000, bytes_accessed=work, transcendentals=0),
        name=name,
    )


def pin(space, *values):
    return [pltpu.with_memory_space_constraint(v, space) for v in values]


def columns(start, size):
    return pl.ds(pl.multiple_of(start, 128), size)


def load_kernel(blocks_count, side, x_hbm, u_hbm, z_hbm, a_hbm, sign_hbm, eta_hbm, rho_hbm, lam_hbm, *refs):
    outs, (eta_row, rho_row, lam_row, both, acc, sems) = refs[:10], refs[10:]
    m_out, pulled_out, a_out, x_out, u_out, z_out, sign_out, scale, mine_out, other_out = outs
    tasks, width = x_hbm.shape
    steps = width // STEP
    rows = ((eta_hbm, eta_row), (rho_hbm, rho_row), (lam_hbm, lam_row), (sign_hbm, sign_out))
    small = [pltpu.make_async_copy(a, b, sems.at[4, k]) for k, (a, b) in enumerate(rows)]

    def chunk(j):
        at = columns(j * STEP, STEP)
        pairs = ((x_hbm, x_out), (u_hbm, u_out), (z_hbm, z_out), (a_hbm, a_out))
        return [pltpu.make_async_copy(a.at[:, at], b.at[:, at], sems.at[k, j]) for k, (a, b) in enumerate(pairs)]

    def begin(j):
        for copy in chunk(j):
            copy.start()

    for copy in small[:3]:
        copy.start()
    for j in range(min(AHEAD, steps)):
        begin(j)
    for copy in small[:3]:
        copy.wait()
    one = lax.broadcasted_iota(jnp.int32, (tasks, tasks), 0) == lax.broadcasted_iota(jnp.int32, (tasks, tasks), 1)
    eta, rho, lam = eta_row[...], rho_row[...], lam_row[...]
    for k, row in enumerate((eta, eta * rho, lam / (rho * blocks_count))):
        upright = jnp.where(one, jnp.broadcast_to(row, (tasks, tasks)), 0.0)
        scale[:, k : k + 1] = jnp.sum(upright, axis=1, keepdims=True)
    acc[...] = jnp.zeros_like(acc)

    @pl.loop(0, steps)
    def _(j):
        for copy in chunk(j):
            copy.wait()

        @pl.when(j + AHEAD < steps)
        def _():
            begin(j + AHEAD)

        @pl.when(j == max(steps - AHEAD, 0))
        def _():
            small[3].start()

        pull = scale[:, 1:2]
        for k in range(0, STEP, NARROW):
            at, here = columns(j * STEP + k, NARROW), pl.ds(k, NARROW)
            x = x_out[:, at]
            v = x - pull * (x - z_out[:, at] + u_out[:, at])
            top = v.astype(BF16)
            both[:tasks, here] = x.astype(BF16)
            both[tasks : 2 * tasks, here] = top
            both[2 * tasks :, here] = (v - top.astype(F32)).astype(BF16)
        acc[...] += nt(both[...], a_out[:, columns(j * STEP, STEP)])

    m_out[...] = acc[:tasks].astype(BF16)
    pulled_out[...] = acc[tasks : 2 * tasks] + acc[2 * tasks :]
    half = width // 2
    mine = columns(side[0] * half, half)
    other = columns((1 - side[0]) * half, half)
    mine_out[...] = x_out[:, mine] + u_out[:, mine]
    other_out[...] = x_out[:, other] + u_out[:, other]
    small[3].wait()


def load(side, x, u, z, design, sign, step_size, rho, penalty, blocks_count):
    tasks, width = x.shape
    samples = design.shape[0]
    full = pltpu.VMEM((tasks, width), F32)
    half = pltpu.VMEM((tasks, width // 2), F32)
    rows = [v.reshape(1, tasks) for v in (step_size, rho, penalty)]
    return call(
        functools.partial(load_kernel, blocks_count),
        "load_and_margins",
        [SMEM] + [HBM] * 8,
        (
            pltpu.VMEM((tasks, samples), BF16), pltpu.VMEM((tasks, samples), F32), pltpu.VMEM(design.shape, BF16),
            full, full, full, pltpu.VMEM(sign.shape, jnp.int32), pltpu.VMEM((tasks, 128), F32), half, half,
        ),
        [VMEM] * 10,
        [pltpu.VMEM((1, tasks), F32)] * 3
        + [
            pltpu.VMEM((3 * tasks, STEP), BF16), pltpu.VMEM((3 * tasks, samples), F32),
            pltpu.SemaphoreType.DMA((5, max(width // STEP, 4))),
        ],
    )(side, *pin(pltpu.HBM, x, u, z, design, sign, *rows))


def gram_block(a_ref, row, cols, size, acc, high, low):
    width = a_ref.shape[1]
    wide = math.gcd(WIDE, width)
    for j in range(width // wide):
        at = pl.ds(j * wide, wide)
        product = nt(a_ref[pl.ds(row, size), at], a_ref[pl.ds(0, cols), at])
        acc[:, :cols] = product if j == 0 else acc[:, :cols] + product
    whole = acc[:, :cols]
    top = whole.astype(BF16)
    high[...] = top
    low[...] = (whole - top.astype(F32)).astype(BF16)


def gram_kernel(row, token, a_ref, high, low, acc):
    size = high.shape[0]
    gram_block(a_ref, row * size, (row + 1) * size, size, acc, high, low)


def gram_row(row, token, design):
    samples = design.shape[0]
    size = samples // 3
    out = pltpu.VMEM((size, (row + 1) * size), BF16)
    return call(
        functools.partial(gram_kernel, row),
        "gram",
        [SMEM, VMEM],
        (out, out),
        [VMEM] * 2,
        [pltpu.VMEM((size, (row + 1) * size), F32)],
        work=WAIT_BYTES * (row + 1) // 3,
    )(token, *pin(pltpu.VMEM, design))


def residual(sign, *terms):
    margin = sum(t.astype(F32) for t in terms)
    sign = sign.astype(F32)
    return (sign * jax.nn.sigmoid(-sign * margin)).astype(BF16)


def turn_kernel(sign, scale, pulled, *refs):
    *terms, resid, out = refs[6:]
    grams = refs[:6]
    size = grams[0].shape[0]
    resid[...] = residual(sign[...], *(t[...] for t in terms))
    eta = scale[:, 0:1]
    r = [resid[:, pl.ds(k * size, size)] for k in range(3)]
    for col in range(3):
        total = jnp.zeros((resid.shape[0], size), F32)
        for row in range(3):
            for part in range(2):
                if row >= col:
                    block = grams[2 * row + part][:, pl.ds(col * size, size)]
                    total += jnp.dot(r[row], block, preferred_element_type=F32)
                else:
                    total += nt(r[row], grams[2 * col + part][:, pl.ds(row * size, size)])
        here = pl.ds(col * size, size)
        out[:, here] = (pulled[:, here] + eta * total).astype(BF16)


def turn(sign, terms, scale, pulled, grams):
    tasks, samples = pulled.shape
    out = pltpu.VMEM((tasks, samples), BF16)
    args = [sign, scale, pulled, *grams, *terms]
    return call(turn_kernel, "turn", [VMEM] * len(args), (out, out), [VMEM] * 2)(*pin(pltpu.VMEM, *args))


def push_kernel(first, mine, begin, offset, size, side, *refs):
    tasks = refs[0].shape[0]
    if first:
        scale, a_ref, resid1, sign, *terms, h_out, sent_out, resid = refs
        resid[:tasks] = resid1[...]
        resid[tasks:] = residual(sign[...], *(t[...] for t in terms))
    else:
        scale, a_ref, resid, *received, h_out, sent_out = refs
    half = a_ref.shape[1] // 2
    eta = scale[:, 0:1]
    keep = 1.0 - scale[:, 1:2]
    base = (side[0] if mine else 1 - side[0]) * half + begin
    step = math.gcd(512, size)
    for j in range(size // step):
        at = columns(base + j * step, step)
        here = pl.ds(j * step, step)
        grads = jnp.dot(resid[...], a_ref[:, at], preferred_element_type=F32)
        push = eta * (keep * grads[:tasks] + grads[tasks:])
        h_out[:, here] = push
        if mine:
            push = push + received[0][:, pl.ds(offset + j * step, step)].astype(F32)
        sent_out[:, here] = push.astype(BF16)


def push(side, resid, scale, design, received, begin, offset, size):
    tasks = scale.shape[0]
    mine = received is not None
    first = isinstance(resid, tuple)
    args = [scale, design, *(resid if first else [resid])] + ([received] if mine else [])
    out = [pltpu.VMEM((tasks, size), F32), pltpu.VMEM((tasks, size), BF16)]
    if first:
        out.append(pltpu.VMEM((2 * tasks, design.shape[0]), BF16))
    return call(
        functools.partial(push_kernel, first, mine, begin, offset, size),
        "push_mine" if mine else "push_other",
        [SMEM] + [VMEM] * len(args),
        tuple(out),
        [VMEM] * len(out),
    )(side, *pin(pltpu.VMEM, *args))


def store_kernel(side, scale, x_ref, u_ref, z_ref, *rest):
    *hs, x_out, stage, sems = rest
    half = x_ref.shape[1] // 2
    keep = 1.0 - scale[:, 1:2]
    copies = []
    done = 0
    for c, h_ref in enumerate(hs):
        size = h_ref.shape[1]
        base = (side[0] if done < half else 1 - side[0]) * half + done % half
        done += size
        for j in range(0, size, NARROW):
            at = columns(base + j, NARROW)
            u, z = u_ref[:, at], z_ref[:, at]
            stage[:, at] = z - u + keep * keep * (x_ref[:, at] - z + u) + h_ref[:, pl.ds(j, NARROW)]
        at = columns(base, size)
        copy = pltpu.make_async_copy(stage.at[:, at], x_out.at[:, at], sems.at[c])
        copy.start()
        copies.append(copy)
    for copy in copies:
        copy.wait()


def store_x(side, scale, x, u, z, mines, others):
    tasks, width = x.shape
    args = [scale, x, u, z, *mines, *others]
    return call(
        store_kernel,
        "store_x",
        [SMEM] + [VMEM] * len(args),
        pltpu.HBM((tasks, width), F32),
        HBM,
        [pltpu.VMEM((tasks, width), F32), pltpu.SemaphoreType.DMA((len(mines) + len(others),))],
    )(side, *pin(pltpu.VMEM, *args))


def final_kernel(blocks_count, pieces, buffered, side, scale, x_ref, u_ref, z_ref, *refs):
    outs = refs[3 * len(pieces) + 2 * buffered :][:2]
    stage, sems = refs[-2:]
    half = x_ref.shape[1] // 2
    pull, limit = scale[:, 1:2], scale[:, 2:3]
    keep = 1.0 - pull
    copies, filled = [], 0
    for k, (mine, begin, offset, size) in enumerate(pieces):
        start, h, pushed = refs[3 * k : 3 * k + 3]
        base = (side[0] if mine else 1 - side[0]) * half + begin
        for j in range(0, size, NARROW):
            cut, here = columns(base + j, NARROW), pl.ds(filled + j, NARROW)
            z = z_ref[:, cut]
            total = keep * keep * start[:, pl.ds(begin + j, NARROW)] + pushed[:, pl.ds(j, NARROW)].astype(F32)
            mean = total * (1.0 / blocks_count) + pull * (1.0 + keep) * z
            new_z = mean - jnp.clip(mean, -limit, limit)
            moved = z + keep * keep * (x_ref[:, cut] - z + u_ref[:, cut]) + h[:, pl.ds(offset + j, NARROW)]
            stage[0, :, here] = new_z
            stage[1, :, here] = moved - new_z
        cut, here = columns(base, size), pl.ds(filled, size)
        for o in range(2):
            copy = pltpu.make_async_copy(stage.at[o, :, here], outs[o].at[:, cut], sems.at[k, o])
            copy.start()
            copies.append(copy)
        filled += size
    for copy in copies:
        copy.wait()


def final(side, scale, x, u, z, pieces, buffers, blocks_count):
    tasks, width = x.shape
    buffered = buffers is not None
    args = pin(pltpu.VMEM, scale, x, u, z, *(v for piece in pieces for v in piece[3:]))
    vmem = len(args)
    places = [(*piece[:3], piece[5].shape[1]) for piece in pieces]
    out = pltpu.HBM((tasks, width), F32)
    aliases = {}
    if buffered:
        aliases = {1 + vmem + o: o for o in range(2)}
        args += pin(pltpu.HBM, *buffers)
    return call(
        functools.partial(final_kernel, blocks_count, places, buffered),
        "final",
        [SMEM] + [VMEM] * vmem + [HBM] * (2 * buffered),
        (out, out),
        [HBM] * 2,
        [pltpu.VMEM((2, tasks, sum(p[3] for p in places)), F32), pltpu.SemaphoreType.DMA((len(pieces), 2))],
        aliases,
    )(side, *args)


def tie(value, *after):
    return lax.optimization_barrier((value, after))[0]


def per_device(design, labels, local_x, dual_u, consensus_z, step_size, rho, penalty):
    tasks, width = consensus_z.shape
    half = width // 2
    blocks_count = lax.axis_size("rows")
    side = (lax.axis_index("rows") & 1).astype(jnp.int32)[None]

    margin1, pulled, design, x0, dual, z, sign, scale, start_mine, start_other = load(
        side, local_x[0], dual_u[0], consensus_z, design, labels, step_size, rho, penalty, blocks_count
    )
    start_mine = start_mine + exchange(start_other, "rows", 1)

    terms, grams = [margin1], []
    for step in range(max(lax.axis_size("feat").bit_length() - 1, 3)):
        more = (1 << step) < lax.axis_size("feat")
        if step > 0 and more:
            terms = [sum(t.astype(F32) for t in terms).astype(BF16)]
        row = gram_row(GRAM_ORDER[step], tie(side, terms[0]), design) if step < 3 else []
        grams.append(row)
        if more:
            got = exchange(terms[0], "feat", 1 << step)
            terms.append(tie(got, row[0], start_mine) if step == 0 else tie(got, row[0]) if step == 1 else got)

    resid1, margin2 = turn(sign, terms, scale, pulled, [g for row in range(3) for g in grams[GRAM_ORDER.index(row)]])
    terms = square_sum(margin2, "feat")
    mask = 2
    while mask < blocks_count:
        start_mine = start_mine + exchange(start_mine, "rows", mask)
        mask *= 2
    sizes = [half * part // sum(MINE) for part in MINE]
    begins = [sum(sizes[:c]) for c in range(len(sizes))]
    other_sizes = [half * part // sum(OTHER) for part in OTHER]
    other_begins = [sum(other_sizes[:c]) for c in range(len(other_sizes))]
    count = len(sizes)
    others, received = [], []
    resid = (resid1, sign, *terms)
    for begin, size in zip(other_begins, other_sizes):
        value, other, *made = push(side, resid, scale, design, None, begin, 0, size)
        resid = made[0] if made else resid
        others.append(value)
        received.append(exchange(other, "rows", 1))
    mines, sums, places = [], [], []
    token = tie(side, others[-1])
    for begin, size in zip(begins, sizes):
        source = max(k for k, b in enumerate(other_begins) if b <= begin)
        places.append((source, begin - other_begins[source]))
        value, sent = push(token, resid, scale, design, received[source], begin, places[-1][1], size)
        mines.append(value)
        sums.append(doubling(sent, "rows", 2))
        token = tie(side, sent)
    new_x = store_x(side, scale, x0, dual, z, mines, others)

    start_theirs = exchange(tie(start_mine, mines[0]), "rows", 1)

    waiting, results = [], None
    for c, (a, b) in enumerate(sums):
        b = tie(b, new_x, results)
        piece = (a.astype(F32) + b.astype(F32)).astype(BF16)
        source, offset = places[c]
        back = exchange(piece, "rows", 1)
        ready = waiting + [(True, begins[c], 0, start_mine, mines[c], piece)]
        results = final(side, scale, x0, dual, z, ready, results, blocks_count)
        waiting = [(False, begins[c], offset, start_theirs, others[source], back)]
    results = final(side, scale, x0, dual, z, waiting, results, blocks_count)
    new_z, new_u = results
    return (new_x[None], new_z, new_u[None])


def solution(mesh):
    in_specs = (
        P("rows", "feat"),
        P(None, "rows"),
        P("rows", None, "feat"),
        P("rows", None, "feat"),
        P(None, "feat"),
        P(),
        P(),
        P(),
    )
    out_specs = (P("rows", None, "feat"), P(None, "feat"), P("rows", None, "feat"))
    return jax.shard_map(
        per_device, mesh=mesh, in_specs=in_specs, out_specs=out_specs, check_vma=False
    )
```

```python
import functools
import math

import jax
import jax.numpy as jnp
from jax import lax
from jax.experimental import pallas as pl
from jax.experimental.pallas import tpu as pltpu
from jax.sharding import PartitionSpec as P

BF16 = jnp.bfloat16
F32 = jnp.float32
MINE = (3, 5)
OTHER = (3, 5)
STEP = 1024
WIDE = 2048
AHEAD = 4
NARROW = 256
WAIT_BYTES = 10_000_000
HBM = pl.BlockSpec(memory_space=pltpu.HBM)
VMEM = pl.BlockSpec(memory_space=pltpu.VMEM)
SMEM = pl.BlockSpec(memory_space=pltpu.SMEM)


def exchange(value, axis, mask):
    n = lax.axis_size(axis)
    return lax.ppermute(value, axis, [(i, i ^ mask) for i in range(n)])


def doubling(value, axis, first=1):
    n = lax.axis_size(axis)
    mask = first
    other = exchange(value, axis, mask)
    while 2 * mask < n:
        mask *= 2
        value = (value.astype(F32) + other.astype(F32)).astype(value.dtype)
        other = exchange(value, axis, mask)
    return value, other


def sum_terms(terms):
    return sum(t.astype(F32) for t in terms).astype(BF16)


def square_stage(value, axis, mask):
    steps = [mask, 2 * mask, 3 * mask] if 2 * mask < lax.axis_size(axis) else [mask]
    return [value] + [exchange(value, axis, step) for step in steps]


def square_sum(value, axis):
    terms, mask = square_stage(value, axis, 1), 4
    while mask < lax.axis_size(axis):
        terms = square_stage(sum_terms(terms), axis, mask)
        mask *= 4
    return terms


def nt(a, b):
    return lax.dot_general(a, b, (((1,), (1,)), ((), ())), preferred_element_type=F32)


def call(kernel, name, in_specs, out_shape, out_specs, scratch=(), aliases=None, limit=16, work=1000):
    return pl.pallas_call(
        kernel,
        in_specs=in_specs,
        out_shape=out_shape,
        out_specs=out_specs,
        scratch_shapes=list(scratch),
        input_output_aliases=aliases or {},
        compiler_params=pltpu.CompilerParams(vmem_limit_bytes=limit * 1024 * 1024),
        cost_estimate=pl.CostEstimate(flops=1000, bytes_accessed=work, transcendentals=0),
        name=name,
    )


def pin(space, *values):
    return [pltpu.with_memory_space_constraint(v, space) for v in values]


def columns(start, size):
    return pl.ds(pl.multiple_of(start, 128), size)


def load_kernel(blocks_count, side, x_hbm, u_hbm, z_hbm, a_hbm, sign_hbm, eta_hbm, rho_hbm, lam_hbm, *refs):
    outs, (eta_row, rho_row, lam_row, both, acc, sems) = refs[:10], refs[10:]
    m_out, pulled_out, a_out, x_out, u_out, z_out, sign_out, scale, mine_out, other_out = outs
    tasks, width = x_hbm.shape
    steps = width // STEP
    rows = ((eta_hbm, eta_row), (rho_hbm, rho_row), (lam_hbm, lam_row), (sign_hbm, sign_out))
    small = [pltpu.make_async_copy(a, b, sems.at[4, k]) for k, (a, b) in enumerate(rows)]

    def chunk(j):
        at = columns(j * STEP, STEP)
        pairs = ((x_hbm, x_out), (u_hbm, u_out), (z_hbm, z_out), (a_hbm, a_out))
        return [pltpu.make_async_copy(a.at[:, at], b.at[:, at], sems.at[k, j]) for k, (a, b) in enumerate(pairs)]

    def begin(j):
        for copy in chunk(j):
            copy.start()

    for copy in small[:3]:
        copy.start()
    for j in range(min(AHEAD, steps)):
        begin(j)
    for copy in small[:3]:
        copy.wait()
    one = lax.broadcasted_iota(jnp.int32, (tasks, tasks), 0) == lax.broadcasted_iota(jnp.int32, (tasks, tasks), 1)
    eta, rho, lam = eta_row[...], rho_row[...], lam_row[...]
    for k, row in enumerate((eta, eta * rho, lam / (rho * blocks_count))):
        upright = jnp.where(one, jnp.broadcast_to(row, (tasks, tasks)), 0.0)
        scale[:, k : k + 1] = jnp.sum(upright, axis=1, keepdims=True)
    acc[...] = jnp.zeros_like(acc)

    @pl.loop(0, steps)
    def _(j):
        for copy in chunk(j):
            copy.wait()

        @pl.when(j + AHEAD < steps)
        def _():
            begin(j + AHEAD)

        @pl.when(j == max(steps - AHEAD, 0))
        def _():
            small[3].start()

        pull = scale[:, 1:2]
        for k in range(0, STEP, NARROW):
            at, here = columns(j * STEP + k, NARROW), pl.ds(k, NARROW)
            x = x_out[:, at]
            v = x - pull * (x - z_out[:, at] + u_out[:, at])
            top = v.astype(BF16)
            both[:tasks, here] = x.astype(BF16)
            both[tasks : 2 * tasks, here] = top
            both[2 * tasks :, here] = (v - top.astype(F32)).astype(BF16)
        acc[...] += nt(both[...], a_out[:, columns(j * STEP, STEP)])

    m_out[...] = acc[:tasks].astype(BF16)
    pulled_out[...] = acc[tasks : 2 * tasks] + acc[2 * tasks :]
    half = width // 2
    mine = columns(side[0] * half, half)
    other = columns((1 - side[0]) * half, half)
    mine_out[...] = x_out[:, mine] + u_out[:, mine]
    other_out[...] = x_out[:, other] + u_out[:, other]
    small[3].wait()


def load(side, x, u, z, design, sign, step_size, rho, penalty, blocks_count):
    tasks, width = x.shape
    samples = design.shape[0]
    full = pltpu.VMEM((tasks, width), F32)
    half = pltpu.VMEM((tasks, width // 2), F32)
    rows = [v.reshape(1, tasks) for v in (step_size, rho, penalty)]
    return call(
        functools.partial(load_kernel, blocks_count),
        "load_and_margins",
        [SMEM] + [HBM] * 8,
        (
            pltpu.VMEM((tasks, samples), BF16), pltpu.VMEM((tasks, samples), F32), pltpu.VMEM(design.shape, BF16),
            full, full, full, pltpu.VMEM(sign.shape, jnp.int32), pltpu.VMEM((tasks, 128), F32), half, half,
        ),
        [VMEM] * 10,
        [pltpu.VMEM((1, tasks), F32)] * 3
        + [
            pltpu.VMEM((3 * tasks, STEP), BF16), pltpu.VMEM((3 * tasks, samples), F32),
            pltpu.SemaphoreType.DMA((5, max(width // STEP, 4))),
        ],
    )(side, *pin(pltpu.HBM, x, u, z, design, sign, *rows))


def gram_block(a_ref, row, cols, size, acc, high, low):
    width = a_ref.shape[1]
    wide = math.gcd(WIDE, width)
    for j in range(width // wide):
        at = pl.ds(j * wide, wide)
        product = nt(a_ref[pl.ds(row, size), at], a_ref[pl.ds(0, cols), at])
        acc[:, :cols] = product if j == 0 else acc[:, :cols] + product
    whole = acc[:, :cols]
    top = whole.astype(BF16)
    high[...] = top
    low[...] = (whole - top.astype(F32)).astype(BF16)


def gram_kernel(row, token, a_ref, high, low, acc):
    size = high.shape[0]
    gram_block(a_ref, row * size, (row + 1) * size, size, acc, high, low)


def gram_row(row, token, design):
    samples = design.shape[0]
    size = samples // 3
    out = pltpu.VMEM((size, (row + 1) * size), BF16)
    return call(
        functools.partial(gram_kernel, row),
        "gram",
        [SMEM, VMEM],
        (out, out),
        [VMEM] * 2,
        [pltpu.VMEM((size, (row + 1) * size), F32)],
        work=WAIT_BYTES * (row + 1) // 3,
    )(token, *pin(pltpu.VMEM, design))


def residual(sign, *terms):
    margin = sum(t.astype(F32) for t in terms)
    sign = sign.astype(F32)
    return (sign * jax.nn.sigmoid(-sign * margin)).astype(BF16)


def turn_kernel(sign, scale, pulled, *refs):
    *terms, resid, out = refs[6:]
    grams = refs[:6]
    size = grams[0].shape[0]
    resid[...] = residual(sign[...], *(t[...] for t in terms))
    eta = scale[:, 0:1]
    r = [resid[:, pl.ds(k * size, size)] for k in range(3)]
    for col in range(3):
        total = jnp.zeros((resid.shape[0], size), F32)
        for row in range(3):
            for part in range(2):
                if row >= col:
                    block = grams[2 * row + part][:, pl.ds(col * size, size)]
                    total += jnp.dot(r[row], block, preferred_element_type=F32)
                else:
                    total += nt(r[row], grams[2 * col + part][:, pl.ds(row * size, size)])
        here = pl.ds(col * size, size)
        out[:, here] = (pulled[:, here] + eta * total).astype(BF16)


def turn(sign, terms, scale, pulled, grams):
    tasks, samples = pulled.shape
    out = pltpu.VMEM((tasks, samples), BF16)
    args = [sign, scale, pulled, *grams, *terms]
    return call(turn_kernel, "turn", [VMEM] * len(args), (out, out), [VMEM] * 2)(*pin(pltpu.VMEM, *args))


def push_kernel(first, mine, begin, offset, size, side, *refs):
    tasks = refs[0].shape[0]
    if first:
        scale, a_ref, resid1, sign, *terms, h_out, sent_out, resid = refs
        resid[:tasks] = resid1[...]
        resid[tasks:] = residual(sign[...], *(t[...] for t in terms))
    else:
        scale, a_ref, resid, *received, h_out, sent_out = refs
    half = a_ref.shape[1] // 2
    eta = scale[:, 0:1]
    keep = 1.0 - scale[:, 1:2]
    base = (side[0] if mine else 1 - side[0]) * half + begin
    step = math.gcd(512, size)
    for j in range(size // step):
        at = columns(base + j * step, step)
        here = pl.ds(j * step, step)
        grads = jnp.dot(resid[...], a_ref[:, at], preferred_element_type=F32)
        push = eta * (keep * grads[:tasks] + grads[tasks:])
        h_out[:, here] = push
        if mine:
            push = push + received[0][:, pl.ds(offset + j * step, step)].astype(F32)
        sent_out[:, here] = push.astype(BF16)


def push(side, resid, scale, design, received, begin, offset, size):
    tasks = scale.shape[0]
    mine = received is not None
    first = isinstance(resid, tuple)
    args = [scale, design, *(resid if first else [resid])] + ([received] if mine else [])
    out = [pltpu.VMEM((tasks, size), F32), pltpu.VMEM((tasks, size), BF16)]
    if first:
        out.append(pltpu.VMEM((2 * tasks, design.shape[0]), BF16))
    return call(
        functools.partial(push_kernel, first, mine, begin, offset, size),
        "push_mine" if mine else "push_other",
        [SMEM] + [VMEM] * len(args),
        tuple(out),
        [VMEM] * len(out),
    )(side, *pin(pltpu.VMEM, *args))


def store_kernel(side, scale, x_ref, u_ref, z_ref, *rest):
    *hs, x_out, stage, sems = rest
    half = x_ref.shape[1] // 2
    keep = 1.0 - scale[:, 1:2]
    copies = []
    done = 0
    for c, h_ref in enumerate(hs):
        size = h_ref.shape[1]
        base = (side[0] if done < half else 1 - side[0]) * half + done % half
        done += size
        for j in range(0, size, NARROW):
            at = columns(base + j, NARROW)
            u, z = u_ref[:, at], z_ref[:, at]
            stage[:, at] = z - u + keep * keep * (x_ref[:, at] - z + u) + h_ref[:, pl.ds(j, NARROW)]
        at = columns(base, size)
        copy = pltpu.make_async_copy(stage.at[:, at], x_out.at[:, at], sems.at[c])
        copy.start()
        copies.append(copy)
    for copy in copies:
        copy.wait()


def store_x(side, scale, x, u, z, mines, others):
    tasks, width = x.shape
    args = [scale, x, u, z, *mines, *others]
    return call(
        store_kernel,
        "store_x",
        [SMEM] + [VMEM] * len(args),
        pltpu.HBM((tasks, width), F32),
        HBM,
        [pltpu.VMEM((tasks, width), F32), pltpu.SemaphoreType.DMA((len(mines) + len(others),))],
    )(side, *pin(pltpu.VMEM, *args))


def final_kernel(blocks_count, pieces, buffered, side, scale, x_ref, u_ref, z_ref, *refs):
    outs = refs[3 * len(pieces) + 2 * buffered :][:2]
    stage, sems = refs[-2:]
    half = x_ref.shape[1] // 2
    pull, limit = scale[:, 1:2], scale[:, 2:3]
    keep = 1.0 - pull
    copies, filled = [], 0
    for k, (mine, begin, offset, size) in enumerate(pieces):
        start, h, pushed = refs[3 * k : 3 * k + 3]
        base = (side[0] if mine else 1 - side[0]) * half + begin
        for j in range(0, size, NARROW):
            cut, here = columns(base + j, NARROW), pl.ds(filled + j, NARROW)
            z = z_ref[:, cut]
            total = keep * keep * start[:, pl.ds(begin + j, NARROW)] + pushed[:, pl.ds(j, NARROW)].astype(F32)
            mean = total * (1.0 / blocks_count) + pull * (1.0 + keep) * z
            new_z = mean - jnp.clip(mean, -limit, limit)
            moved = z + keep * keep * (x_ref[:, cut] - z + u_ref[:, cut]) + h[:, pl.ds(offset + j, NARROW)]
            stage[0, :, here] = new_z
            stage[1, :, here] = moved - new_z
        cut, here = columns(base, size), pl.ds(filled, size)
        for o in range(2):
            copy = pltpu.make_async_copy(stage.at[o, :, here], outs[o].at[:, cut], sems.at[k, o])
            copy.start()
            copies.append(copy)
        filled += size
    for copy in copies:
        copy.wait()


def final(side, scale, x, u, z, pieces, buffers, blocks_count):
    tasks, width = x.shape
    buffered = buffers is not None
    args = pin(pltpu.VMEM, scale, x, u, z, *(v for piece in pieces for v in piece[3:]))
    vmem = len(args)
    places = [(*piece[:3], piece[5].shape[1]) for piece in pieces]
    out = pltpu.HBM((tasks, width), F32)
    aliases = {}
    if buffered:
        aliases = {1 + vmem + o: o for o in range(2)}
        args += pin(pltpu.HBM, *buffers)
    return call(
        functools.partial(final_kernel, blocks_count, places, buffered),
        "final",
        [SMEM] + [VMEM] * vmem + [HBM] * (2 * buffered),
        (out, out),
        [HBM] * 2,
        [pltpu.VMEM((2, tasks, sum(p[3] for p in places)), F32), pltpu.SemaphoreType.DMA((len(pieces), 2))],
        aliases,
    )(side, *args)


def tie(value, *after):
    return lax.optimization_barrier((value, after))[0]


def per_device(design, labels, local_x, dual_u, consensus_z, step_size, rho, penalty):
    tasks, width = consensus_z.shape
    half = width // 2
    blocks_count = lax.axis_size("rows")
    side = (lax.axis_index("rows") & 1).astype(jnp.int32)[None]

    margin1, pulled, design, x0, dual, z, sign, scale, start_mine, start_other = load(
        side, local_x[0], dual_u[0], consensus_z, design, labels, step_size, rho, penalty, blocks_count
    )
    start_mine = start_mine + exchange(start_other, "rows", 1)

    half_rows = [gram_row(row, side, design) for row in range(2)]
    terms = square_stage(margin1, "feat", 1)
    terms = [terms[0]] + [tie(t, half_rows, start_mine) for t in terms[1:]]
    stage, mask = terms, 4
    last_row = None
    while mask < lax.axis_size("feat"):
        value = sum_terms(stage)
        if last_row is None:
            last_row = gram_row(2, tie(side, value), design)
        stage = square_stage(value, "feat", mask)
        mask *= 4
    terms = stage
    if last_row is None:
        last_row = gram_row(2, side, design)
    grams = [*half_rows[0], *half_rows[1], *last_row]

    resid1, margin2 = turn(sign, terms, scale, pulled, grams)
    terms = square_sum(margin2, "feat")
    mask = 2
    while mask < blocks_count:
        start_mine = start_mine + exchange(start_mine, "rows", mask)
        mask *= 2
    sizes = [half * part // sum(MINE) for part in MINE]
    begins = [sum(sizes[:c]) for c in range(len(sizes))]
    other_sizes = [half * part // sum(OTHER) for part in OTHER]
    other_begins = [sum(other_sizes[:c]) for c in range(len(other_sizes))]
    count = len(sizes)
    others, received = [], []
    resid = (resid1, sign, *terms)
    for begin, size in zip(other_begins, other_sizes):
        value, other, *made = push(side, resid, scale, design, None, begin, 0, size)
        resid = made[0] if made else resid
        others.append(value)
        received.append(exchange(other, "rows", 1))
    mines, sums, places = [], [], []
    token = tie(side, others[-1])
    for begin, size in zip(begins, sizes):
        source = max(k for k, b in enumerate(other_begins) if b <= begin)
        places.append((source, begin - other_begins[source]))
        value, sent = push(token, resid, scale, design, received[source], begin, places[-1][1], size)
        mines.append(value)
        sums.append(doubling(sent, "rows", 2))
        token = tie(side, sent)
    new_x = store_x(side, scale, x0, dual, z, mines, others)

    start_theirs = exchange(tie(start_mine, mines[0]), "rows", 1)

    waiting, results = [], None
    for c, (a, b) in enumerate(sums):
        b = tie(b, new_x, results)
        piece = (a.astype(F32) + b.astype(F32)).astype(BF16)
        source, offset = places[c]
        back = exchange(piece, "rows", 1)
        results = final(
            side, scale, x0, dual, z, [(True, begins[c], 0, start_mine, mines[c], piece)], results, blocks_count
        )
        results = final(
            side, scale, x0, dual, z, [(False, begins[c], offset, start_theirs, others[source], back)], results, blocks_count
        )
    new_z, new_u = results
    return (new_x[None], new_z, new_u[None])


def solution(mesh):
    in_specs = (
        P("rows", "feat"),
        P(None, "rows"),
        P("rows", None, "feat"),
        P("rows", None, "feat"),
        P(None, "feat"),
        P(),
        P(),
        P(),
    )
    out_specs = (P("rows", None, "feat"), P(None, "feat"), P("rows", None, "feat"))
    return jax.shard_map(
        per_device, mesh=mesh, in_specs=in_specs, out_specs=out_specs, check_vma=False
    )
```

```python
import functools
import math

import jax
import jax.numpy as jnp
from jax import lax
from jax.experimental import pallas as pl
from jax.experimental.pallas import tpu as pltpu
from jax.sharding import PartitionSpec as P

BF16 = jnp.bfloat16
F32 = jnp.float32
PLAN = ((((True, 0),),), (((False, 0), (True, 1)),), (((False, 1), (True, 2)), ((False, 2),)))
MINE = (3, 3, 2)
OTHER = (3, 5)
STEP = 1024
WIDE = 2048
AHEAD = 8
NARROW = 256
WAIT_BYTES = 10_000_000
GRAM_ORDER = (0, 1, 2)
HBM = pl.BlockSpec(memory_space=pltpu.HBM)
VMEM = pl.BlockSpec(memory_space=pltpu.VMEM)
SMEM = pl.BlockSpec(memory_space=pltpu.SMEM)


def exchange(value, axis, mask):
    n = lax.axis_size(axis)
    return lax.ppermute(value, axis, [(i, i ^ mask) for i in range(n)])


def doubling(value, axis, first=1):
    n = lax.axis_size(axis)
    mask = first
    other = exchange(value, axis, mask)
    while 2 * mask < n:
        mask *= 2
        value = (value.astype(F32) + other.astype(F32)).astype(value.dtype)
        other = exchange(value, axis, mask)
    return value, other


def square_sum(value, axis):
    n = lax.axis_size(axis)
    terms = [value]
    mask = 1
    while mask < n:
        if len(terms) > 1:
            terms = [sum(t.astype(F32) for t in terms).astype(value.dtype)]
        steps = [mask, 2 * mask, 3 * mask] if 2 * mask < n else [mask]
        terms += [exchange(terms[0], axis, step) for step in steps]
        mask *= 4
    return terms


def nt(a, b):
    return lax.dot_general(a, b, (((1,), (1,)), ((), ())), preferred_element_type=F32)


def call(kernel, name, in_specs, out_shape, out_specs, scratch=(), aliases=None, limit=16, work=1000):
    return pl.pallas_call(
        kernel,
        in_specs=in_specs,
        out_shape=out_shape,
        out_specs=out_specs,
        scratch_shapes=list(scratch),
        input_output_aliases=aliases or {},
        compiler_params=pltpu.CompilerParams(vmem_limit_bytes=limit * 1024 * 1024),
        cost_estimate=pl.CostEstimate(flops=1000, bytes_accessed=work, transcendentals=0),
        name=name,
    )


def pin(space, *values):
    return [pltpu.with_memory_space_constraint(v, space) for v in values]


def columns(start, size):
    return pl.ds(pl.multiple_of(start, 128), size)


def load_kernel(blocks_count, side, x_hbm, u_hbm, z_hbm, a_hbm, sign_hbm, eta_hbm, rho_hbm, lam_hbm, *refs):
    outs, (eta_row, rho_row, lam_row, both, acc, sems) = refs[:10], refs[10:]
    m_out, pulled_out, a_out, x_out, u_out, z_out, sign_out, scale, mine_out, other_out = outs
    tasks, width = x_hbm.shape
    steps = width // STEP
    rows = ((eta_hbm, eta_row), (rho_hbm, rho_row), (lam_hbm, lam_row), (sign_hbm, sign_out))
    small = [pltpu.make_async_copy(a, b, sems.at[4, k]) for k, (a, b) in enumerate(rows)]

    def chunk(j):
        at = columns(j * STEP, STEP)
        pairs = ((x_hbm, x_out), (u_hbm, u_out), (z_hbm, z_out), (a_hbm, a_out))
        return [pltpu.make_async_copy(a.at[:, at], b.at[:, at], sems.at[k, j]) for k, (a, b) in enumerate(pairs)]

    def begin(j):
        for copy in chunk(j):
            copy.start()

    for copy in small[:3]:
        copy.start()
    for j in range(min(AHEAD, steps)):
        begin(j)
    for copy in small[:3]:
        copy.wait()
    one = lax.broadcasted_iota(jnp.int32, (tasks, tasks), 0) == lax.broadcasted_iota(jnp.int32, (tasks, tasks), 1)
    eta, rho, lam = eta_row[...], rho_row[...], lam_row[...]
    for k, row in enumerate((eta, eta * rho, lam / (rho * blocks_count))):
        upright = jnp.where(one, jnp.broadcast_to(row, (tasks, tasks)), 0.0)
        scale[:, k : k + 1] = jnp.sum(upright, axis=1, keepdims=True)
    acc[...] = jnp.zeros_like(acc)

    @pl.loop(0, steps)
    def _(j):
        for copy in chunk(j):
            copy.wait()

        @pl.when(j + AHEAD < steps)
        def _():
            begin(j + AHEAD)

        @pl.when(j == max(steps - AHEAD, 0))
        def _():
            small[3].start()

        pull = scale[:, 1:2]
        for k in range(0, STEP, NARROW):
            at, here = columns(j * STEP + k, NARROW), pl.ds(k, NARROW)
            x = x_out[:, at]
            v = x - pull * (x - z_out[:, at] + u_out[:, at])
            top = v.astype(BF16)
            both[:tasks, here] = x.astype(BF16)
            both[tasks : 2 * tasks, here] = top
            both[2 * tasks :, here] = (v - top.astype(F32)).astype(BF16)
        acc[...] += nt(both[...], a_out[:, columns(j * STEP, STEP)])

    m_out[...] = acc[:tasks].astype(BF16)
    pulled_out[...] = acc[tasks : 2 * tasks] + acc[2 * tasks :]
    half = width // 2
    mine = columns(side[0] * half, half)
    other = columns((1 - side[0]) * half, half)
    mine_out[...] = x_out[:, mine] + u_out[:, mine]
    other_out[...] = x_out[:, other] + u_out[:, other]
    small[3].wait()


def load(side, x, u, z, design, sign, step_size, rho, penalty, blocks_count):
    tasks, width = x.shape
    samples = design.shape[0]
    full = pltpu.VMEM((tasks, width), F32)
    half = pltpu.VMEM((tasks, width // 2), F32)
    rows = [v.reshape(1, tasks) for v in (step_size, rho, penalty)]
    return call(
        functools.partial(load_kernel, blocks_count),
        "load_and_margins",
        [SMEM] + [HBM] * 8,
        (
            pltpu.VMEM((tasks, samples), BF16), pltpu.VMEM((tasks, samples), F32), pltpu.VMEM(design.shape, BF16),
            full, full, full, pltpu.VMEM(sign.shape, jnp.int32), pltpu.VMEM((tasks, 128), F32), half, half,
        ),
        [VMEM] * 10,
        [pltpu.VMEM((1, tasks), F32)] * 3
        + [
            pltpu.VMEM((3 * tasks, STEP), BF16), pltpu.VMEM((3 * tasks, samples), F32),
            pltpu.SemaphoreType.DMA((5, max(width // STEP, 4))),
        ],
    )(side, *pin(pltpu.HBM, x, u, z, design, sign, *rows))


def gram_block(a_ref, row, cols, size, acc, high, low):
    width = a_ref.shape[1]
    wide = math.gcd(WIDE, width)
    for j in range(width // wide):
        at = pl.ds(j * wide, wide)
        product = nt(a_ref[pl.ds(row, size), at], a_ref[pl.ds(0, cols), at])
        acc[:, :cols] = product if j == 0 else acc[:, :cols] + product
    whole = acc[:, :cols]
    top = whole.astype(BF16)
    high[...] = top
    low[...] = (whole - top.astype(F32)).astype(BF16)


def gram_kernel(row, token, a_ref, high, low, acc):
    size = high.shape[0]
    gram_block(a_ref, row * size, (row + 1) * size, size, acc, high, low)


def gram_row(row, token, design):
    samples = design.shape[0]
    size = samples // 3
    out = pltpu.VMEM((size, (row + 1) * size), BF16)
    return call(
        functools.partial(gram_kernel, row),
        "gram",
        [SMEM, VMEM],
        (out, out),
        [VMEM] * 2,
        [pltpu.VMEM((size, (row + 1) * size), F32)],
        work=WAIT_BYTES * (row + 1) // 3,
    )(token, *pin(pltpu.VMEM, design))


def residual(sign, *terms):
    margin = sum(t.astype(F32) for t in terms)
    sign = sign.astype(F32)
    return (sign * jax.nn.sigmoid(-sign * margin)).astype(BF16)


def turn_kernel(sign, scale, pulled, *refs):
    *terms, resid, out = refs[6:]
    grams = refs[:6]
    size = grams[0].shape[0]
    resid[...] = residual(sign[...], *(t[...] for t in terms))
    eta = scale[:, 0:1]
    r = [resid[:, pl.ds(k * size, size)] for k in range(3)]
    for col in range(3):
        total = jnp.zeros((resid.shape[0], size), F32)
        for row in range(3):
            for part in range(2):
                if row >= col:
                    block = grams[2 * row + part][:, pl.ds(col * size, size)]
                    total += jnp.dot(r[row], block, preferred_element_type=F32)
                else:
                    total += nt(r[row], grams[2 * col + part][:, pl.ds(row * size, size)])
        here = pl.ds(col * size, size)
        out[:, here] = (pulled[:, here] + eta * total).astype(BF16)


def turn(sign, terms, scale, pulled, grams):
    tasks, samples = pulled.shape
    out = pltpu.VMEM((tasks, samples), BF16)
    args = [sign, scale, pulled, *grams, *terms]
    return call(turn_kernel, "turn", [VMEM] * len(args), (out, out), [VMEM] * 2)(*pin(pltpu.VMEM, *args))


def push_kernel(first, mine, begin, offset, size, side, *refs):
    tasks = refs[0].shape[0]
    if first:
        scale, a_ref, resid1, sign, *terms, h_out, sent_out, resid = refs
        resid[:tasks] = resid1[...]
        resid[tasks:] = residual(sign[...], *(t[...] for t in terms))
    else:
        scale, a_ref, resid, *received, h_out, sent_out = refs
    half = a_ref.shape[1] // 2
    eta = scale[:, 0:1]
    keep = 1.0 - scale[:, 1:2]
    base = (side[0] if mine else 1 - side[0]) * half + begin
    step = math.gcd(512, size)
    for j in range(size // step):
        at = columns(base + j * step, step)
        here = pl.ds(j * step, step)
        grads = jnp.dot(resid[...], a_ref[:, at], preferred_element_type=F32)
        push = eta * (keep * grads[:tasks] + grads[tasks:])
        h_out[:, here] = push
        if mine:
            push = push + received[0][:, pl.ds(offset + j * step, step)].astype(F32)
        sent_out[:, here] = push.astype(BF16)


def push(side, resid, scale, design, received, begin, offset, size):
    tasks = scale.shape[0]
    mine = received is not None
    first = isinstance(resid, tuple)
    args = [scale, design, *(resid if first else [resid])] + ([received] if mine else [])
    out = [pltpu.VMEM((tasks, size), F32), pltpu.VMEM((tasks, size), BF16)]
    if first:
        out.append(pltpu.VMEM((2 * tasks, design.shape[0]), BF16))
    return call(
        functools.partial(push_kernel, first, mine, begin, offset, size),
        "push_mine" if mine else "push_other",
        [SMEM] + [VMEM] * len(args),
        tuple(out),
        [VMEM] * len(out),
    )(side, *pin(pltpu.VMEM, *args))


def store_kernel(side, scale, x_ref, u_ref, z_ref, *rest):
    *hs, x_out, stage, sems = rest
    half = x_ref.shape[1] // 2
    keep = 1.0 - scale[:, 1:2]
    copies = []
    done = 0
    for c, h_ref in enumerate(hs):
        size = h_ref.shape[1]
        base = (side[0] if done < half else 1 - side[0]) * half + done % half
        done += size
        for j in range(0, size, NARROW):
            at = columns(base + j, NARROW)
            u, z = u_ref[:, at], z_ref[:, at]
            stage[:, at] = z - u + keep * keep * (x_ref[:, at] - z + u) + h_ref[:, pl.ds(j, NARROW)]
        at = columns(base, size)
        copy = pltpu.make_async_copy(stage.at[:, at], x_out.at[:, at], sems.at[c])
        copy.start()
        copies.append(copy)
    for copy in copies:
        copy.wait()


def store_x(side, scale, x, u, z, mines, others):
    tasks, width = x.shape
    args = [scale, x, u, z, *mines, *others]
    return call(
        store_kernel,
        "store_x",
        [SMEM] + [VMEM] * len(args),
        pltpu.HBM((tasks, width), F32),
        HBM,
        [pltpu.VMEM((tasks, width), F32), pltpu.SemaphoreType.DMA((len(mines) + len(others),))],
    )(side, *pin(pltpu.VMEM, *args))


def final_kernel(blocks_count, pieces, buffered, side, scale, x_ref, u_ref, z_ref, *refs):
    outs = refs[3 * len(pieces) + 2 * buffered :][:2]
    stage, sems = refs[-2:]
    half = x_ref.shape[1] // 2
    pull, limit = scale[:, 1:2], scale[:, 2:3]
    keep = 1.0 - pull
    copies, filled = [], 0
    for k, (mine, begin, offset, size) in enumerate(pieces):
        start, h, pushed = refs[3 * k : 3 * k + 3]
        base = (side[0] if mine else 1 - side[0]) * half + begin
        for j in range(0, size, NARROW):
            cut, here = columns(base + j, NARROW), pl.ds(filled + j, NARROW)
            z = z_ref[:, cut]
            total = keep * keep * start[:, pl.ds(begin + j, NARROW)] + pushed[:, pl.ds(j, NARROW)].astype(F32)
            mean = total * (1.0 / blocks_count) + pull * (1.0 + keep) * z
            new_z = mean - jnp.clip(mean, -limit, limit)
            moved = z + keep * keep * (x_ref[:, cut] - z + u_ref[:, cut]) + h[:, pl.ds(offset + j, NARROW)]
            stage[0, :, here] = new_z
            stage[1, :, here] = moved - new_z
        cut, here = columns(base, size), pl.ds(filled, size)
        for o in range(2):
            copy = pltpu.make_async_copy(stage.at[o, :, here], outs[o].at[:, cut], sems.at[k, o])
            copy.start()
            copies.append(copy)
        filled += size
    for copy in copies:
        copy.wait()


def final(side, scale, x, u, z, pieces, buffers, blocks_count):
    tasks, width = x.shape
    buffered = buffers is not None
    args = pin(pltpu.VMEM, scale, x, u, z, *(v for piece in pieces for v in piece[3:]))
    vmem = len(args)
    places = [(*piece[:3], piece[5].shape[1]) for piece in pieces]
    out = pltpu.HBM((tasks, width), F32)
    aliases = {}
    if buffered:
        aliases = {1 + vmem + o: o for o in range(2)}
        args += pin(pltpu.HBM, *buffers)
    return call(
        functools.partial(final_kernel, blocks_count, places, buffered),
        "final",
        [SMEM] + [VMEM] * vmem + [HBM] * (2 * buffered),
        (out, out),
        [HBM] * 2,
        [pltpu.VMEM((2, tasks, sum(p[3] for p in places)), F32), pltpu.SemaphoreType.DMA((len(pieces), 2))],
        aliases,
    )(side, *args)


def tie(value, *after):
    return lax.optimization_barrier((value, after))[0]


def per_device(design, labels, local_x, dual_u, consensus_z, step_size, rho, penalty):
    tasks, width = consensus_z.shape
    half = width // 2
    blocks_count = lax.axis_size("rows")
    side = (lax.axis_index("rows") & 1).astype(jnp.int32)[None]

    margin1, pulled, design, x0, dual, z, sign, scale, start_mine, start_other = load(
        side, local_x[0], dual_u[0], consensus_z, design, labels, step_size, rho, penalty, blocks_count
    )
    start_mine = start_mine + exchange(start_other, "rows", 1)

    terms, grams = [margin1], []
    for step in range(max(lax.axis_size("feat").bit_length() - 1, 3)):
        more = (1 << step) < lax.axis_size("feat")
        if step > 0 and more:
            terms = [sum(t.astype(F32) for t in terms).astype(BF16)]
        row = gram_row(GRAM_ORDER[step], tie(side, terms[0]), design) if step < 3 else []
        grams.append(row)
        if more:
            got = exchange(terms[0], "feat", 1 << step)
            terms.append(tie(got, row[0], start_mine) if step == 0 else tie(got, row[0]) if step == 1 else got)

    resid1, margin2 = turn(sign, terms, scale, pulled, [g for row in range(3) for g in grams[GRAM_ORDER.index(row)]])
    terms = square_sum(margin2, "feat")
    mask = 2
    while mask < blocks_count:
        start_mine = start_mine + exchange(start_mine, "rows", mask)
        mask *= 2
    terms = tie(terms, start_mine)
    sizes = [half * part // sum(MINE) for part in MINE]
    begins = [sum(sizes[:c]) for c in range(len(sizes))]
    other_sizes = [half * part // sum(OTHER) for part in OTHER]
    other_begins = [sum(other_sizes[:c]) for c in range(len(other_sizes))]
    count = len(sizes)
    others, received = [], []
    resid = (resid1, sign, *terms)
    for begin, size in zip(other_begins, other_sizes):
        value, other, *made = push(side, resid, scale, design, None, begin, 0, size)
        resid = made[0] if made else resid
        others.append(value)
        received.append(exchange(other, "rows", 1))
    mines, sums, places = [], [], []
    token = tie(side, others[-1])
    for begin, size in zip(begins, sizes):
        source = max(k for k, b in enumerate(other_begins) if b <= begin)
        places.append((source, begin - other_begins[source]))
        value, sent = push(token, resid, scale, design, received[source], begin, places[-1][1], size)
        mines.append(value)
        sums.append(doubling(sent, "rows", 2))
        token = tie(side, sent)
    new_x = store_x(side, scale, x0, dual, z, mines, others)

    start_theirs = exchange(tie(start_mine, mines[0]), "rows", 1)

    pieces, backs, results = [], [], None
    for c, (a, b) in enumerate(sums):
        b = tie(b, new_x, results)
        pieces.append((a.astype(F32) + b.astype(F32)).astype(BF16))
        backs.append(exchange(pieces[c], "rows", 1))
        for group in PLAN[c]:
            work = []
            for mine, k in group:
                source, offset = places[k]
                if mine:
                    work.append((True, begins[k], 0, start_mine, mines[k], pieces[k]))
                else:
                    work.append((False, begins[k], offset, start_theirs, others[source], backs[k]))
            results = final(side, scale, x0, dual, z, work, results, blocks_count)
    new_z, new_u = results
    return (new_x[None], new_z, new_u[None])


def solution(mesh):
    in_specs = (
        P("rows", "feat"),
        P(None, "rows"),
        P("rows", None, "feat"),
        P("rows", None, "feat"),
        P(None, "feat"),
        P(),
        P(),
        P(),
    )
    out_specs = (P("rows", None, "feat"), P(None, "feat"), P("rows", None, "feat"))
    return jax.shard_map(
        per_device, mesh=mesh, in_specs=in_specs, out_specs=out_specs, check_vma=False
    )
```

```python
import functools
import math

import jax
import jax.numpy as jnp
from jax import lax
from jax.experimental import pallas as pl
from jax.experimental.pallas import tpu as pltpu
from jax.sharding import PartitionSpec as P

BF16 = jnp.bfloat16
F32 = jnp.float32
PLAN = ((((True, 0),),), (((False, 0), (True, 1)),), (((False, 1), (True, 2)), ((False, 2),)))
MINE = (3, 3, 2)
OTHER = (3, 5)
STEP = 1024
WIDE = 2048
AHEAD = 8
NARROW = 256
FINISH = 512
WAIT_BYTES = 10_000_000
GRAM_ORDER = (0, 1, 2)
HBM = pl.BlockSpec(memory_space=pltpu.HBM)
VMEM = pl.BlockSpec(memory_space=pltpu.VMEM)
SMEM = pl.BlockSpec(memory_space=pltpu.SMEM)


def exchange(value, axis, mask):
    n = lax.axis_size(axis)
    return lax.ppermute(value, axis, [(i, i ^ mask) for i in range(n)])


def doubling(value, axis, first=1):
    n = lax.axis_size(axis)
    mask = first
    other = exchange(value, axis, mask)
    while 2 * mask < n:
        mask *= 2
        value = (value.astype(F32) + other.astype(F32)).astype(value.dtype)
        other = exchange(value, axis, mask)
    return value, other


def square_sum(value, axis):
    n = lax.axis_size(axis)
    terms = [value]
    mask = 1
    while mask < n:
        if len(terms) > 1:
            terms = [sum(t.astype(F32) for t in terms).astype(value.dtype)]
        steps = [3 * mask, 2 * mask, mask] if 2 * mask < n else [mask]
        terms += [exchange(terms[0], axis, step) for step in steps]
        mask *= 4
    return terms


def nt(a, b):
    return lax.dot_general(a, b, (((1,), (1,)), ((), ())), preferred_element_type=F32)


def call(kernel, name, in_specs, out_shape, out_specs, scratch=(), aliases=None, limit=16, work=1000):
    return pl.pallas_call(
        kernel,
        in_specs=in_specs,
        out_shape=out_shape,
        out_specs=out_specs,
        scratch_shapes=list(scratch),
        input_output_aliases=aliases or {},
        compiler_params=pltpu.CompilerParams(vmem_limit_bytes=limit * 1024 * 1024),
        cost_estimate=pl.CostEstimate(flops=1000, bytes_accessed=work, transcendentals=0),
        name=name,
    )


def pin(space, *values):
    return [pltpu.with_memory_space_constraint(v, space) for v in values]


def columns(start, size):
    return pl.ds(pl.multiple_of(start, 128), size)


def split(whole, high, low):
    top = whole.astype(BF16)
    high[...] = top
    low[...] = (whole - top.astype(F32)).astype(BF16)


def load_kernel(blocks_count, side, x_hbm, u_hbm, z_hbm, a_hbm, sign_hbm, eta_hbm, rho_hbm, lam_hbm, *refs):
    outs, (eta_row, rho_row, lam_row, both, acc, block, sems) = refs[:12], refs[12:]
    m_out, pulled_out, a_out, x_out, u_out, z_out, sign_out, scale, mine_out, other_out, high, low = outs
    tasks, width = x_hbm.shape
    steps = width // STEP
    rows = ((eta_hbm, eta_row), (rho_hbm, rho_row), (lam_hbm, lam_row), (sign_hbm, sign_out))
    small = [pltpu.make_async_copy(a, b, sems.at[4, k]) for k, (a, b) in enumerate(rows)]

    def chunk(j):
        at = columns(j * STEP, STEP)
        pairs = ((x_hbm, x_out), (u_hbm, u_out), (z_hbm, z_out), (a_hbm, a_out))
        return [pltpu.make_async_copy(a.at[:, at], b.at[:, at], sems.at[k, j]) for k, (a, b) in enumerate(pairs)]

    def begin(j):
        for copy in chunk(j):
            copy.start()

    for copy in small[:3]:
        copy.start()
    for j in range(min(AHEAD, steps)):
        begin(j)
    for copy in small[:3]:
        copy.wait()
    one = lax.broadcasted_iota(jnp.int32, (tasks, tasks), 0) == lax.broadcasted_iota(jnp.int32, (tasks, tasks), 1)
    eta, rho, lam = eta_row[...], rho_row[...], lam_row[...]
    for k, row in enumerate((eta, eta * rho, lam / (rho * blocks_count))):
        upright = jnp.where(one, jnp.broadcast_to(row, (tasks, tasks)), 0.0)
        scale[:, k : k + 1] = jnp.sum(upright, axis=1, keepdims=True)
    acc[...] = jnp.zeros_like(acc)
    block[...] = jnp.zeros_like(block)

    @pl.loop(0, steps)
    def _(j):
        for copy in chunk(j):
            copy.wait()

        @pl.when(j + AHEAD < steps)
        def _():
            begin(j + AHEAD)

        @pl.when(j == max(steps - AHEAD, 0))
        def _():
            small[3].start()

        pull = scale[:, 1:2]
        for k in range(0, STEP, NARROW):
            at, here = columns(j * STEP + k, NARROW), pl.ds(k, NARROW)
            x = x_out[:, at]
            v = x - pull * (x - z_out[:, at] + u_out[:, at])
            top = v.astype(BF16)
            both[:tasks, here] = x.astype(BF16)
            both[tasks : 2 * tasks, here] = top
            both[2 * tasks :, here] = (v - top.astype(F32)).astype(BF16)
        at = columns(j * STEP, STEP)
        acc[...] += nt(both[...], a_out[:, at])
        last = a_out[pl.ds(a_out.shape[0] - block.shape[0], block.shape[0]), at]
        block[...] += nt(last, last)

    split(block[...], high, low)
    m_out[...] = acc[:tasks].astype(BF16)
    pulled_out[...] = acc[tasks : 2 * tasks] + acc[2 * tasks :]
    half = width // 2
    mine = columns(side[0] * half, half)
    other = columns((1 - side[0]) * half, half)
    mine_out[...] = x_out[:, mine] + u_out[:, mine]
    other_out[...] = x_out[:, other] + u_out[:, other]
    small[3].wait()


def load(side, x, u, z, design, sign, step_size, rho, penalty, blocks_count):
    tasks, width = x.shape
    samples = design.shape[0]
    full = pltpu.VMEM((tasks, width), F32)
    half = pltpu.VMEM((tasks, width // 2), F32)
    rows = [v.reshape(1, tasks) for v in (step_size, rho, penalty)]
    return call(
        functools.partial(load_kernel, blocks_count),
        "load_and_margins",
        [SMEM] + [HBM] * 8,
        (
            pltpu.VMEM((tasks, samples), BF16), pltpu.VMEM((tasks, samples), F32), pltpu.VMEM(design.shape, BF16),
            full, full, full, pltpu.VMEM(sign.shape, jnp.int32), pltpu.VMEM((tasks, 128), F32), half, half,
            *[pltpu.VMEM((samples // 3, samples // 3), BF16)] * 2,
        ),
        [VMEM] * 12,
        [pltpu.VMEM((1, tasks), F32)] * 3
        + [
            pltpu.VMEM((3 * tasks, STEP), BF16), pltpu.VMEM((3 * tasks, samples), F32),
            pltpu.VMEM((samples // 3, samples // 3), F32),
            pltpu.SemaphoreType.DMA((5, max(width // STEP, 4))),
        ],
    )(side, *pin(pltpu.HBM, x, u, z, design, sign, *rows))


def gram_kernel(row, token, a_ref, high, low, acc):
    size, cols = high.shape
    width = a_ref.shape[1]
    wide = math.gcd(WIDE, width)
    for j in range(width // wide):
        at = pl.ds(j * wide, wide)
        product = nt(a_ref[pl.ds(row * size, size), at], a_ref[pl.ds(0, cols), at])
        acc[...] = product if j == 0 else acc[...] + product
    split(acc[...], high, low)


def gram_row(row, token, design):
    samples = design.shape[0]
    size = samples // 3
    cols = min(row + 1, 2) * size
    out = pltpu.VMEM((size, cols), BF16)
    return call(
        functools.partial(gram_kernel, row),
        "gram",
        [SMEM, VMEM],
        (out, out),
        [VMEM] * 2,
        [pltpu.VMEM((size, cols), F32)],
        work=WAIT_BYTES * (row + 1) // 3,
    )(token, *pin(pltpu.VMEM, design))


def residual(sign, *terms):
    margin = sum(t.astype(F32) for t in terms)
    sign = sign.astype(F32)
    return (sign * jax.nn.sigmoid(-sign * margin)).astype(BF16)


def turn_kernel(sign, scale, pulled, *refs):
    *terms, resid, out = refs[8:]
    grams = refs[:8]
    size = grams[0].shape[0]
    resid[...] = residual(sign[...], *(t[...] for t in terms))
    eta = scale[:, 0:1]
    r = [resid[:, pl.ds(k * size, size)] for k in range(3)]
    for col in range(3):
        total = jnp.zeros((resid.shape[0], size), F32)
        for row in range(3):
            for part in range(2):
                if row == 2 and col == 2:
                    total += jnp.dot(r[row], grams[6 + part][...], preferred_element_type=F32)
                elif row >= col:
                    block = grams[2 * row + part][:, pl.ds(col * size, size)]
                    total += jnp.dot(r[row], block, preferred_element_type=F32)
                else:
                    total += nt(r[row], grams[2 * col + part][:, pl.ds(row * size, size)])
        here = pl.ds(col * size, size)
        out[:, here] = (pulled[:, here] + eta * total).astype(BF16)


def turn(sign, terms, scale, pulled, grams):
    tasks, samples = pulled.shape
    out = pltpu.VMEM((tasks, samples), BF16)
    args = [sign, scale, pulled, *grams, *terms]
    return call(turn_kernel, "turn", [VMEM] * len(args), (out, out), [VMEM] * 2)(*pin(pltpu.VMEM, *args))


def push_kernel(first, mine, begin, offset, size, side, *refs):
    tasks = refs[0].shape[0]
    if first:
        scale, a_ref, resid1, sign, *terms, h_out, sent_out, resid = refs
        resid[:tasks] = resid1[...]
        resid[tasks:] = residual(sign[...], *(t[...] for t in terms))
    else:
        scale, a_ref, resid, *received, h_out, sent_out = refs
    half = a_ref.shape[1] // 2
    eta = scale[:, 0:1]
    keep = 1.0 - scale[:, 1:2]
    base = (side[0] if mine else 1 - side[0]) * half + begin
    step = math.gcd(512, size)
    for j in range(size // step):
        at = columns(base + j * step, step)
        here = pl.ds(j * step, step)
        grads = jnp.dot(resid[...], a_ref[:, at], preferred_element_type=F32)
        push = eta * (keep * grads[:tasks] + grads[tasks:])
        h_out[:, here] = push
        if mine:
            push = push + received[0][:, pl.ds(offset + j * step, step)].astype(F32)
        sent_out[:, here] = push.astype(BF16)


def push(side, resid, scale, design, received, begin, offset, size):
    tasks = scale.shape[0]
    mine = received is not None
    first = isinstance(resid, tuple)
    args = [scale, design, *(resid if first else [resid])] + ([received] if mine else [])
    out = [pltpu.VMEM((tasks, size), F32), pltpu.VMEM((tasks, size), BF16)]
    if first:
        out.append(pltpu.VMEM((2 * tasks, design.shape[0]), BF16))
    return call(
        functools.partial(push_kernel, first, mine, begin, offset, size),
        "push_mine" if mine else "push_other",
        [SMEM] + [VMEM] * len(args),
        tuple(out),
        [VMEM] * len(out),
    )(side, *pin(pltpu.VMEM, *args))


def store_kernel(side, scale, x_ref, u_ref, z_ref, *rest):
    *hs, x_out, stage, sems = rest
    half = x_ref.shape[1] // 2
    keep = 1.0 - scale[:, 1:2]
    copies = []
    done = 0
    for c, h_ref in enumerate(hs):
        size = h_ref.shape[1]
        base = (side[0] if done < half else 1 - side[0]) * half + done % half
        done += size
        for j in range(0, size, NARROW):
            at = columns(base + j, NARROW)
            u, z = u_ref[:, at], z_ref[:, at]
            stage[:, at] = z - u + keep * keep * (x_ref[:, at] - z + u) + h_ref[:, pl.ds(j, NARROW)]
        at = columns(base, size)
        copy = pltpu.make_async_copy(stage.at[:, at], x_out.at[:, at], sems.at[c])
        copy.start()
        copies.append(copy)
    for copy in copies:
        copy.wait()


def store_x(side, scale, x, u, z, mines, others):
    tasks, width = x.shape
    args = [scale, x, u, z, *mines, *others]
    return call(
        store_kernel,
        "store_x",
        [SMEM] + [VMEM] * len(args),
        pltpu.HBM((tasks, width), F32),
        HBM,
        [pltpu.VMEM((tasks, width), F32), pltpu.SemaphoreType.DMA((len(mines) + len(others),))],
    )(side, *pin(pltpu.VMEM, *args))


def final_kernel(blocks_count, pieces, buffered, side, scale, x_ref, u_ref, z_ref, *refs):
    outs = refs[3 * len(pieces) + 2 * buffered :][:2]
    stage, sems = refs[-2:]
    half = x_ref.shape[1] // 2
    pull, limit = scale[:, 1:2], scale[:, 2:3]
    keep = 1.0 - pull
    copies, filled = [], 0
    for k, (mine, begin, offset, size) in enumerate(pieces):
        start, h, pushed = refs[3 * k : 3 * k + 3]
        base = (side[0] if mine else 1 - side[0]) * half + begin
        for j in range(0, size, NARROW):
            cut, here = columns(base + j, NARROW), pl.ds(filled + j, NARROW)
            z = z_ref[:, cut]
            total = keep * keep * start[:, pl.ds(begin + j, NARROW)] + pushed[:, pl.ds(j, NARROW)].astype(F32)
            mean = total * (1.0 / blocks_count) + pull * (1.0 + keep) * z
            new_z = mean - jnp.clip(mean, -limit, limit)
            moved = z + keep * keep * (x_ref[:, cut] - z + u_ref[:, cut]) + h[:, pl.ds(offset + j, NARROW)]
            stage[0, :, here] = new_z
            stage[1, :, here] = moved - new_z
            if (j + NARROW) % FINISH == 0 or j + NARROW == size:
                long = j % FINISH + NARROW
                cut, here = columns(base + j + NARROW - long, long), pl.ds(filled + j + NARROW - long, long)
                for o in range(2):
                    copy = pltpu.make_async_copy(stage.at[o, :, here], outs[o].at[:, cut], sems.at[len(copies) // 2, o])
                    copy.start()
                    copies.append(copy)
        filled += size
    for copy in copies:
        copy.wait()


def final(side, scale, x, u, z, pieces, buffers, blocks_count):
    tasks, width = x.shape
    buffered = buffers is not None
    args = pin(pltpu.VMEM, scale, x, u, z, *(v for piece in pieces for v in piece[3:]))
    vmem = len(args)
    places = [(*piece[:3], piece[5].shape[1]) for piece in pieces]
    out = pltpu.HBM((tasks, width), F32)
    aliases = {}
    if buffered:
        aliases = {1 + vmem + o: o for o in range(2)}
        args += pin(pltpu.HBM, *buffers)
    return call(
        functools.partial(final_kernel, blocks_count, places, buffered),
        "final",
        [SMEM] + [VMEM] * vmem + [HBM] * (2 * buffered),
        (out, out),
        [HBM] * 2,
        [pltpu.VMEM((2, tasks, sum(p[3] for p in places)), F32), pltpu.SemaphoreType.DMA((sum(-(-p[3] // FINISH) for p in places), 2))],
        aliases,
    )(side, *args)


def tie(value, *after):
    return lax.optimization_barrier((value, after))[0]


def per_device(design, labels, local_x, dual_u, consensus_z, step_size, rho, penalty):
    tasks, width = consensus_z.shape
    half = width // 2
    blocks_count = lax.axis_size("rows")
    side = (lax.axis_index("rows") & 1).astype(jnp.int32)[None]

    margin1, pulled, design, x0, dual, z, sign, scale, start_mine, start_other, *block = load(
        side, local_x[0], dual_u[0], consensus_z, design, labels, step_size, rho, penalty, blocks_count
    )
    start_mine = start_mine + exchange(start_other, "rows", 1)

    terms, grams = [margin1], []
    for step in range(max(lax.axis_size("feat").bit_length() - 1, 3)):
        more = (1 << step) < lax.axis_size("feat")
        if step > 0 and more:
            terms = [sum(t.astype(F32) for t in terms).astype(BF16)]
        row = gram_row(GRAM_ORDER[step], tie(side, terms[0]), design) if step < 3 else []
        grams.append(row)
        if more:
            got = exchange(terms[0], "feat", 1 << step)
            terms.append(tie(got, row[0], start_mine) if step == 0 else tie(got, row[0]) if step == 1 else got)

    resid1, margin2 = turn(sign, terms, scale, pulled, [g for row in range(3) for g in grams[GRAM_ORDER.index(row)]] + block)
    terms = square_sum(margin2, "feat")
    mask = 2
    while mask < blocks_count:
        start_mine = start_mine + exchange(start_mine, "rows", mask)
        mask *= 2
    terms = tie(terms, start_mine)
    sizes = [half * part // sum(MINE) for part in MINE]
    begins = [sum(sizes[:c]) for c in range(len(sizes))]
    other_sizes = [half * part // sum(OTHER) for part in OTHER]
    other_begins = [sum(other_sizes[:c]) for c in range(len(other_sizes))]
    count = len(sizes)
    others, received = [], []
    resid = (resid1, sign, *terms)
    for begin, size in zip(other_begins, other_sizes):
        value, other, *made = push(side, resid, scale, design, None, begin, 0, size)
        resid = made[0] if made else resid
        others.append(value)
        received.append(exchange(other, "rows", 1))
    mines, sums, places = [], [], []
    token = tie(side, others[-1])
    for begin, size in zip(begins, sizes):
        source = max(k for k, b in enumerate(other_begins) if b <= begin)
        places.append((source, begin - other_begins[source]))
        value, sent = push(token, resid, scale, design, received[source], begin, places[-1][1], size)
        mines.append(value)
        sums.append(doubling(sent, "rows", 2))
        token = tie(side, sent)
    new_x = store_x(side, scale, x0, dual, z, mines, others)

    start_theirs = exchange(tie(start_mine, mines[0]), "rows", 1)

    pieces, backs, results = [], [], None
    for c, (a, b) in enumerate(sums):
        b = tie(b, new_x, results)
        pieces.append((a.astype(F32) + b.astype(F32)).astype(BF16))
        backs.append(exchange(pieces[c], "rows", 1))
        for group in PLAN[c]:
            work = []
            for mine, k in group:
                source, offset = places[k]
                if mine:
                    work.append((True, begins[k], 0, start_mine, mines[k], pieces[k]))
                else:
                    work.append((False, begins[k], offset, start_theirs, others[source], backs[k]))
            results = final(side, scale, x0, dual, z, work, results, blocks_count)
    new_z, new_u = results
    return (new_x[None], new_z, new_u[None])


def solution(mesh):
    in_specs = (
        P("rows", "feat"),
        P(None, "rows"),
        P("rows", None, "feat"),
        P("rows", None, "feat"),
        P(None, "feat"),
        P(),
        P(),
        P(),
    )
    out_specs = (P("rows", None, "feat"), P(None, "feat"), P("rows", None, "feat"))
    return jax.shard_map(
        per_device, mesh=mesh, in_specs=in_specs, out_specs=out_specs, check_vma=False
    )
```

```python
import functools
import math

import jax
import jax.numpy as jnp
from jax import lax
from jax.experimental import pallas as pl
from jax.experimental.pallas import tpu as pltpu
from jax.sharding import PartitionSpec as P

BF16 = jnp.bfloat16
F32 = jnp.float32
PLAN = ((((True, 0),),), (((False, 0), (True, 1)),), (((False, 1), (True, 2)), ((False, 2),)))
MINE = (3, 3, 2)
OTHER = (3, 5)
STEP = 1024
WIDE = 2048
NARROW = 256
WAIT_BYTES = 10_000_000
GRAM_ORDER = (0, 1, 2)
HBM = pl.BlockSpec(memory_space=pltpu.HBM)
VMEM = pl.BlockSpec(memory_space=pltpu.VMEM)
SMEM = pl.BlockSpec(memory_space=pltpu.SMEM)


def exchange(value, axis, mask):
    n = lax.axis_size(axis)
    return lax.ppermute(value, axis, [(i, i ^ mask) for i in range(n)])


def doubling(value, axis, first=1):
    n = lax.axis_size(axis)
    mask = first
    other = exchange(value, axis, mask)
    while 2 * mask < n:
        mask *= 2
        value = (value.astype(F32) + other.astype(F32)).astype(value.dtype)
        other = exchange(value, axis, mask)
    return value, other


def square_sum(value, axis):
    n = lax.axis_size(axis)
    terms = [value]
    mask = 1
    while mask < n:
        if len(terms) > 1:
            terms = [sum(t.astype(F32) for t in terms).astype(value.dtype)]
        steps = [mask, 2 * mask, 3 * mask] if 2 * mask < n else [mask]
        terms += [exchange(terms[0], axis, step) for step in steps]
        mask *= 4
    return terms


def nt(a, b):
    return lax.dot_general(a, b, (((1,), (1,)), ((), ())), preferred_element_type=F32)


def call(kernel, name, in_specs, out_shape, out_specs, scratch=(), aliases=None, limit=16, work=1000):
    return pl.pallas_call(
        kernel,
        in_specs=in_specs,
        out_shape=out_shape,
        out_specs=out_specs,
        scratch_shapes=list(scratch),
        input_output_aliases=aliases or {},
        compiler_params=pltpu.CompilerParams(vmem_limit_bytes=limit * 1024 * 1024),
        cost_estimate=pl.CostEstimate(flops=1000, bytes_accessed=work, transcendentals=0),
        name=name,
    )


def pin(space, *values):
    return [pltpu.with_memory_space_constraint(v, space) for v in values]


def columns(start, size):
    return pl.ds(pl.multiple_of(start, 128), size)


def load_kernel(blocks_count, side, x_hbm, u_hbm, z_hbm, a_hbm, sign_hbm, eta_hbm, rho_hbm, lam_hbm, *refs):
    outs, (eta_row, rho_row, lam_row, *boths, acc, sems) = refs[:10], refs[10:]
    m_out, pulled_out, a_out, x_out, u_out, z_out, sign_out, scale, mine_out, other_out = outs
    tasks, width = x_hbm.shape
    steps = width // STEP
    rows = ((eta_hbm, eta_row), (rho_hbm, rho_row), (lam_hbm, lam_row), (sign_hbm, sign_out))
    small = [pltpu.make_async_copy(a, b, sems.at[4, k]) for k, (a, b) in enumerate(rows)]

    def vectors(j):
        at = pl.ds(j * STEP, STEP)
        pairs = ((x_hbm, x_out), (u_hbm, u_out), (z_hbm, z_out))
        return [pltpu.make_async_copy(a.at[:, at], b.at[:, at], sems.at[k, j]) for k, (a, b) in enumerate(pairs)]

    def matrix(j):
        at = pl.ds(j * STEP, STEP)
        return pltpu.make_async_copy(a_hbm.at[:, at], a_out.at[:, at], sems.at[3, j])

    for copy in small[:3] + vectors(0):
        copy.start()
    for j in range(steps):
        if j + 1 < steps:
            for copy in vectors(j + 1):
                copy.start()
        matrix(j).start()
    small[3].start()
    for copy in small[:3]:
        copy.wait()
    one = lax.broadcasted_iota(jnp.int32, (tasks, tasks), 0) == lax.broadcasted_iota(jnp.int32, (tasks, tasks), 1)
    eta, rho, lam = eta_row[...], rho_row[...], lam_row[...]
    for k, row in enumerate((eta, eta * rho, lam / (rho * blocks_count))):
        upright = jnp.where(one, jnp.broadcast_to(row, (tasks, tasks)), 0.0)
        scale[:, k : k + 1] = jnp.sum(upright, axis=1, keepdims=True)
    pull = scale[:, 1:2]

    def prepare(j, both):
        for k in range(0, STEP, NARROW):
            at, here = pl.ds(j * STEP + k, NARROW), pl.ds(k, NARROW)
            x = x_out[:, at]
            v = x - pull * (x - z_out[:, at] + u_out[:, at])
            both[:tasks, here] = x.astype(BF16)
            both[tasks:, here] = v.astype(BF16)

    for copy in vectors(0):
        copy.wait()
    prepare(0, boths[0])
    for j in range(steps):
        matrix(j).wait()
        if j + 1 < steps:
            for copy in vectors(j + 1):
                copy.wait()
            prepare(j + 1, boths[(j + 1) % 2])
        product = nt(boths[j % 2][...], a_out[:, pl.ds(j * STEP, STEP)])
        acc[...] = product if j == 0 else acc[...] + product

    m_out[...] = acc[:tasks].astype(BF16)
    pulled_out[...] = acc[tasks:]
    half = width // 2
    mine = columns(side[0] * half, half)
    other = columns((1 - side[0]) * half, half)
    mine_out[...] = x_out[:, mine] + u_out[:, mine]
    other_out[...] = x_out[:, other] + u_out[:, other]
    small[3].wait()


def load(side, x, u, z, design, sign, step_size, rho, penalty, blocks_count):
    tasks, width = x.shape
    samples = design.shape[0]
    full = pltpu.VMEM((tasks, width), F32)
    half = pltpu.VMEM((tasks, width // 2), F32)
    rows = [v.reshape(1, tasks) for v in (step_size, rho, penalty)]
    return call(
        functools.partial(load_kernel, blocks_count),
        "load_and_margins",
        [SMEM] + [HBM] * 8,
        (
            pltpu.VMEM((tasks, samples), BF16), pltpu.VMEM((tasks, samples), F32), pltpu.VMEM(design.shape, BF16),
            full, full, full, pltpu.VMEM(sign.shape, jnp.int32), pltpu.VMEM((tasks, 128), F32), half, half,
        ),
        [VMEM] * 10,
        [pltpu.VMEM((1, tasks), F32)] * 3
        + [
            *[pltpu.VMEM((2 * tasks, STEP), BF16)] * 2, pltpu.VMEM((2 * tasks, samples), F32),
            pltpu.SemaphoreType.DMA((5, max(width // STEP, 4))),
        ],
    )(side, *pin(pltpu.HBM, x, u, z, design, sign, *rows))


def gram_block(a_ref, row, cols, size, acc, high, low):
    width = a_ref.shape[1]
    wide = math.gcd(WIDE, width)
    for j in range(width // wide):
        at = pl.ds(j * wide, wide)
        product = nt(a_ref[pl.ds(row, size), at], a_ref[pl.ds(0, cols), at])
        acc[:, :cols] = product if j == 0 else acc[:, :cols] + product
    whole = acc[:, :cols]
    top = whole.astype(BF16)
    high[...] = top
    low[...] = (whole - top.astype(F32)).astype(BF16)


def gram_kernel(row, token, a_ref, high, low, acc):
    size = high.shape[0]
    gram_block(a_ref, row * size, (row + 1) * size, size, acc, high, low)


def gram_row(row, token, design):
    samples = design.shape[0]
    size = samples // 3
    out = pltpu.VMEM((size, (row + 1) * size), BF16)
    return call(
        functools.partial(gram_kernel, row),
        "gram",
        [SMEM, VMEM],
        (out, out),
        [VMEM] * 2,
        [pltpu.VMEM((size, (row + 1) * size), F32)],
        work=WAIT_BYTES * (row + 1) // 3,
    )(token, *pin(pltpu.VMEM, design))


def residual(sign, *terms):
    margin = sum(t.astype(F32) for t in terms)
    sign = sign.astype(F32)
    return (sign * jax.nn.sigmoid(-sign * margin)).astype(BF16)


def turn_kernel(sign, scale, pulled, *refs):
    *terms, resid, out = refs[6:]
    grams = refs[:6]
    size = grams[0].shape[0]
    resid[...] = residual(sign[...], *(t[...] for t in terms))
    eta = scale[:, 0:1]
    r = [resid[:, pl.ds(k * size, size)] for k in range(3)]
    for col in range(3):
        total = jnp.zeros((resid.shape[0], size), F32)
        for row in range(3):
            for part in range(2):
                if row >= col:
                    block = grams[2 * row + part][:, pl.ds(col * size, size)]
                    total += jnp.dot(r[row], block, preferred_element_type=F32)
                else:
                    total += nt(r[row], grams[2 * col + part][:, pl.ds(row * size, size)])
        here = pl.ds(col * size, size)
        out[:, here] = (pulled[:, here] + eta * total).astype(BF16)


def turn(sign, terms, scale, pulled, grams):
    tasks, samples = pulled.shape
    out = pltpu.VMEM((tasks, samples), BF16)
    args = [sign, scale, pulled, *grams, *terms]
    return call(turn_kernel, "turn", [VMEM] * len(args), (out, out), [VMEM] * 2)(*pin(pltpu.VMEM, *args))


def push_kernel(first, mine, begin, offset, size, side, *refs):
    tasks = refs[0].shape[0]
    if first:
        scale, a_ref, resid1, sign, *terms, h_out, sent_out, resid = refs
        resid[:tasks] = resid1[...]
        resid[tasks:] = residual(sign[...], *(t[...] for t in terms))
    else:
        scale, a_ref, resid, *received, h_out, sent_out = refs
    half = a_ref.shape[1] // 2
    eta = scale[:, 0:1]
    keep = 1.0 - scale[:, 1:2]
    base = (side[0] if mine else 1 - side[0]) * half + begin
    step = math.gcd(512, size)
    for j in range(size // step):
        at = columns(base + j * step, step)
        here = pl.ds(j * step, step)
        grads = jnp.dot(resid[...], a_ref[:, at], preferred_element_type=F32)
        push = eta * (keep * grads[:tasks] + grads[tasks:])
        h_out[:, here] = push
        if mine:
            push = push + received[0][:, pl.ds(offset + j * step, step)].astype(F32)
        sent_out[:, here] = push.astype(BF16)


def push(side, resid, scale, design, received, begin, offset, size):
    tasks = scale.shape[0]
    mine = received is not None
    first = isinstance(resid, tuple)
    args = [scale, design, *(resid if first else [resid])] + ([received] if mine else [])
    out = [pltpu.VMEM((tasks, size), F32), pltpu.VMEM((tasks, size), BF16)]
    if first:
        out.append(pltpu.VMEM((2 * tasks, design.shape[0]), BF16))
    return call(
        functools.partial(push_kernel, first, mine, begin, offset, size),
        "push_mine" if mine else "push_other",
        [SMEM] + [VMEM] * len(args),
        tuple(out),
        [VMEM] * len(out),
    )(side, *pin(pltpu.VMEM, *args))


def store_kernel(side, scale, x_ref, u_ref, z_ref, *rest):
    *hs, x_out, stage, sems = rest
    half = x_ref.shape[1] // 2
    keep = 1.0 - scale[:, 1:2]
    copies = []
    done = 0
    for c, h_ref in enumerate(hs):
        size = h_ref.shape[1]
        base = (side[0] if done < half else 1 - side[0]) * half + done % half
        done += size
        for j in range(0, size, NARROW):
            at = columns(base + j, NARROW)
            u, z = u_ref[:, at], z_ref[:, at]
            stage[:, at] = z - u + keep * keep * (x_ref[:, at] - z + u) + h_ref[:, pl.ds(j, NARROW)]
        at = columns(base, size)
        copy = pltpu.make_async_copy(stage.at[:, at], x_out.at[:, at], sems.at[c])
        copy.start()
        copies.append(copy)
    for copy in copies:
        copy.wait()


def store_x(side, scale, x, u, z, mines, others):
    tasks, width = x.shape
    args = [scale, x, u, z, *mines, *others]
    return call(
        store_kernel,
        "store_x",
        [SMEM] + [VMEM] * len(args),
        pltpu.HBM((tasks, width), F32),
        HBM,
        [pltpu.VMEM((tasks, width), F32), pltpu.SemaphoreType.DMA((len(mines) + len(others),))],
    )(side, *pin(pltpu.VMEM, *args))


def final_kernel(blocks_count, pieces, buffered, side, scale, x_ref, u_ref, z_ref, *refs):
    outs = refs[3 * len(pieces) + 2 * buffered :][:2]
    stage, sems = refs[-2:]
    half = x_ref.shape[1] // 2
    pull, limit = scale[:, 1:2], scale[:, 2:3]
    keep = 1.0 - pull
    copies, filled = [], 0
    for k, (mine, begin, offset, size) in enumerate(pieces):
        start, h, pushed = refs[3 * k : 3 * k + 3]
        base = (side[0] if mine else 1 - side[0]) * half + begin
        for j in range(0, size, NARROW):
            cut, here = columns(base + j, NARROW), pl.ds(filled + j, NARROW)
            z = z_ref[:, cut]
            total = keep * keep * start[:, pl.ds(begin + j, NARROW)] + pushed[:, pl.ds(j, NARROW)].astype(F32)
            mean = total * (1.0 / blocks_count) + pull * (1.0 + keep) * z
            new_z = mean - jnp.clip(mean, -limit, limit)
            moved = z + keep * keep * (x_ref[:, cut] - z + u_ref[:, cut]) + h[:, pl.ds(offset + j, NARROW)]
            stage[0, :, here] = new_z
            stage[1, :, here] = moved - new_z
        cut, here = columns(base, size), pl.ds(filled, size)
        for o in range(2):
            copy = pltpu.make_async_copy(stage.at[o, :, here], outs[o].at[:, cut], sems.at[k, o])
            copy.start()
            copies.append(copy)
        filled += size
    for copy in copies:
        copy.wait()


def final(side, scale, x, u, z, pieces, buffers, blocks_count):
    tasks, width = x.shape
    buffered = buffers is not None
    args = pin(pltpu.VMEM, scale, x, u, z, *(v for piece in pieces for v in piece[3:]))
    vmem = len(args)
    places = [(*piece[:3], piece[5].shape[1]) for piece in pieces]
    out = pltpu.HBM((tasks, width), F32)
    aliases = {}
    if buffered:
        aliases = {1 + vmem + o: o for o in range(2)}
        args += pin(pltpu.HBM, *buffers)
    return call(
        functools.partial(final_kernel, blocks_count, places, buffered),
        "final",
        [SMEM] + [VMEM] * vmem + [HBM] * (2 * buffered),
        (out, out),
        [HBM] * 2,
        [pltpu.VMEM((2, tasks, sum(p[3] for p in places)), F32), pltpu.SemaphoreType.DMA((len(pieces), 2))],
        aliases,
    )(side, *args)


def tie(value, *after):
    return lax.optimization_barrier((value, after))[0]


def per_device(design, labels, local_x, dual_u, consensus_z, step_size, rho, penalty):
    tasks, width = consensus_z.shape
    half = width // 2
    blocks_count = lax.axis_size("rows")
    side = (lax.axis_index("rows") & 1).astype(jnp.int32)[None]

    margin1, pulled, design, x0, dual, z, sign, scale, start_mine, start_other = load(
        side, local_x[0], dual_u[0], consensus_z, design, labels, step_size, rho, penalty, blocks_count
    )
    start_mine = start_mine + exchange(start_other, "rows", 1)

    terms, grams = [margin1], []
    for step in range(max(lax.axis_size("feat").bit_length() - 1, 3)):
        more = (1 << step) < lax.axis_size("feat")
        if step > 0 and more:
            terms = [sum(t.astype(F32) for t in terms).astype(BF16)]
        row = gram_row(GRAM_ORDER[step], tie(side, terms[0]), design) if step < 3 else []
        grams.append(row)
        if more:
            got = exchange(terms[0], "feat", 1 << step)
            terms.append(tie(got, row[0], start_mine) if step == 0 else tie(got, row[0]) if step == 1 else got)

    resid1, margin2 = turn(sign, terms, scale, pulled, [g for row in range(3) for g in grams[GRAM_ORDER.index(row)]])
    terms = square_sum(margin2, "feat")
    mask = 2
    while mask < blocks_count:
        start_mine = start_mine + exchange(start_mine, "rows", mask)
        mask *= 2
    terms = tie(terms, start_mine)
    sizes = [half * part // sum(MINE) for part in MINE]
    begins = [sum(sizes[:c]) for c in range(len(sizes))]
    other_sizes = [half * part // sum(OTHER) for part in OTHER]
    other_begins = [sum(other_sizes[:c]) for c in range(len(other_sizes))]
    count = len(sizes)
    others, received = [], []
    resid = (resid1, sign, *terms)
    for begin, size in zip(other_begins, other_sizes):
        value, other, *made = push(side, resid, scale, design, None, begin, 0, size)
        resid = made[0] if made else resid
        others.append(value)
        received.append(exchange(other, "rows", 1))
    mines, sums, places = [], [], []
    token = tie(side, others[-1])
    for begin, size in zip(begins, sizes):
        source = max(k for k, b in enumerate(other_begins) if b <= begin)
        places.append((source, begin - other_begins[source]))
        value, sent = push(token, resid, scale, design, received[source], begin, places[-1][1], size)
        mines.append(value)
        sums.append(doubling(sent, "rows", 2))
        token = tie(side, sent)
    new_x = store_x(side, scale, x0, dual, z, mines, others)

    start_theirs = exchange(tie(start_mine, mines[0]), "rows", 1)

    pieces, backs, results = [], [], None
    for c, (a, b) in enumerate(sums):
        b = tie(b, new_x, results)
        pieces.append((a.astype(F32) + b.astype(F32)).astype(BF16))
        backs.append(exchange(pieces[c], "rows", 1))
        for group in PLAN[c]:
            work = []
            for mine, k in group:
                source, offset = places[k]
                if mine:
                    work.append((True, begins[k], 0, start_mine, mines[k], pieces[k]))
                else:
                    work.append((False, begins[k], offset, start_theirs, others[source], backs[k]))
            results = final(side, scale, x0, dual, z, work, results, blocks_count)
    new_z, new_u = results
    return (new_x[None], new_z, new_u[None])


def solution(mesh):
    in_specs = (
        P("rows", "feat"),
        P(None, "rows"),
        P("rows", None, "feat"),
        P("rows", None, "feat"),
        P(None, "feat"),
        P(),
        P(),
        P(),
    )
    out_specs = (P("rows", None, "feat"), P(None, "feat"), P("rows", None, "feat"))
    return jax.shard_map(
        per_device, mesh=mesh, in_specs=in_specs, out_specs=out_specs, check_vma=False
    )
```

```python
import functools
import math

import jax
import jax.numpy as jnp
from jax import lax
from jax.experimental import pallas as pl
from jax.experimental.pallas import tpu as pltpu
from jax.sharding import PartitionSpec as P

BF16 = jnp.bfloat16
F32 = jnp.float32
PLAN = ((((True, 0),),), (((False, 0), (True, 1)),), (((False, 1), (True, 2)), ((False, 2),)))
MINE = (3, 3, 2)
OTHER = (3, 5)
STEP = 1024
WIDE = 2048
AHEAD = 8
NARROW = 256
WAIT_BYTES = 10_000_000
HBM = pl.BlockSpec(memory_space=pltpu.HBM)
VMEM = pl.BlockSpec(memory_space=pltpu.VMEM)
SMEM = pl.BlockSpec(memory_space=pltpu.SMEM)


def exchange(value, axis, mask):
    n = lax.axis_size(axis)
    return lax.ppermute(value, axis, [(i, i ^ mask) for i in range(n)])


def doubling(value, axis, first=1):
    n = lax.axis_size(axis)
    mask = first
    other = exchange(value, axis, mask)
    while 2 * mask < n:
        mask *= 2
        value = (value.astype(F32) + other.astype(F32)).astype(value.dtype)
        other = exchange(value, axis, mask)
    return value, other


def square_sum(value, axis):
    n = lax.axis_size(axis)
    terms = [value]
    mask = 1
    while mask < n:
        if len(terms) > 1:
            terms = [sum(t.astype(F32) for t in terms).astype(value.dtype)]
        steps = [mask, 2 * mask, 3 * mask] if 2 * mask < n else [mask]
        terms += [exchange(terms[0], axis, step) for step in steps]
        mask *= 4
    return terms


def nt(a, b):
    return lax.dot_general(a, b, (((1,), (1,)), ((), ())), preferred_element_type=F32)


def call(kernel, name, in_specs, out_shape, out_specs, scratch=(), aliases=None, limit=16, work=1000):
    return pl.pallas_call(
        kernel,
        in_specs=in_specs,
        out_shape=out_shape,
        out_specs=out_specs,
        scratch_shapes=list(scratch),
        input_output_aliases=aliases or {},
        compiler_params=pltpu.CompilerParams(vmem_limit_bytes=limit * 1024 * 1024),
        cost_estimate=pl.CostEstimate(flops=1000, bytes_accessed=work, transcendentals=0),
        name=name,
    )


def pin(space, *values):
    return [pltpu.with_memory_space_constraint(v, space) for v in values]


def columns(start, size):
    return pl.ds(pl.multiple_of(start, 128), size)


def load_kernel(blocks_count, side, x_hbm, u_hbm, z_hbm, a_hbm, sign_hbm, eta_hbm, rho_hbm, lam_hbm, *refs):
    outs, (eta_row, rho_row, lam_row, both, acc, sems) = refs[:10], refs[10:]
    m_out, pulled_out, a_out, x_out, u_out, z_out, sign_out, scale, mine_out, other_out = outs
    tasks, width = x_hbm.shape
    steps = width // STEP
    rows = ((eta_hbm, eta_row), (rho_hbm, rho_row), (lam_hbm, lam_row), (sign_hbm, sign_out))
    small = [pltpu.make_async_copy(a, b, sems.at[4, k]) for k, (a, b) in enumerate(rows)]

    def chunk(j):
        at = columns(j * STEP, STEP)
        pairs = ((x_hbm, x_out), (u_hbm, u_out), (z_hbm, z_out), (a_hbm, a_out))
        return [pltpu.make_async_copy(a.at[:, at], b.at[:, at], sems.at[k, j]) for k, (a, b) in enumerate(pairs)]

    def begin(j):
        for copy in chunk(j):
            copy.start()

    for copy in small[:3]:
        copy.start()
    for j in range(min(AHEAD, steps)):
        begin(j)
    for copy in small[:3]:
        copy.wait()
    one = lax.broadcasted_iota(jnp.int32, (tasks, tasks), 0) == lax.broadcasted_iota(jnp.int32, (tasks, tasks), 1)
    eta, rho, lam = eta_row[...], rho_row[...], lam_row[...]
    for k, row in enumerate((eta, eta * rho, lam / (rho * blocks_count))):
        upright = jnp.where(one, jnp.broadcast_to(row, (tasks, tasks)), 0.0)
        scale[:, k : k + 1] = jnp.sum(upright, axis=1, keepdims=True)
    acc[...] = jnp.zeros_like(acc)

    @pl.loop(0, steps)
    def _(j):
        for copy in chunk(j):
            copy.wait()

        @pl.when(j + AHEAD < steps)
        def _():
            begin(j + AHEAD)

        @pl.when(j == max(steps - AHEAD, 0))
        def _():
            small[3].start()

        pull = scale[:, 1:2]
        for k in range(0, STEP, NARROW):
            at, here = columns(j * STEP + k, NARROW), pl.ds(k, NARROW)
            x = x_out[:, at]
            v = x - pull * (x - z_out[:, at] + u_out[:, at])
            both[:tasks, here] = x.astype(BF16)
            both[tasks:, here] = v.astype(BF16)
        acc[...] += nt(both[...], a_out[:, columns(j * STEP, STEP)])

    m_out[...] = acc[:tasks].astype(BF16)
    pulled_out[...] = acc[tasks:]
    half = width // 2
    mine = columns(side[0] * half, half)
    other = columns((1 - side[0]) * half, half)
    mine_out[...] = x_out[:, mine] + u_out[:, mine]
    other_out[...] = x_out[:, other] + u_out[:, other]
    small[3].wait()


def load(side, x, u, z, design, sign, step_size, rho, penalty, blocks_count):
    tasks, width = x.shape
    samples = design.shape[0]
    full = pltpu.VMEM((tasks, width), F32)
    half = pltpu.VMEM((tasks, width // 2), F32)
    rows = [v.reshape(1, tasks) for v in (step_size, rho, penalty)]
    return call(
        functools.partial(load_kernel, blocks_count),
        "load_and_margins",
        [SMEM] + [HBM] * 8,
        (
            pltpu.VMEM((tasks, samples), BF16), pltpu.VMEM((tasks, samples), F32), pltpu.VMEM(design.shape, BF16),
            full, full, full, pltpu.VMEM(sign.shape, jnp.int32), pltpu.VMEM((tasks, 128), F32), half, half,
        ),
        [VMEM] * 10,
        [pltpu.VMEM((1, tasks), F32)] * 3
        + [
            pltpu.VMEM((2 * tasks, STEP), BF16), pltpu.VMEM((2 * tasks, samples), F32),
            pltpu.SemaphoreType.DMA((5, max(width // STEP, 4))),
        ],
    )(side, *pin(pltpu.HBM, x, u, z, design, sign, *rows))


GRAM_STEPS = (((0, 0),), ((1, 0), (1, 1), (2, 2)), ((2, 0), (2, 1)))


def gram_kernel(blocks, token, a_ref, *refs):
    *outs, acc = refs
    size = outs[0].shape[0]
    width = a_ref.shape[1]
    wide = math.gcd(WIDE, width)
    rows = sorted({row for row, _ in blocks})
    done = 0
    for row in rows:
        cols = [col for r, col in blocks if r == row]
        span = pl.ds(cols[0] * size, len(cols) * size)
        here = pl.ds(0, len(cols) * size)
        for j in range(width // wide):
            at = pl.ds(j * wide, wide)
            product = nt(a_ref[pl.ds(row * size, size), at], a_ref[span, at])
            acc[:, here] = product if j == 0 else acc[:, here] + product
        for k in range(len(cols)):
            whole = acc[:, pl.ds(k * size, size)]
            top = whole.astype(BF16)
            outs[2 * done][...] = top
            outs[2 * done + 1][...] = (whole - top.astype(F32)).astype(BF16)
            done += 1


def gram_blocks(step, token, design):
    samples = design.shape[0]
    size = samples // 3
    blocks = GRAM_STEPS[step]
    out = pltpu.VMEM((size, size), BF16)
    parts = call(
        functools.partial(gram_kernel, blocks),
        "gram",
        [SMEM, VMEM],
        (out,) * (2 * len(blocks)),
        [VMEM] * (2 * len(blocks)),
        [pltpu.VMEM((size, 2 * size), F32)],
        work=WAIT_BYTES * (step + 1) // 3,
    )(token, *pin(pltpu.VMEM, design))
    return {block: parts[2 * k : 2 * k + 2] for k, block in enumerate(blocks)}


def residual(sign, *terms):
    margin = sum(t.astype(F32) for t in terms)
    sign = sign.astype(F32)
    return (sign * jax.nn.sigmoid(-sign * margin)).astype(BF16)


LOWER = [(row, col) for row in range(3) for col in range(row + 1)]


def turn_kernel(sign, scale, pulled, *refs):
    *terms, resid, out = refs[12:]
    grams = {block: refs[2 * k : 2 * k + 2] for k, block in enumerate(LOWER)}
    size = refs[0].shape[0]
    resid[...] = residual(sign[...], *(t[...] for t in terms))
    eta = scale[:, 0:1]
    r = [resid[:, pl.ds(k * size, size)] for k in range(3)]
    for col in range(3):
        total = jnp.zeros((resid.shape[0], size), F32)
        for row in range(3):
            for part in range(2):
                if row >= col:
                    total += jnp.dot(r[row], grams[row, col][part][...], preferred_element_type=F32)
                else:
                    total += nt(r[row], grams[col, row][part][...])
        here = pl.ds(col * size, size)
        out[:, here] = (pulled[:, here] + eta * total).astype(BF16)


def turn(sign, terms, scale, pulled, grams):
    tasks, samples = pulled.shape
    out = pltpu.VMEM((tasks, samples), BF16)
    args = [sign, scale, pulled, *(part for block in LOWER for part in grams[block]), *terms]
    return call(turn_kernel, "turn", [VMEM] * len(args), (out, out), [VMEM] * 2)(*pin(pltpu.VMEM, *args))


def push_kernel(first, mine, begin, offset, size, side, *refs):
    tasks = refs[0].shape[0]
    if first:
        scale, a_ref, resid1, sign, *terms, h_out, sent_out, resid = refs
        resid[:tasks] = resid1[...]
        resid[tasks:] = residual(sign[...], *(t[...] for t in terms))
    else:
        scale, a_ref, resid, *received, h_out, sent_out = refs
    half = a_ref.shape[1] // 2
    eta = scale[:, 0:1]
    keep = 1.0 - scale[:, 1:2]
    base = (side[0] if mine else 1 - side[0]) * half + begin
    step = math.gcd(512, size)
    for j in range(size // step):
        at = columns(base + j * step, step)
        here = pl.ds(j * step, step)
        grads = jnp.dot(resid[...], a_ref[:, at], preferred_element_type=F32)
        push = eta * (keep * grads[:tasks] + grads[tasks:])
        h_out[:, here] = push
        if mine:
            push = push + received[0][:, pl.ds(offset + j * step, step)].astype(F32)
        sent_out[:, here] = push.astype(BF16)


def push(side, resid, scale, design, received, begin, offset, size):
    tasks = scale.shape[0]
    mine = received is not None
    first = isinstance(resid, tuple)
    args = [scale, design, *(resid if first else [resid])] + ([received] if mine else [])
    out = [pltpu.VMEM((tasks, size), F32), pltpu.VMEM((tasks, size), BF16)]
    if first:
        out.append(pltpu.VMEM((2 * tasks, design.shape[0]), BF16))
    return call(
        functools.partial(push_kernel, first, mine, begin, offset, size),
        "push_mine" if mine else "push_other",
        [SMEM] + [VMEM] * len(args),
        tuple(out),
        [VMEM] * len(out),
    )(side, *pin(pltpu.VMEM, *args))


def store_kernel(side, scale, x_ref, u_ref, z_ref, *rest):
    *hs, x_out, stage, sems = rest
    half = x_ref.shape[1] // 2
    keep = 1.0 - scale[:, 1:2]
    copies = []
    done = 0
    for c, h_ref in enumerate(hs):
        size = h_ref.shape[1]
        base = (side[0] if done < half else 1 - side[0]) * half + done % half
        done += size
        for j in range(0, size, NARROW):
            at = columns(base + j, NARROW)
            u, z = u_ref[:, at], z_ref[:, at]
            stage[:, at] = z - u + keep * keep * (x_ref[:, at] - z + u) + h_ref[:, pl.ds(j, NARROW)]
        at = columns(base, size)
        copy = pltpu.make_async_copy(stage.at[:, at], x_out.at[:, at], sems.at[c])
        copy.start()
        copies.append(copy)
    for copy in copies:
        copy.wait()


def store_x(side, scale, x, u, z, mines, others):
    tasks, width = x.shape
    args = [scale, x, u, z, *mines, *others]
    return call(
        store_kernel,
        "store_x",
        [SMEM] + [VMEM] * len(args),
        pltpu.HBM((tasks, width), F32),
        HBM,
        [pltpu.VMEM((tasks, width), F32), pltpu.SemaphoreType.DMA((len(mines) + len(others),))],
    )(side, *pin(pltpu.VMEM, *args))


def final_kernel(blocks_count, pieces, buffered, side, scale, x_ref, u_ref, z_ref, *refs):
    outs = refs[3 * len(pieces) + 2 * buffered :][:2]
    stage, sems = refs[-2:]
    half = x_ref.shape[1] // 2
    pull, limit = scale[:, 1:2], scale[:, 2:3]
    keep = 1.0 - pull
    copies, filled = [], 0
    for k, (mine, begin, offset, size) in enumerate(pieces):
        start, h, pushed = refs[3 * k : 3 * k + 3]
        base = (side[0] if mine else 1 - side[0]) * half + begin
        for j in range(0, size, NARROW):
            cut, here = columns(base + j, NARROW), pl.ds(filled + j, NARROW)
            z = z_ref[:, cut]
            total = keep * keep * start[:, pl.ds(begin + j, NARROW)] + pushed[:, pl.ds(j, NARROW)].astype(F32)
            mean = total * (1.0 / blocks_count) + pull * (1.0 + keep) * z
            new_z = mean - jnp.clip(mean, -limit, limit)
            moved = z + keep * keep * (x_ref[:, cut] - z + u_ref[:, cut]) + h[:, pl.ds(offset + j, NARROW)]
            stage[0, :, here] = new_z
            stage[1, :, here] = moved - new_z
        cut, here = columns(base, size), pl.ds(filled, size)
        for o in range(2):
            copy = pltpu.make_async_copy(stage.at[o, :, here], outs[o].at[:, cut], sems.at[k, o])
            copy.start()
            copies.append(copy)
        filled += size
    for copy in copies:
        copy.wait()


def final(side, scale, x, u, z, pieces, buffers, blocks_count):
    tasks, width = x.shape
    buffered = buffers is not None
    args = pin(pltpu.VMEM, scale, x, u, z, *(v for piece in pieces for v in piece[3:]))
    vmem = len(args)
    places = [(*piece[:3], piece[5].shape[1]) for piece in pieces]
    out = pltpu.HBM((tasks, width), F32)
    aliases = {}
    if buffered:
        aliases = {1 + vmem + o: o for o in range(2)}
        args += pin(pltpu.HBM, *buffers)
    return call(
        functools.partial(final_kernel, blocks_count, places, buffered),
        "final",
        [SMEM] + [VMEM] * vmem + [HBM] * (2 * buffered),
        (out, out),
        [HBM] * 2,
        [pltpu.VMEM((2, tasks, sum(p[3] for p in places)), F32), pltpu.SemaphoreType.DMA((len(pieces), 2))],
        aliases,
    )(side, *args)


def tie(value, *after):
    return lax.optimization_barrier((value, after))[0]


def per_device(design, labels, local_x, dual_u, consensus_z, step_size, rho, penalty):
    tasks, width = consensus_z.shape
    half = width // 2
    blocks_count = lax.axis_size("rows")
    side = (lax.axis_index("rows") & 1).astype(jnp.int32)[None]

    margin1, pulled, design, x0, dual, z, sign, scale, start_mine, start_other = load(
        side, local_x[0], dual_u[0], consensus_z, design, labels, step_size, rho, penalty, blocks_count
    )
    start_mine = start_mine + exchange(start_other, "rows", 1)

    terms, grams = [margin1], {}
    for step in range(max(lax.axis_size("feat").bit_length() - 1, 3)):
        more = (1 << step) < lax.axis_size("feat")
        if step > 0 and more:
            terms = [sum(t.astype(F32) for t in terms).astype(BF16)]
        made = gram_blocks(step, tie(side, terms[0]), design) if step < 3 else {}
        grams.update(made)
        if more:
            got = exchange(terms[0], "feat", 1 << step)
            terms.append(tie(got, made, start_mine) if step == 0 else tie(got, made) if step == 1 else got)

    resid1, margin2 = turn(sign, terms, scale, pulled, grams)
    terms = square_sum(margin2, "feat")
    mask = 2
    while mask < blocks_count:
        start_mine = start_mine + exchange(start_mine, "rows", mask)
        mask *= 2
    terms = tie(terms, start_mine)
    sizes = [half * part // sum(MINE) for part in MINE]
    begins = [sum(sizes[:c]) for c in range(len(sizes))]
    other_sizes = [half * part // sum(OTHER) for part in OTHER]
    other_begins = [sum(other_sizes[:c]) for c in range(len(other_sizes))]
    count = len(sizes)
    others, received = [], []
    resid = (resid1, sign, *terms)
    for begin, size in zip(other_begins, other_sizes):
        value, other, *made = push(side, resid, scale, design, None, begin, 0, size)
        resid = made[0] if made else resid
        others.append(value)
        received.append(exchange(other, "rows", 1))
    mines, sums, places = [], [], []
    token = tie(side, others[-1])
    for begin, size in zip(begins, sizes):
        source = max(k for k, b in enumerate(other_begins) if b <= begin)
        places.append((source, begin - other_begins[source]))
        value, sent = push(token, resid, scale, design, received[source], begin, places[-1][1], size)
        mines.append(value)
        sums.append(doubling(sent, "rows", 2))
        token = tie(side, sent)
    new_x = store_x(side, scale, x0, dual, z, mines, others)

    start_theirs = exchange(tie(start_mine, mines[0]), "rows", 1)

    pieces, backs, results = [], [], None
    for c, (a, b) in enumerate(sums):
        b = tie(b, new_x, results)
        pieces.append((a.astype(F32) + b.astype(F32)).astype(BF16))
        backs.append(exchange(pieces[c], "rows", 1))
        for group in PLAN[c]:
            work = []
            for mine, k in group:
                source, offset = places[k]
                if mine:
                    work.append((True, begins[k], 0, start_mine, mines[k], pieces[k]))
                else:
                    work.append((False, begins[k], offset, start_theirs, others[source], backs[k]))
            results = final(side, scale, x0, dual, z, work, results, blocks_count)
    new_z, new_u = results
    return (new_x[None], new_z, new_u[None])


def solution(mesh):
    in_specs = (
        P("rows", "feat"),
        P(None, "rows"),
        P("rows", None, "feat"),
        P("rows", None, "feat"),
        P(None, "feat"),
        P(),
        P(),
        P(),
    )
    out_specs = (P("rows", None, "feat"), P(None, "feat"), P("rows", None, "feat"))
    return jax.shard_map(
        per_device, mesh=mesh, in_specs=in_specs, out_specs=out_specs, check_vma=False
    )
```

```python
import functools
import math

import jax
import jax.numpy as jnp
from jax import lax
from jax.experimental import pallas as pl
from jax.experimental.pallas import tpu as pltpu
from jax.sharding import PartitionSpec as P

BF16 = jnp.bfloat16
F32 = jnp.float32
PLAN = ((((True, 0),),), (((False, 0), (True, 1)),), (((False, 1), (True, 2)), ((False, 2),)))
MINE = (3, 3, 2)
OTHER = (3, 5)
STEP = 1024
WIDE = 2048
AHEAD = 8
NARROW = 256
WAIT_BYTES = 10_000_000
HBM = pl.BlockSpec(memory_space=pltpu.HBM)
VMEM = pl.BlockSpec(memory_space=pltpu.VMEM)
SMEM = pl.BlockSpec(memory_space=pltpu.SMEM)


def exchange(value, axis, mask):
    n = lax.axis_size(axis)
    return lax.ppermute(value, axis, [(i, i ^ mask) for i in range(n)])


def doubling(value, axis, first=1):
    n = lax.axis_size(axis)
    mask = first
    other = exchange(value, axis, mask)
    while 2 * mask < n:
        mask *= 2
        value = (value.astype(F32) + other.astype(F32)).astype(value.dtype)
        other = exchange(value, axis, mask)
    return value, other


def square_sum(value, axis):
    n = lax.axis_size(axis)
    terms = [value]
    mask = 1
    while mask < n:
        if len(terms) > 1:
            terms = [sum(t.astype(F32) for t in terms).astype(value.dtype)]
        steps = [3 * mask, 2 * mask, mask] if 2 * mask < n else [mask]
        terms += [exchange(terms[0], axis, step) for step in steps]
        mask *= 4
    return terms


def nt(a, b):
    return lax.dot_general(a, b, (((1,), (1,)), ((), ())), preferred_element_type=F32)


def call(kernel, name, in_specs, out_shape, out_specs, scratch=(), aliases=None, limit=16, work=1000):
    return pl.pallas_call(
        kernel,
        in_specs=in_specs,
        out_shape=out_shape,
        out_specs=out_specs,
        scratch_shapes=list(scratch),
        input_output_aliases=aliases or {},
        compiler_params=pltpu.CompilerParams(vmem_limit_bytes=limit * 1024 * 1024),
        cost_estimate=pl.CostEstimate(flops=1000, bytes_accessed=work, transcendentals=0),
        name=name,
    )


def pin(space, *values):
    return [pltpu.with_memory_space_constraint(v, space) for v in values]


def columns(start, size):
    return pl.ds(pl.multiple_of(start, 128), size)


def load_kernel(blocks_count, side, x_hbm, u_hbm, z_hbm, a_hbm, sign_hbm, eta_hbm, rho_hbm, lam_hbm, *refs):
    outs, (eta_row, rho_row, lam_row, both, acc, sems) = refs[:10], refs[10:]
    m_out, pulled_out, a_out, x_out, u_out, z_out, sign_out, scale, mine_out, other_out = outs
    tasks, width = x_hbm.shape
    steps = width // STEP
    rows = ((eta_hbm, eta_row), (rho_hbm, rho_row), (lam_hbm, lam_row), (sign_hbm, sign_out))
    small = [pltpu.make_async_copy(a, b, sems.at[4, k]) for k, (a, b) in enumerate(rows)]

    def chunk(j):
        at = columns(j * STEP, STEP)
        pairs = ((x_hbm, x_out), (u_hbm, u_out), (z_hbm, z_out), (a_hbm, a_out))
        return [pltpu.make_async_copy(a.at[:, at], b.at[:, at], sems.at[k, j]) for k, (a, b) in enumerate(pairs)]

    def begin(j):
        for copy in chunk(j):
            copy.start()

    for copy in small[:3]:
        copy.start()
    for j in range(min(AHEAD, steps)):
        begin(j)
    for copy in small[:3]:
        copy.wait()
    one = lax.broadcasted_iota(jnp.int32, (tasks, tasks), 0) == lax.broadcasted_iota(jnp.int32, (tasks, tasks), 1)
    eta, rho, lam = eta_row[...], rho_row[...], lam_row[...]
    for k, row in enumerate((eta, eta * rho, lam / (rho * blocks_count))):
        upright = jnp.where(one, jnp.broadcast_to(row, (tasks, tasks)), 0.0)
        scale[:, k : k + 1] = jnp.sum(upright, axis=1, keepdims=True)
    acc[...] = jnp.zeros_like(acc)

    @pl.loop(0, steps)
    def _(j):
        for copy in chunk(j):
            copy.wait()

        @pl.when(j + AHEAD < steps)
        def _():
            begin(j + AHEAD)

        @pl.when(j == max(steps - AHEAD, 0))
        def _():
            small[3].start()

        pull = scale[:, 1:2]
        for k in range(0, STEP, NARROW):
            at, here = columns(j * STEP + k, NARROW), pl.ds(k, NARROW)
            x = x_out[:, at]
            v = x - pull * (x - z_out[:, at] + u_out[:, at])
            both[:tasks, here] = x.astype(BF16)
            both[tasks:, here] = v.astype(BF16)
        acc[...] += nt(both[...], a_out[:, columns(j * STEP, STEP)])

    m_out[...] = acc[:tasks].astype(BF16)
    pulled_out[...] = acc[tasks:]
    half = width // 2
    mine = columns(side[0] * half, half)
    other = columns((1 - side[0]) * half, half)
    mine_out[...] = x_out[:, mine] + u_out[:, mine]
    other_out[...] = x_out[:, other] + u_out[:, other]
    small[3].wait()


def load(side, x, u, z, design, sign, step_size, rho, penalty, blocks_count):
    tasks, width = x.shape
    samples = design.shape[0]
    full = pltpu.VMEM((tasks, width), F32)
    half = pltpu.VMEM((tasks, width // 2), F32)
    rows = [v.reshape(1, tasks) for v in (step_size, rho, penalty)]
    return call(
        functools.partial(load_kernel, blocks_count),
        "load_and_margins",
        [SMEM] + [HBM] * 8,
        (
            pltpu.VMEM((tasks, samples), BF16), pltpu.VMEM((tasks, samples), F32), pltpu.VMEM(design.shape, BF16),
            full, full, full, pltpu.VMEM(sign.shape, jnp.int32), pltpu.VMEM((tasks, 128), F32), half, half,
        ),
        [VMEM] * 10,
        [pltpu.VMEM((1, tasks), F32)] * 3
        + [
            pltpu.VMEM((2 * tasks, STEP), BF16), pltpu.VMEM((2 * tasks, samples), F32),
            pltpu.SemaphoreType.DMA((5, max(width // STEP, 4))),
        ],
    )(side, *pin(pltpu.HBM, x, u, z, design, sign, *rows))


GRAM_STEPS = (((0, 0), (2, 2)), ((1, 0), (1, 1)), ((2, 0), (2, 1)))


def gram_kernel(blocks, token, a_ref, *refs):
    high, low, acc = refs
    size = high.shape[0]
    width = a_ref.shape[1]
    wide = math.gcd(WIDE, width)
    rows = sorted({row for row, _ in blocks})
    done = 0
    for row in rows:
        cols = [col for r, col in blocks if r == row]
        span = pl.ds(cols[0] * size, len(cols) * size)
        here = pl.ds(0, len(cols) * size)
        for j in range(width // wide):
            at = pl.ds(j * wide, wide)
            product = nt(a_ref[pl.ds(row * size, size), at], a_ref[span, at])
            acc[:, here] = product if j == 0 else acc[:, here] + product
        there = pl.ds(done * size, len(cols) * size)
        whole = acc[:, here]
        top = whole.astype(BF16)
        high[:, there] = top
        low[:, there] = (whole - top.astype(F32)).astype(BF16)
        done += len(cols)


def gram_blocks(step, token, design):
    samples = design.shape[0]
    size = samples // 3
    blocks = GRAM_STEPS[step]
    out = pltpu.VMEM((size, len(blocks) * size), BF16)
    return call(
        functools.partial(gram_kernel, blocks),
        "gram",
        [SMEM, VMEM],
        (out, out),
        [VMEM] * 2,
        [pltpu.VMEM((size, 2 * size), F32)],
        work=WAIT_BYTES * (step + 1) // 3,
    )(token, *pin(pltpu.VMEM, design))


def residual(sign, *terms):
    margin = sum(t.astype(F32) for t in terms)
    sign = sign.astype(F32)
    return (sign * jax.nn.sigmoid(-sign * margin)).astype(BF16)


def turn_kernel(sign, scale, pulled, *refs):
    *terms, resid, out = refs[6:]
    size = refs[0].shape[0]
    grams = {}
    for k, blocks in enumerate(GRAM_STEPS):
        for j, block in enumerate(blocks):
            grams[block] = [refs[2 * k + part].at[:, pl.ds(j * size, size)] for part in range(2)]
    resid[...] = residual(sign[...], *(t[...] for t in terms))
    eta = scale[:, 0:1]
    r = [resid[:, pl.ds(k * size, size)] for k in range(3)]
    for col in range(3):
        total = jnp.zeros((resid.shape[0], size), F32)
        for row in range(3):
            for part in range(2):
                if row >= col:
                    total += jnp.dot(r[row], grams[row, col][part][...], preferred_element_type=F32)
                else:
                    total += nt(r[row], grams[col, row][part][...])
        here = pl.ds(col * size, size)
        out[:, here] = (pulled[:, here] + eta * total).astype(BF16)


def turn(sign, terms, scale, pulled, grams):
    tasks, samples = pulled.shape
    out = pltpu.VMEM((tasks, samples), BF16)
    args = [sign, scale, pulled, *grams, *terms]
    return call(turn_kernel, "turn", [VMEM] * len(args), (out, out), [VMEM] * 2)(*pin(pltpu.VMEM, *args))


def push_kernel(first, mine, begin, offset, size, side, *refs):
    tasks = refs[0].shape[0]
    if first:
        scale, a_ref, resid1, sign, *terms, h_out, sent_out, resid = refs
        resid[:tasks] = resid1[...]
        resid[tasks:] = residual(sign[...], *(t[...] for t in terms))
    else:
        scale, a_ref, resid, *received, h_out, sent_out = refs
    half = a_ref.shape[1] // 2
    eta = scale[:, 0:1]
    keep = 1.0 - scale[:, 1:2]
    base = (side[0] if mine else 1 - side[0]) * half + begin
    step = math.gcd(512, size)
    for j in range(size // step):
        at = columns(base + j * step, step)
        here = pl.ds(j * step, step)
        grads = jnp.dot(resid[...], a_ref[:, at], preferred_element_type=F32)
        push = eta * (keep * grads[:tasks] + grads[tasks:])
        h_out[:, here] = push
        if mine:
            push = push + received[0][:, pl.ds(offset + j * step, step)].astype(F32)
        sent_out[:, here] = push.astype(BF16)


def push(side, resid, scale, design, received, begin, offset, size):
    tasks = scale.shape[0]
    mine = received is not None
    first = isinstance(resid, tuple)
    args = [scale, design, *(resid if first else [resid])] + ([received] if mine else [])
    out = [pltpu.VMEM((tasks, size), F32), pltpu.VMEM((tasks, size), BF16)]
    if first:
        out.append(pltpu.VMEM((2 * tasks, design.shape[0]), BF16))
    return call(
        functools.partial(push_kernel, first, mine, begin, offset, size),
        "push_mine" if mine else "push_other",
        [SMEM] + [VMEM] * len(args),
        tuple(out),
        [VMEM] * len(out),
    )(side, *pin(pltpu.VMEM, *args))


def store_kernel(side, scale, x_ref, u_ref, z_ref, *rest):
    *hs, x_out, stage, sems = rest
    half = x_ref.shape[1] // 2
    keep = 1.0 - scale[:, 1:2]
    copies = []
    done = 0
    for c, h_ref in enumerate(hs):
        size = h_ref.shape[1]
        base = (side[0] if done < half else 1 - side[0]) * half + done % half
        done += size
        for j in range(0, size, NARROW):
            at = columns(base + j, NARROW)
            u, z = u_ref[:, at], z_ref[:, at]
            stage[:, at] = z - u + keep * keep * (x_ref[:, at] - z + u) + h_ref[:, pl.ds(j, NARROW)]
        at = columns(base, size)
        copy = pltpu.make_async_copy(stage.at[:, at], x_out.at[:, at], sems.at[c])
        copy.start()
        copies.append(copy)
    for copy in copies:
        copy.wait()


def store_x(side, scale, x, u, z, mines, others):
    tasks, width = x.shape
    args = [scale, x, u, z, *mines, *others]
    return call(
        store_kernel,
        "store_x",
        [SMEM] + [VMEM] * len(args),
        pltpu.HBM((tasks, width), F32),
        HBM,
        [pltpu.VMEM((tasks, width), F32), pltpu.SemaphoreType.DMA((len(mines) + len(others),))],
    )(side, *pin(pltpu.VMEM, *args))


def final_kernel(blocks_count, pieces, buffered, side, scale, x_ref, u_ref, z_ref, *refs):
    outs = refs[3 * len(pieces) + 2 * buffered :][:2]
    stage, sems = refs[-2:]
    half = x_ref.shape[1] // 2
    pull, limit = scale[:, 1:2], scale[:, 2:3]
    keep = 1.0 - pull
    copies, filled = [], 0
    for k, (mine, begin, offset, size) in enumerate(pieces):
        start, h, pushed = refs[3 * k : 3 * k + 3]
        base = (side[0] if mine else 1 - side[0]) * half + begin
        for j in range(0, size, NARROW):
            cut, here = columns(base + j, NARROW), pl.ds(filled + j, NARROW)
            z = z_ref[:, cut]
            total = keep * keep * start[:, pl.ds(begin + j, NARROW)] + pushed[:, pl.ds(j, NARROW)].astype(F32)
            mean = total * (1.0 / blocks_count) + pull * (1.0 + keep) * z
            new_z = mean - jnp.clip(mean, -limit, limit)
            moved = z + keep * keep * (x_ref[:, cut] - z + u_ref[:, cut]) + h[:, pl.ds(offset + j, NARROW)]
            stage[0, :, here] = new_z
            stage[1, :, here] = moved - new_z
        cut, here = columns(base, size), pl.ds(filled, size)
        for o in range(2):
            copy = pltpu.make_async_copy(stage.at[o, :, here], outs[o].at[:, cut], sems.at[k, o])
            copy.start()
            copies.append(copy)
        filled += size
    for copy in copies:
        copy.wait()


def final(side, scale, x, u, z, pieces, buffers, blocks_count):
    tasks, width = x.shape
    buffered = buffers is not None
    args = pin(pltpu.VMEM, scale, x, u, z, *(v for piece in pieces for v in piece[3:]))
    vmem = len(args)
    places = [(*piece[:3], piece[5].shape[1]) for piece in pieces]
    out = pltpu.HBM((tasks, width), F32)
    aliases = {}
    if buffered:
        aliases = {1 + vmem + o: o for o in range(2)}
        args += pin(pltpu.HBM, *buffers)
    return call(
        functools.partial(final_kernel, blocks_count, places, buffered),
        "final",
        [SMEM] + [VMEM] * vmem + [HBM] * (2 * buffered),
        (out, out),
        [HBM] * 2,
        [pltpu.VMEM((2, tasks, sum(p[3] for p in places)), F32), pltpu.SemaphoreType.DMA((len(pieces), 2))],
        aliases,
    )(side, *args)


def tie(value, *after):
    return lax.optimization_barrier((value, after))[0]


def per_device(design, labels, local_x, dual_u, consensus_z, step_size, rho, penalty):
    tasks, width = consensus_z.shape
    half = width // 2
    blocks_count = lax.axis_size("rows")
    side = (lax.axis_index("rows") & 1).astype(jnp.int32)[None]

    margin1, pulled, design, x0, dual, z, sign, scale, start_mine, start_other = load(
        side, local_x[0], dual_u[0], consensus_z, design, labels, step_size, rho, penalty, blocks_count
    )
    start_mine = start_mine + exchange(start_other, "rows", 1)

    terms, grams = [margin1], []
    for step in range(max(lax.axis_size("feat").bit_length() - 1, 3)):
        more = (1 << step) < lax.axis_size("feat")
        if step > 0 and more:
            terms = [sum(t.astype(F32) for t in terms).astype(BF16)]
        made = gram_blocks(step, tie(side, terms[0]), design) if step < 3 else []
        grams += made
        if more:
            got = exchange(terms[0], "feat", 1 << step)
            terms.append(tie(got, made[0], start_mine) if step == 0 else tie(got, made[0]) if step == 1 else got)

    resid1, margin2 = turn(sign, terms, scale, pulled, grams)
    terms = square_sum(margin2, "feat")
    mask = 2
    while mask < blocks_count:
        start_mine = start_mine + exchange(start_mine, "rows", mask)
        mask *= 2
    terms = tie(terms, start_mine)
    sizes = [half * part // sum(MINE) for part in MINE]
    begins = [sum(sizes[:c]) for c in range(len(sizes))]
    other_sizes = [half * part // sum(OTHER) for part in OTHER]
    other_begins = [sum(other_sizes[:c]) for c in range(len(other_sizes))]
    count = len(sizes)
    others, received = [], []
    resid = (resid1, sign, *terms)
    for begin, size in zip(other_begins, other_sizes):
        value, other, *made = push(side, resid, scale, design, None, begin, 0, size)
        resid = made[0] if made else resid
        others.append(value)
        received.append(exchange(other, "rows", 1))
    mines, sums, places = [], [], []
    token = tie(side, others[-1])
    for begin, size in zip(begins, sizes):
        source = max(k for k, b in enumerate(other_begins) if b <= begin)
        places.append((source, begin - other_begins[source]))
        value, sent = push(token, resid, scale, design, received[source], begin, places[-1][1], size)
        mines.append(value)
        sums.append(doubling(sent, "rows", 2))
        token = tie(side, sent)
    new_x = store_x(side, scale, x0, dual, z, mines, others)

    start_theirs = exchange(tie(start_mine, mines[0]), "rows", 1)

    pieces, backs, results = [], [], None
    for c, (a, b) in enumerate(sums):
        b = tie(b, new_x, results)
        pieces.append((a.astype(F32) + b.astype(F32)).astype(BF16))
        backs.append(exchange(pieces[c], "rows", 1))
        for group in PLAN[c]:
            work = []
            for mine, k in group:
                source, offset = places[k]
                if mine:
                    work.append((True, begins[k], 0, start_mine, mines[k], pieces[k]))
                else:
                    work.append((False, begins[k], offset, start_theirs, others[source], backs[k]))
            results = final(side, scale, x0, dual, z, work, results, blocks_count)
    new_z, new_u = results
    return (new_x[None], new_z, new_u[None])


def solution(mesh):
    in_specs = (
        P("rows", "feat"),
        P(None, "rows"),
        P("rows", None, "feat"),
        P("rows", None, "feat"),
        P(None, "feat"),
        P(),
        P(),
        P(),
    )
    out_specs = (P("rows", None, "feat"), P(None, "feat"), P("rows", None, "feat"))
    return jax.shard_map(
        per_device, mesh=mesh, in_specs=in_specs, out_specs=out_specs, check_vma=False
    )
```

```python
import functools
import math

import jax
import jax.numpy as jnp
from jax import lax
from jax.experimental import pallas as pl
from jax.experimental.pallas import tpu as pltpu
from jax.sharding import PartitionSpec as P

BF16 = jnp.bfloat16
F32 = jnp.float32
PLAN = ((((True, 0),),), (((False, 0), (True, 1)),), (((False, 1), (True, 2)), ((False, 2),)))
MINE = (2, 4, 2)
OTHER = (2, 6)
STEP = 1024
WIDE = 2048
AHEAD = 8
NARROW = 256
WAIT_BYTES = 10_000_000
HBM = pl.BlockSpec(memory_space=pltpu.HBM)
VMEM = pl.BlockSpec(memory_space=pltpu.VMEM)
SMEM = pl.BlockSpec(memory_space=pltpu.SMEM)


def exchange(value, axis, mask):
    n = lax.axis_size(axis)
    return lax.ppermute(value, axis, [(i, i ^ mask) for i in range(n)])


def doubling(value, axis, first=1):
    n = lax.axis_size(axis)
    mask = first
    other = exchange(value, axis, mask)
    while 2 * mask < n:
        mask *= 2
        value = (value.astype(F32) + other.astype(F32)).astype(value.dtype)
        other = exchange(value, axis, mask)
    return value, other


def square_sum(value, axis):
    n = lax.axis_size(axis)
    terms = [value]
    mask = 1
    while mask < n:
        if len(terms) > 1:
            terms = [sum(t.astype(F32) for t in terms).astype(value.dtype)]
        steps = [3 * mask, 2 * mask, mask] if 2 * mask < n else [mask]
        terms += [exchange(terms[0], axis, step) for step in steps]
        mask *= 4
    return terms


def nt(a, b):
    return lax.dot_general(a, b, (((1,), (1,)), ((), ())), preferred_element_type=F32)


def call(kernel, name, in_specs, out_shape, out_specs, scratch=(), aliases=None, limit=16, work=1000):
    return pl.pallas_call(
        kernel,
        in_specs=in_specs,
        out_shape=out_shape,
        out_specs=out_specs,
        scratch_shapes=list(scratch),
        input_output_aliases=aliases or {},
        compiler_params=pltpu.CompilerParams(vmem_limit_bytes=limit * 1024 * 1024),
        cost_estimate=pl.CostEstimate(flops=1000, bytes_accessed=work, transcendentals=0),
        name=name,
    )


def pin(space, *values):
    return [pltpu.with_memory_space_constraint(v, space) for v in values]


def columns(start, size):
    return pl.ds(pl.multiple_of(start, 128), size)


def load_kernel(blocks_count, side, x_hbm, u_hbm, z_hbm, a_hbm, sign_hbm, eta_hbm, rho_hbm, lam_hbm, *refs):
    outs, (eta_row, rho_row, lam_row, both, acc, sems) = refs[:10], refs[10:]
    m_out, pulled_out, a_out, x_out, u_out, z_out, sign_out, scale, mine_out, other_out = outs
    tasks, width = x_hbm.shape
    steps = width // STEP
    rows = ((eta_hbm, eta_row), (rho_hbm, rho_row), (lam_hbm, lam_row), (sign_hbm, sign_out))
    small = [pltpu.make_async_copy(a, b, sems.at[4, k]) for k, (a, b) in enumerate(rows)]

    def chunk(j):
        at = columns(j * STEP, STEP)
        pairs = ((x_hbm, x_out), (u_hbm, u_out), (z_hbm, z_out), (a_hbm, a_out))
        return [pltpu.make_async_copy(a.at[:, at], b.at[:, at], sems.at[k, j]) for k, (a, b) in enumerate(pairs)]

    def begin(j):
        for copy in chunk(j):
            copy.start()

    for copy in small[:3]:
        copy.start()
    for j in range(min(AHEAD, steps)):
        begin(j)
    for copy in small[:3]:
        copy.wait()
    one = lax.broadcasted_iota(jnp.int32, (tasks, tasks), 0) == lax.broadcasted_iota(jnp.int32, (tasks, tasks), 1)
    eta, rho, lam = eta_row[...], rho_row[...], lam_row[...]
    for k, row in enumerate((eta, eta * rho, lam / (rho * blocks_count))):
        upright = jnp.where(one, jnp.broadcast_to(row, (tasks, tasks)), 0.0)
        scale[:, k : k + 1] = jnp.sum(upright, axis=1, keepdims=True)
    acc[...] = jnp.zeros_like(acc)

    @pl.loop(0, steps)
    def _(j):
        for copy in chunk(j):
            copy.wait()

        @pl.when(j + AHEAD < steps)
        def _():
            begin(j + AHEAD)

        @pl.when(j == max(steps - AHEAD, 0))
        def _():
            small[3].start()

        pull = scale[:, 1:2]
        for k in range(0, STEP, NARROW):
            at, here = columns(j * STEP + k, NARROW), pl.ds(k, NARROW)
            x = x_out[:, at]
            v = x - pull * (x - z_out[:, at] + u_out[:, at])
            both[:tasks, here] = x.astype(BF16)
            both[tasks:, here] = v.astype(BF16)
        acc[...] += nt(both[...], a_out[:, columns(j * STEP, STEP)])

    m_out[...] = acc[:tasks].astype(BF16)
    pulled_out[...] = acc[tasks:]
    half = width // 2
    mine = columns(side[0] * half, half)
    other = columns((1 - side[0]) * half, half)
    mine_out[...] = x_out[:, mine] + u_out[:, mine]
    other_out[...] = x_out[:, other] + u_out[:, other]
    small[3].wait()


def load(side, x, u, z, design, sign, step_size, rho, penalty, blocks_count):
    tasks, width = x.shape
    samples = design.shape[0]
    full = pltpu.VMEM((tasks, width), F32)
    half = pltpu.VMEM((tasks, width // 2), F32)
    rows = [v.reshape(1, tasks) for v in (step_size, rho, penalty)]
    return call(
        functools.partial(load_kernel, blocks_count),
        "load_and_margins",
        [SMEM] + [HBM] * 8,
        (
            pltpu.VMEM((tasks, samples), BF16), pltpu.VMEM((tasks, samples), F32), pltpu.VMEM(design.shape, BF16),
            full, full, full, pltpu.VMEM(sign.shape, jnp.int32), pltpu.VMEM((tasks, 128), F32), half, half,
        ),
        [VMEM] * 10,
        [pltpu.VMEM((1, tasks), F32)] * 3
        + [
            pltpu.VMEM((2 * tasks, STEP), BF16), pltpu.VMEM((2 * tasks, samples), F32),
            pltpu.SemaphoreType.DMA((5, max(width // STEP, 4))),
        ],
    )(side, *pin(pltpu.HBM, x, u, z, design, sign, *rows))


GRAM_STEPS = (((0, 0), (2, 2)), ((1, 0), (1, 1)), ((2, 0), (2, 1)))


def gram_kernel(blocks, token, a_ref, *refs):
    high, low, acc = refs
    size = high.shape[0]
    width = a_ref.shape[1]
    wide = math.gcd(WIDE, width)
    rows = sorted({row for row, _ in blocks})
    done = 0
    for row in rows:
        cols = [col for r, col in blocks if r == row]
        span = pl.ds(cols[0] * size, len(cols) * size)
        here = pl.ds(0, len(cols) * size)
        for j in range(width // wide):
            at = pl.ds(j * wide, wide)
            product = nt(a_ref[pl.ds(row * size, size), at], a_ref[span, at])
            acc[:, here] = product if j == 0 else acc[:, here] + product
        there = pl.ds(done * size, len(cols) * size)
        whole = acc[:, here]
        top = whole.astype(BF16)
        high[:, there] = top
        low[:, there] = (whole - top.astype(F32)).astype(BF16)
        done += len(cols)


def gram_blocks(step, token, design):
    samples = design.shape[0]
    size = samples // 3
    blocks = GRAM_STEPS[step]
    out = pltpu.VMEM((size, len(blocks) * size), BF16)
    return call(
        functools.partial(gram_kernel, blocks),
        "gram",
        [SMEM, VMEM],
        (out, out),
        [VMEM] * 2,
        [pltpu.VMEM((size, 2 * size), F32)],
        work=WAIT_BYTES * (step + 1) // 3,
    )(token, *pin(pltpu.VMEM, design))


def residual(sign, *terms):
    margin = sum(t.astype(F32) for t in terms)
    sign = sign.astype(F32)
    return (sign * jax.nn.sigmoid(-sign * margin)).astype(BF16)


def turn_kernel(sign, scale, pulled, *refs):
    *terms, resid, out = refs[6:]
    size = refs[0].shape[0]
    grams = {}
    for k, blocks in enumerate(GRAM_STEPS):
        for j, block in enumerate(blocks):
            grams[block] = [refs[2 * k + part].at[:, pl.ds(j * size, size)] for part in range(2)]
    resid[...] = residual(sign[...], *(t[...] for t in terms))
    eta = scale[:, 0:1]
    r = [resid[:, pl.ds(k * size, size)] for k in range(3)]
    for col in range(3):
        total = jnp.zeros((resid.shape[0], size), F32)
        for row in range(3):
            for part in range(2):
                if row >= col:
                    total += jnp.dot(r[row], grams[row, col][part][...], preferred_element_type=F32)
                else:
                    total += nt(r[row], grams[col, row][part][...])
        here = pl.ds(col * size, size)
        out[:, here] = (pulled[:, here] + eta * total).astype(BF16)


def turn(sign, terms, scale, pulled, grams):
    tasks, samples = pulled.shape
    out = pltpu.VMEM((tasks, samples), BF16)
    args = [sign, scale, pulled, *grams, *terms]
    return call(turn_kernel, "turn", [VMEM] * len(args), (out, out), [VMEM] * 2)(*pin(pltpu.VMEM, *args))


def push_kernel(first, mine, begin, offset, size, side, *refs):
    tasks = refs[0].shape[0]
    if first:
        scale, a_ref, resid1, sign, *terms, h_out, sent_out, resid = refs
        resid[:tasks] = resid1[...]
        resid[tasks:] = residual(sign[...], *(t[...] for t in terms))
    else:
        scale, a_ref, resid, *received, h_out, sent_out = refs
    half = a_ref.shape[1] // 2
    eta = scale[:, 0:1]
    keep = 1.0 - scale[:, 1:2]
    base = (side[0] if mine else 1 - side[0]) * half + begin
    step = math.gcd(512, size)
    for j in range(size // step):
        at = columns(base + j * step, step)
        here = pl.ds(j * step, step)
        grads = jnp.dot(resid[...], a_ref[:, at], preferred_element_type=F32)
        push = eta * (keep * grads[:tasks] + grads[tasks:])
        h_out[:, here] = push
        if mine:
            push = push + received[0][:, pl.ds(offset + j * step, step)].astype(F32)
        sent_out[:, here] = push.astype(BF16)


def push(side, resid, scale, design, received, begin, offset, size):
    tasks = scale.shape[0]
    mine = received is not None
    first = isinstance(resid, tuple)
    args = [scale, design, *(resid if first else [resid])] + ([received] if mine else [])
    out = [pltpu.VMEM((tasks, size), F32), pltpu.VMEM((tasks, size), BF16)]
    if first:
        out.append(pltpu.VMEM((2 * tasks, design.shape[0]), BF16))
    return call(
        functools.partial(push_kernel, first, mine, begin, offset, size),
        "push_mine" if mine else "push_other",
        [SMEM] + [VMEM] * len(args),
        tuple(out),
        [VMEM] * len(out),
    )(side, *pin(pltpu.VMEM, *args))


def store_kernel(side, scale, x_ref, u_ref, z_ref, *rest):
    *hs, x_out, stage, sems = rest
    half = x_ref.shape[1] // 2
    keep = 1.0 - scale[:, 1:2]
    copies = []
    done = 0
    for c, h_ref in enumerate(hs):
        size = h_ref.shape[1]
        base = (side[0] if done < half else 1 - side[0]) * half + done % half
        done += size
        for j in range(0, size, NARROW):
            at = columns(base + j, NARROW)
            u, z = u_ref[:, at], z_ref[:, at]
            stage[:, at] = z - u + keep * keep * (x_ref[:, at] - z + u) + h_ref[:, pl.ds(j, NARROW)]
        at = columns(base, size)
        copy = pltpu.make_async_copy(stage.at[:, at], x_out.at[:, at], sems.at[c])
        copy.start()
        copies.append(copy)
    for copy in copies:
        copy.wait()


def store_x(side, scale, x, u, z, mines, others):
    tasks, width = x.shape
    args = [scale, x, u, z, *mines, *others]
    return call(
        store_kernel,
        "store_x",
        [SMEM] + [VMEM] * len(args),
        pltpu.HBM((tasks, width), F32),
        HBM,
        [pltpu.VMEM((tasks, width), F32), pltpu.SemaphoreType.DMA((len(mines) + len(others),))],
    )(side, *pin(pltpu.VMEM, *args))


def final_kernel(blocks_count, pieces, buffered, side, scale, x_ref, u_ref, z_ref, *refs):
    outs = refs[3 * len(pieces) + 2 * buffered :][:2]
    stage, sems = refs[-2:]
    half = x_ref.shape[1] // 2
    pull, limit = scale[:, 1:2], scale[:, 2:3]
    keep = 1.0 - pull
    copies, filled = [], 0
    for k, (mine, begin, offset, size) in enumerate(pieces):
        start, h, pushed = refs[3 * k : 3 * k + 3]
        base = (side[0] if mine else 1 - side[0]) * half + begin
        for j in range(0, size, NARROW):
            cut, here = columns(base + j, NARROW), pl.ds(filled + j, NARROW)
            z = z_ref[:, cut]
            total = keep * keep * start[:, pl.ds(begin + j, NARROW)] + pushed[:, pl.ds(j, NARROW)].astype(F32)
            mean = total * (1.0 / blocks_count) + pull * (1.0 + keep) * z
            new_z = mean - jnp.clip(mean, -limit, limit)
            moved = z + keep * keep * (x_ref[:, cut] - z + u_ref[:, cut]) + h[:, pl.ds(offset + j, NARROW)]
            stage[0, :, here] = new_z
            stage[1, :, here] = moved - new_z
        cut, here = columns(base, size), pl.ds(filled, size)
        for o in range(2):
            copy = pltpu.make_async_copy(stage.at[o, :, here], outs[o].at[:, cut], sems.at[k, o])
            copy.start()
            copies.append(copy)
        filled += size
    for copy in copies:
        copy.wait()


def final(side, scale, x, u, z, pieces, buffers, blocks_count):
    tasks, width = x.shape
    buffered = buffers is not None
    args = pin(pltpu.VMEM, scale, x, u, z, *(v for piece in pieces for v in piece[3:]))
    vmem = len(args)
    places = [(*piece[:3], piece[5].shape[1]) for piece in pieces]
    out = pltpu.HBM((tasks, width), F32)
    aliases = {}
    if buffered:
        aliases = {1 + vmem + o: o for o in range(2)}
        args += pin(pltpu.HBM, *buffers)
    return call(
        functools.partial(final_kernel, blocks_count, places, buffered),
        "final",
        [SMEM] + [VMEM] * vmem + [HBM] * (2 * buffered),
        (out, out),
        [HBM] * 2,
        [pltpu.VMEM((2, tasks, sum(p[3] for p in places)), F32), pltpu.SemaphoreType.DMA((len(pieces), 2))],
        aliases,
    )(side, *args)


def tie(value, *after):
    return lax.optimization_barrier((value, after))[0]


def per_device(design, labels, local_x, dual_u, consensus_z, step_size, rho, penalty):
    tasks, width = consensus_z.shape
    half = width // 2
    blocks_count = lax.axis_size("rows")
    side = (lax.axis_index("rows") & 1).astype(jnp.int32)[None]

    margin1, pulled, design, x0, dual, z, sign, scale, start_mine, start_other = load(
        side, local_x[0], dual_u[0], consensus_z, design, labels, step_size, rho, penalty, blocks_count
    )
    start_mine = start_mine + exchange(start_other, "rows", 1)

    terms, grams = [margin1], []
    for step in range(max(lax.axis_size("feat").bit_length() - 1, 3)):
        more = (1 << step) < lax.axis_size("feat")
        if step > 0 and more:
            terms = [sum(t.astype(F32) for t in terms).astype(BF16)]
        made = gram_blocks(step, tie(side, terms[0]), design) if step < 3 else []
        grams += made
        if more:
            got = exchange(terms[0], "feat", 1 << step)
            terms.append(tie(got, made[0], start_mine) if step == 0 else tie(got, made[0]) if step == 1 else got)

    resid1, margin2 = turn(sign, terms, scale, pulled, grams)
    terms = square_sum(margin2, "feat")
    mask = 2
    while mask < blocks_count:
        start_mine = start_mine + exchange(start_mine, "rows", mask)
        mask *= 2
    terms = tie(terms, start_mine)
    sizes = [half * part // sum(MINE) for part in MINE]
    begins = [sum(sizes[:c]) for c in range(len(sizes))]
    other_sizes = [half * part // sum(OTHER) for part in OTHER]
    other_begins = [sum(other_sizes[:c]) for c in range(len(other_sizes))]
    count = len(sizes)
    others, received = [], []
    resid = (resid1, sign, *terms)
    for begin, size in zip(other_begins, other_sizes):
        value, other, *made = push(side, resid, scale, design, None, begin, 0, size)
        resid = made[0] if made else resid
        others.append(value)
        received.append(exchange(other, "rows", 1))
    mines, sums, places = [], [], []
    token = tie(side, others[-1])
    for begin, size in zip(begins, sizes):
        source = max(k for k, b in enumerate(other_begins) if b <= begin)
        places.append((source, begin - other_begins[source]))
        value, sent = push(token, resid, scale, design, received[source], begin, places[-1][1], size)
        mines.append(value)
        sums.append(doubling(sent, "rows", 2))
        token = tie(side, sent)
    new_x = store_x(side, scale, x0, dual, z, mines, others)

    start_theirs = exchange(tie(start_mine, mines[0]), "rows", 1)

    pieces, backs, results = [], [], None
    for c, (a, b) in enumerate(sums):
        b = tie(b, new_x, results)
        pieces.append((a.astype(F32) + b.astype(F32)).astype(BF16))
        backs.append(exchange(pieces[c], "rows", 1))
        for group in PLAN[c]:
            work = []
            for mine, k in group:
                source, offset = places[k]
                if mine:
                    work.append((True, begins[k], 0, start_mine, mines[k], pieces[k]))
                else:
                    work.append((False, begins[k], offset, start_theirs, others[source], backs[k]))
            results = final(side, scale, x0, dual, z, work, results, blocks_count)
    new_z, new_u = results
    return (new_x[None], new_z, new_u[None])


def solution(mesh):
    in_specs = (
        P("rows", "feat"),
        P(None, "rows"),
        P("rows", None, "feat"),
        P("rows", None, "feat"),
        P(None, "feat"),
        P(),
        P(),
        P(),
    )
    out_specs = (P("rows", None, "feat"), P(None, "feat"), P("rows", None, "feat"))
    return jax.shard_map(
        per_device, mesh=mesh, in_specs=in_specs, out_specs=out_specs, check_vma=False
    )
```

```python
import functools
import math

import jax
import jax.numpy as jnp
from jax import lax
from jax.experimental import pallas as pl
from jax.experimental.pallas import tpu as pltpu
from jax.sharding import PartitionSpec as P

BF16 = jnp.bfloat16
F32 = jnp.float32
PLAN = ((((True, 0),),), (((False, 0), (True, 1)),), (((False, 1), (True, 2)), ((False, 2),)))
MINE = (3, 3, 2)
OTHER = (3, 5)
STEP = 1024
WIDE = 2048
AHEAD = 8
NARROW = 256
WAIT_BYTES = 10_000_000
GRAM_ORDER = (0, 1, 2)
HBM = pl.BlockSpec(memory_space=pltpu.HBM)
VMEM = pl.BlockSpec(memory_space=pltpu.VMEM)
SMEM = pl.BlockSpec(memory_space=pltpu.SMEM)


def exchange(value, axis, mask):
    n = lax.axis_size(axis)
    return lax.ppermute(value, axis, [(i, i ^ mask) for i in range(n)])


def doubling(value, axis, first=1):
    n = lax.axis_size(axis)
    mask = first
    other = exchange(value, axis, mask)
    while 2 * mask < n:
        mask *= 2
        value = (value.astype(F32) + other.astype(F32)).astype(value.dtype)
        other = exchange(value, axis, mask)
    return value, other


def square_sum(value, axis):
    n = lax.axis_size(axis)
    terms = [value]
    mask = 1
    while mask < n:
        if len(terms) > 1:
            terms = [sum(t.astype(F32) for t in terms).astype(value.dtype)]
        steps = [mask, 2 * mask, 3 * mask] if 2 * mask < n else [mask]
        terms += [exchange(terms[0], axis, step) for step in steps]
        mask *= 4
    return terms


def nt(a, b):
    return lax.dot_general(a, b, (((1,), (1,)), ((), ())), preferred_element_type=F32)


def call(kernel, name, in_specs, out_shape, out_specs, scratch=(), aliases=None, limit=16, work=1000):
    return pl.pallas_call(
        kernel,
        in_specs=in_specs,
        out_shape=out_shape,
        out_specs=out_specs,
        scratch_shapes=list(scratch),
        input_output_aliases=aliases or {},
        compiler_params=pltpu.CompilerParams(vmem_limit_bytes=limit * 1024 * 1024),
        cost_estimate=pl.CostEstimate(flops=1000, bytes_accessed=work, transcendentals=0),
        name=name,
    )


def pin(space, *values):
    return [pltpu.with_memory_space_constraint(v, space) for v in values]


def columns(start, size):
    return pl.ds(pl.multiple_of(start, 128), size)


def load_kernel(blocks_count, side, x_hbm, u_hbm, z_hbm, a_hbm, sign_hbm, eta_hbm, rho_hbm, lam_hbm, *refs):
    outs, (eta_row, rho_row, lam_row, both, acc, sems) = refs[:10], refs[10:]
    m_out, pulled_out, a_out, x_out, u_out, z_out, sign_out, scale, mine_out, other_out = outs
    tasks, width = x_hbm.shape
    steps = width // STEP
    rows = ((eta_hbm, eta_row), (rho_hbm, rho_row), (lam_hbm, lam_row), (sign_hbm, sign_out))
    small = [pltpu.make_async_copy(a, b, sems.at[4, k]) for k, (a, b) in enumerate(rows)]

    def chunk(j):
        at = columns(j * STEP, STEP)
        pairs = ((x_hbm, x_out), (u_hbm, u_out), (z_hbm, z_out), (a_hbm, a_out))
        return [pltpu.make_async_copy(a.at[:, at], b.at[:, at], sems.at[k, j]) for k, (a, b) in enumerate(pairs)]

    def begin(j):
        for copy in chunk(j):
            copy.start()

    for copy in small[:3]:
        copy.start()
    for j in range(min(AHEAD, steps)):
        begin(j)
    for copy in small[:3]:
        copy.wait()
    one = lax.broadcasted_iota(jnp.int32, (tasks, tasks), 0) == lax.broadcasted_iota(jnp.int32, (tasks, tasks), 1)
    eta, rho, lam = eta_row[...], rho_row[...], lam_row[...]
    for k, row in enumerate((eta, eta * rho, lam / (rho * blocks_count))):
        upright = jnp.where(one, jnp.broadcast_to(row, (tasks, tasks)), 0.0)
        scale[:, k : k + 1] = jnp.sum(upright, axis=1, keepdims=True)
    acc[...] = jnp.zeros_like(acc)

    @pl.loop(0, steps)
    def _(j):
        for copy in chunk(j):
            copy.wait()

        @pl.when(j + AHEAD < steps)
        def _():
            begin(j + AHEAD)

        @pl.when(j == max(steps - AHEAD, 0))
        def _():
            small[3].start()

        pull = scale[:, 1:2]
        for k in range(0, STEP, NARROW):
            at, here = columns(j * STEP + k, NARROW), pl.ds(k, NARROW)
            x = x_out[:, at]
            v = x - pull * (x - z_out[:, at] + u_out[:, at])
            both[:tasks, here] = x.astype(BF16)
            both[tasks:, here] = v.astype(BF16)
        acc[...] += nt(both[...], a_out[:, columns(j * STEP, STEP)])

    m_out[...] = acc[:tasks].astype(BF16)
    pulled_out[...] = acc[tasks:]
    half = width // 2
    mine = columns(side[0] * half, half)
    other = columns((1 - side[0]) * half, half)
    mine_out[...] = x_out[:, mine] + u_out[:, mine]
    other_out[...] = x_out[:, other] + u_out[:, other]
    small[3].wait()


def load(side, x, u, z, design, sign, step_size, rho, penalty, blocks_count):
    tasks, width = x.shape
    samples = design.shape[0]
    full = pltpu.VMEM((tasks, width), F32)
    half = pltpu.VMEM((tasks, width // 2), F32)
    rows = [v.reshape(1, tasks) for v in (step_size, rho, penalty)]
    return call(
        functools.partial(load_kernel, blocks_count),
        "load_and_margins",
        [SMEM] + [HBM] * 8,
        (
            pltpu.VMEM((tasks, samples), BF16), pltpu.VMEM((tasks, samples), F32), pltpu.VMEM(design.shape, BF16),
            full, full, full, pltpu.VMEM(sign.shape, jnp.int32), pltpu.VMEM((tasks, 128), F32), half, half,
        ),
        [VMEM] * 10,
        [pltpu.VMEM((1, tasks), F32)] * 3
        + [
            pltpu.VMEM((2 * tasks, STEP), BF16), pltpu.VMEM((2 * tasks, samples), F32),
            pltpu.SemaphoreType.DMA((5, max(width // STEP, 4))),
        ],
    )(side, *pin(pltpu.HBM, x, u, z, design, sign, *rows))


def gram_block(a_ref, row, cols, size, acc, high, low):
    width = a_ref.shape[1]
    wide = math.gcd(WIDE, width)
    for j in range(width // wide):
        at = pl.ds(j * wide, wide)
        product = nt(a_ref[pl.ds(row, size), at], a_ref[pl.ds(0, cols), at])
        acc[:, :cols] = product if j == 0 else acc[:, :cols] + product
    whole = acc[:, :cols]
    top = whole.astype(BF16)
    high[...] = top
    low[...] = (whole - top.astype(F32)).astype(BF16)


def gram_kernel(row, token, a_ref, high, low, acc):
    size = high.shape[0]
    gram_block(a_ref, row * size, (row + 1) * size, size, acc, high, low)


def gram_row(row, token, design):
    samples = design.shape[0]
    size = samples // 3
    out = pltpu.VMEM((size, (row + 1) * size), BF16)
    return call(
        functools.partial(gram_kernel, row),
        "gram",
        [SMEM, VMEM],
        (out, out),
        [VMEM] * 2,
        [pltpu.VMEM((size, (row + 1) * size), F32)],
        work=WAIT_BYTES * (row + 1) // 3,
    )(token, *pin(pltpu.VMEM, design))


def residual(sign, *terms):
    margin = sum(t.astype(F32) for t in terms)
    sign = sign.astype(F32)
    return (sign * jax.nn.sigmoid(-sign * margin)).astype(BF16)


def turn_kernel(sign, scale, pulled, *refs):
    *terms, resid, out = refs[6:]
    grams = refs[:6]
    size = grams[0].shape[0]
    resid[...] = residual(sign[...], *(t[...] for t in terms))
    eta = scale[:, 0:1]
    r = [resid[:, pl.ds(k * size, size)] for k in range(3)]
    for col in range(3):
        total = jnp.zeros((resid.shape[0], size), F32)
        for row in range(3):
            for part in range(2):
                if row >= col:
                    block = grams[2 * row + part][:, pl.ds(col * size, size)]
                    total += jnp.dot(r[row], block, preferred_element_type=F32)
                else:
                    total += nt(r[row], grams[2 * col + part][:, pl.ds(row * size, size)])
        here = pl.ds(col * size, size)
        out[:, here] = (pulled[:, here] + eta * total).astype(BF16)


def turn(sign, terms, scale, pulled, grams):
    tasks, samples = pulled.shape
    out = pltpu.VMEM((tasks, samples), BF16)
    args = [sign, scale, pulled, *grams, *terms]
    return call(turn_kernel, "turn", [VMEM] * len(args), (out, out), [VMEM] * 2)(*pin(pltpu.VMEM, *args))


def push_kernel(first, mine, begin, offset, size, side, *refs):
    tasks = refs[0].shape[0]
    if first:
        scale, a_ref, resid1, sign, *terms, h_out, sent_out, resid = refs
        resid[:tasks] = resid1[...]
        resid[tasks:] = residual(sign[...], *(t[...] for t in terms))
    else:
        scale, a_ref, resid, *received, h_out, sent_out = refs
    half = a_ref.shape[1] // 2
    eta = scale[:, 0:1]
    keep = 1.0 - scale[:, 1:2]
    base = (side[0] if mine else 1 - side[0]) * half + begin
    step = math.gcd(512, size)
    for j in range(size // step):
        at = columns(base + j * step, step)
        here = pl.ds(j * step, step)
        grads = jnp.dot(resid[...], a_ref[:, at], preferred_element_type=F32)
        push = eta * (keep * grads[:tasks] + grads[tasks:])
        h_out[:, here] = push
        if mine:
            push = push + received[0][:, pl.ds(offset + j * step, step)].astype(F32)
        sent_out[:, here] = push.astype(BF16)


def push(side, resid, scale, design, received, begin, offset, size):
    tasks = scale.shape[0]
    mine = received is not None
    first = isinstance(resid, tuple)
    args = [scale, design, *(resid if first else [resid])] + ([received] if mine else [])
    out = [pltpu.VMEM((tasks, size), F32), pltpu.VMEM((tasks, size), BF16)]
    if first:
        out.append(pltpu.VMEM((2 * tasks, design.shape[0]), BF16))
    return call(
        functools.partial(push_kernel, first, mine, begin, offset, size),
        "push_mine" if mine else "push_other",
        [SMEM] + [VMEM] * len(args),
        tuple(out),
        [VMEM] * len(out),
    )(side, *pin(pltpu.VMEM, *args))


def store_kernel(side, scale, x_ref, u_ref, z_ref, *rest):
    *hs, x_out, stage, sems = rest
    half = x_ref.shape[1] // 2
    keep = 1.0 - scale[:, 1:2]
    copies = []
    done = 0
    for c, h_ref in enumerate(hs):
        size = h_ref.shape[1]
        base = (side[0] if done < half else 1 - side[0]) * half + done % half
        done += size
        for j in range(0, size, NARROW):
            at = columns(base + j, NARROW)
            u, z = u_ref[:, at], z_ref[:, at]
            stage[:, at] = z - u + keep * keep * (x_ref[:, at] - z + u) + h_ref[:, pl.ds(j, NARROW)]
        at = columns(base, size)
        copy = pltpu.make_async_copy(stage.at[:, at], x_out.at[:, at], sems.at[c])
        copy.start()
        copies.append(copy)
    for copy in copies:
        copy.wait()


def store_x(side, scale, x, u, z, mines, others):
    tasks, width = x.shape
    args = [scale, x, u, z, *mines, *others]
    return call(
        store_kernel,
        "store_x",
        [SMEM] + [VMEM] * len(args),
        pltpu.HBM((tasks, width), F32),
        HBM,
        [pltpu.VMEM((tasks, width), F32), pltpu.SemaphoreType.DMA((len(mines) + len(others),))],
    )(side, *pin(pltpu.VMEM, *args))


def final_kernel(blocks_count, pieces, buffered, side, scale, x_ref, u_ref, z_ref, *refs):
    outs = refs[3 * len(pieces) + 2 * buffered :][:2]
    stage, sems = refs[-2:]
    half = x_ref.shape[1] // 2
    pull, limit = scale[:, 1:2], scale[:, 2:3]
    keep = 1.0 - pull
    copies, filled = [], 0
    for k, (mine, begin, offset, size) in enumerate(pieces):
        start, h, pushed = refs[3 * k : 3 * k + 3]
        base = (side[0] if mine else 1 - side[0]) * half + begin
        for j in range(0, size, NARROW):
            cut, here = columns(base + j, NARROW), pl.ds(filled + j, NARROW)
            z = z_ref[:, cut]
            total = keep * keep * start[:, pl.ds(begin + j, NARROW)] + pushed[:, pl.ds(j, NARROW)].astype(F32)
            mean = total * (1.0 / blocks_count) + pull * (1.0 + keep) * z
            new_z = mean - jnp.clip(mean, -limit, limit)
            moved = z + keep * keep * (x_ref[:, cut] - z + u_ref[:, cut]) + h[:, pl.ds(offset + j, NARROW)]
            stage[0, :, here] = new_z
            stage[1, :, here] = moved - new_z
        cut, here = columns(base, size), pl.ds(filled, size)
        for o in range(2):
            copy = pltpu.make_async_copy(stage.at[o, :, here], outs[o].at[:, cut], sems.at[k, o])
            copy.start()
            copies.append(copy)
        filled += size
    for copy in copies:
        copy.wait()


def final(side, scale, x, u, z, pieces, buffers, blocks_count):
    tasks, width = x.shape
    buffered = buffers is not None
    args = pin(pltpu.VMEM, scale, x, u, z, *(v for piece in pieces for v in piece[3:]))
    vmem = len(args)
    places = [(*piece[:3], piece[5].shape[1]) for piece in pieces]
    out = pltpu.HBM((tasks, width), F32)
    aliases = {}
    if buffered:
        aliases = {1 + vmem + o: o for o in range(2)}
        args += pin(pltpu.HBM, *buffers)
    return call(
        functools.partial(final_kernel, blocks_count, places, buffered),
        "final",
        [SMEM] + [VMEM] * vmem + [HBM] * (2 * buffered),
        (out, out),
        [HBM] * 2,
        [pltpu.VMEM((2, tasks, sum(p[3] for p in places)), F32), pltpu.SemaphoreType.DMA((len(pieces), 2))],
        aliases,
    )(side, *args)


def tie(value, *after):
    return lax.optimization_barrier((value, after))[0]


def per_device(design, labels, local_x, dual_u, consensus_z, step_size, rho, penalty):
    tasks, width = consensus_z.shape
    half = width // 2
    blocks_count = lax.axis_size("rows")
    side = (lax.axis_index("rows") & 1).astype(jnp.int32)[None]

    margin1, pulled, design, x0, dual, z, sign, scale, start_mine, start_other = load(
        side, local_x[0], dual_u[0], consensus_z, design, labels, step_size, rho, penalty, blocks_count
    )
    start_mine = start_mine + exchange(start_other, "rows", 1)

    terms, grams = [margin1], []
    for step in range(max(lax.axis_size("feat").bit_length() - 1, 3)):
        more = (1 << step) < lax.axis_size("feat")
        if step > 0 and more:
            terms = [sum(t.astype(F32) for t in terms).astype(BF16)]
        row = gram_row(GRAM_ORDER[step], tie(side, terms[0]), design) if step < 3 else []
        grams.append(row)
        if more:
            got = exchange(terms[0], "feat", 1 << step)
            terms.append(tie(got, row[0], start_mine) if step == 0 else tie(got, row[0]) if step == 1 else got)

    resid1, margin2 = turn(sign, terms, scale, pulled, [g for row in range(3) for g in grams[GRAM_ORDER.index(row)]])
    terms = square_sum(margin2, "feat")
    mask = 2
    while mask < blocks_count:
        start_mine = start_mine + exchange(start_mine, "rows", mask)
        mask *= 2
    terms = tie(terms, start_mine)
    sizes = [half * part // sum(MINE) for part in MINE]
    begins = [sum(sizes[:c]) for c in range(len(sizes))]
    other_sizes = [half * part // sum(OTHER) for part in OTHER]
    other_begins = [sum(other_sizes[:c]) for c in range(len(other_sizes))]
    count = len(sizes)
    others, received = [], []
    resid = (resid1, sign, *terms)
    for begin, size in zip(other_begins, other_sizes):
        value, other, *made = push(side, resid, scale, design, None, begin, 0, size)
        resid = made[0] if made else resid
        others.append(value)
        received.append(exchange(other, "rows", 1))
    mines, sums, places = [], [], []
    token = tie(side, others[-1])
    for begin, size in zip(begins, sizes):
        source = max(k for k, b in enumerate(other_begins) if b <= begin)
        places.append((source, begin - other_begins[source]))
        value, sent = push(token, resid, scale, design, received[source], begin, places[-1][1], size)
        mines.append(value)
        sums.append(doubling(sent, "rows", 2))
        token = tie(side, sent)
    new_x = store_x(side, scale, x0, dual, z, mines, others)

    start_theirs = exchange(tie(start_mine, mines[0]), "rows", 1)

    pieces, backs, results = [], [], None
    for c, (a, b) in enumerate(sums):
        b = tie(b, new_x, results)
        pieces.append((a.astype(F32) + b.astype(F32)).astype(BF16))
        backs.append(exchange(pieces[c], "rows", 1))
        for group in PLAN[c]:
            work = []
            for mine, k in group:
                source, offset = places[k]
                if mine:
                    work.append((True, begins[k], 0, start_mine, mines[k], pieces[k]))
                else:
                    work.append((False, begins[k], offset, start_theirs, others[source], backs[k]))
            results = final(side, scale, x0, dual, z, work, results, blocks_count)
    new_z, new_u = results
    return (new_x[None], new_z, new_u[None])


def solution(mesh):
    in_specs = (
        P("rows", "feat"),
        P(None, "rows"),
        P("rows", None, "feat"),
        P("rows", None, "feat"),
        P(None, "feat"),
        P(),
        P(),
        P(),
    )
    out_specs = (P("rows", None, "feat"), P(None, "feat"), P("rows", None, "feat"))
    return jax.shard_map(
        per_device, mesh=mesh, in_specs=in_specs, out_specs=out_specs, check_vma=False
    )
```

```python
import functools
import math

import jax
import jax.numpy as jnp
from jax import lax
from jax.experimental import pallas as pl
from jax.experimental.pallas import tpu as pltpu
from jax.sharding import PartitionSpec as P

BF16 = jnp.bfloat16
F32 = jnp.float32
PLAN = ((((True, 0),),), (((False, 0), (True, 1)),), (((False, 1), (True, 2)), ((False, 2),)))
MINE = (3, 3, 2)
OTHER = (3, 5)
STEP = 512
WIDE = 2048
AHEAD = 8
NARROW = 256
WAIT_BYTES = 10_000_000
GRAM_ORDER = (0, 1, 2)
HBM = pl.BlockSpec(memory_space=pltpu.HBM)
VMEM = pl.BlockSpec(memory_space=pltpu.VMEM)
SMEM = pl.BlockSpec(memory_space=pltpu.SMEM)


def exchange(value, axis, mask):
    n = lax.axis_size(axis)
    return lax.ppermute(value, axis, [(i, i ^ mask) for i in range(n)])


def doubling(value, axis, first=1):
    n = lax.axis_size(axis)
    mask = first
    other = exchange(value, axis, mask)
    while 2 * mask < n:
        mask *= 2
        value = (value.astype(F32) + other.astype(F32)).astype(value.dtype)
        other = exchange(value, axis, mask)
    return value, other


def square_sum(value, axis):
    n = lax.axis_size(axis)
    terms = [value]
    mask = 1
    while mask < n:
        if len(terms) > 1:
            terms = [sum(t.astype(F32) for t in terms).astype(value.dtype)]
        steps = [mask, 2 * mask, 3 * mask] if 2 * mask < n else [mask]
        terms += [exchange(terms[0], axis, step) for step in steps]
        mask *= 4
    return terms


def nt(a, b):
    return lax.dot_general(a, b, (((1,), (1,)), ((), ())), preferred_element_type=F32)


def call(kernel, name, in_specs, out_shape, out_specs, scratch=(), aliases=None, limit=16, work=1000):
    return pl.pallas_call(
        kernel,
        in_specs=in_specs,
        out_shape=out_shape,
        out_specs=out_specs,
        scratch_shapes=list(scratch),
        input_output_aliases=aliases or {},
        compiler_params=pltpu.CompilerParams(vmem_limit_bytes=limit * 1024 * 1024),
        cost_estimate=pl.CostEstimate(flops=1000, bytes_accessed=work, transcendentals=0),
        name=name,
    )


def pin(space, *values):
    return [pltpu.with_memory_space_constraint(v, space) for v in values]


def columns(start, size):
    return pl.ds(pl.multiple_of(start, 128), size)


def load_kernel(blocks_count, side, x_hbm, u_hbm, z_hbm, a_hbm, sign_hbm, eta_hbm, rho_hbm, lam_hbm, *refs):
    outs, (eta_row, rho_row, lam_row, both, acc, sems) = refs[:10], refs[10:]
    m_out, pulled_out, a_out, x_out, u_out, z_out, sign_out, scale, mine_out, other_out = outs
    tasks, width = x_hbm.shape
    steps = width // STEP
    rows = ((eta_hbm, eta_row), (rho_hbm, rho_row), (lam_hbm, lam_row), (sign_hbm, sign_out))
    small = [pltpu.make_async_copy(a, b, sems.at[4, k]) for k, (a, b) in enumerate(rows)]

    def chunk(j):
        at = columns(j * STEP, STEP)
        pairs = ((x_hbm, x_out), (u_hbm, u_out), (z_hbm, z_out), (a_hbm, a_out))
        return [pltpu.make_async_copy(a.at[:, at], b.at[:, at], sems.at[k, j]) for k, (a, b) in enumerate(pairs)]

    def begin(j):
        for copy in chunk(j):
            copy.start()

    for copy in small[:3]:
        copy.start()
    for j in range(min(AHEAD, steps)):
        begin(j)
    for copy in small[:3]:
        copy.wait()
    one = lax.broadcasted_iota(jnp.int32, (tasks, tasks), 0) == lax.broadcasted_iota(jnp.int32, (tasks, tasks), 1)
    eta, rho, lam = eta_row[...], rho_row[...], lam_row[...]
    for k, row in enumerate((eta, eta * rho, lam / (rho * blocks_count))):
        upright = jnp.where(one, jnp.broadcast_to(row, (tasks, tasks)), 0.0)
        scale[:, k : k + 1] = jnp.sum(upright, axis=1, keepdims=True)
    acc[...] = jnp.zeros_like(acc)

    @pl.loop(0, steps)
    def _(j):
        for copy in chunk(j):
            copy.wait()

        @pl.when(j + AHEAD < steps)
        def _():
            begin(j + AHEAD)

        @pl.when(j == max(steps - AHEAD, 0))
        def _():
            small[3].start()

        pull = scale[:, 1:2]
        for k in range(0, STEP, NARROW):
            at, here = columns(j * STEP + k, NARROW), pl.ds(k, NARROW)
            x = x_out[:, at]
            v = x - pull * (x - z_out[:, at] + u_out[:, at])
            both[:tasks, here] = x.astype(BF16)
            both[tasks:, here] = v.astype(BF16)
        acc[...] += nt(both[...], a_out[:, columns(j * STEP, STEP)])

    m_out[...] = acc[:tasks].astype(BF16)
    pulled_out[...] = acc[tasks:]
    half = width // 2
    mine = columns(side[0] * half, half)
    other = columns((1 - side[0]) * half, half)
    mine_out[...] = x_out[:, mine] + u_out[:, mine]
    other_out[...] = x_out[:, other] + u_out[:, other]
    small[3].wait()


def load(side, x, u, z, design, sign, step_size, rho, penalty, blocks_count):
    tasks, width = x.shape
    samples = design.shape[0]
    full = pltpu.VMEM((tasks, width), F32)
    half = pltpu.VMEM((tasks, width // 2), F32)
    rows = [v.reshape(1, tasks) for v in (step_size, rho, penalty)]
    return call(
        functools.partial(load_kernel, blocks_count),
        "load_and_margins",
        [SMEM] + [HBM] * 8,
        (
            pltpu.VMEM((tasks, samples), BF16), pltpu.VMEM((tasks, samples), F32), pltpu.VMEM(design.shape, BF16),
            full, full, full, pltpu.VMEM(sign.shape, jnp.int32), pltpu.VMEM((tasks, 128), F32), half, half,
        ),
        [VMEM] * 10,
        [pltpu.VMEM((1, tasks), F32)] * 3
        + [
            pltpu.VMEM((2 * tasks, STEP), BF16), pltpu.VMEM((2 * tasks, samples), F32),
            pltpu.SemaphoreType.DMA((5, max(width // STEP, 4))),
        ],
    )(side, *pin(pltpu.HBM, x, u, z, design, sign, *rows))


def gram_block(a_ref, row, cols, size, acc, high, low):
    width = a_ref.shape[1]
    wide = math.gcd(WIDE, width)
    for j in range(width // wide):
        at = pl.ds(j * wide, wide)
        product = nt(a_ref[pl.ds(row, size), at], a_ref[pl.ds(0, cols), at])
        acc[:, :cols] = product if j == 0 else acc[:, :cols] + product
    whole = acc[:, :cols]
    top = whole.astype(BF16)
    high[...] = top
    low[...] = (whole - top.astype(F32)).astype(BF16)


def gram_kernel(row, token, a_ref, high, low, acc):
    size = high.shape[0]
    gram_block(a_ref, row * size, (row + 1) * size, size, acc, high, low)


def gram_row(row, token, design):
    samples = design.shape[0]
    size = samples // 3
    out = pltpu.VMEM((size, (row + 1) * size), BF16)
    return call(
        functools.partial(gram_kernel, row),
        "gram",
        [SMEM, VMEM],
        (out, out),
        [VMEM] * 2,
        [pltpu.VMEM((size, (row + 1) * size), F32)],
        work=WAIT_BYTES * (row + 1) // 3,
    )(token, *pin(pltpu.VMEM, design))


def residual(sign, *terms):
    margin = sum(t.astype(F32) for t in terms)
    sign = sign.astype(F32)
    return (sign * jax.nn.sigmoid(-sign * margin)).astype(BF16)


def turn_kernel(sign, scale, pulled, *refs):
    *terms, resid, out = refs[6:]
    grams = refs[:6]
    size = grams[0].shape[0]
    resid[...] = residual(sign[...], *(t[...] for t in terms))
    eta = scale[:, 0:1]
    r = [resid[:, pl.ds(k * size, size)] for k in range(3)]
    for col in range(3):
        total = jnp.zeros((resid.shape[0], size), F32)
        for row in range(3):
            for part in range(2):
                if row >= col:
                    block = grams[2 * row + part][:, pl.ds(col * size, size)]
                    total += jnp.dot(r[row], block, preferred_element_type=F32)
                else:
                    total += nt(r[row], grams[2 * col + part][:, pl.ds(row * size, size)])
        here = pl.ds(col * size, size)
        out[:, here] = (pulled[:, here] + eta * total).astype(BF16)


def turn(sign, terms, scale, pulled, grams):
    tasks, samples = pulled.shape
    out = pltpu.VMEM((tasks, samples), BF16)
    args = [sign, scale, pulled, *grams, *terms]
    return call(turn_kernel, "turn", [VMEM] * len(args), (out, out), [VMEM] * 2)(*pin(pltpu.VMEM, *args))


def push_kernel(first, mine, begin, offset, size, side, *refs):
    tasks = refs[0].shape[0]
    if first:
        scale, a_ref, resid1, sign, *terms, h_out, sent_out, resid = refs
        resid[:tasks] = resid1[...]
        resid[tasks:] = residual(sign[...], *(t[...] for t in terms))
    else:
        scale, a_ref, resid, *received, h_out, sent_out = refs
    half = a_ref.shape[1] // 2
    eta = scale[:, 0:1]
    keep = 1.0 - scale[:, 1:2]
    base = (side[0] if mine else 1 - side[0]) * half + begin
    step = math.gcd(512, size)
    for j in range(size // step):
        at = columns(base + j * step, step)
        here = pl.ds(j * step, step)
        grads = jnp.dot(resid[...], a_ref[:, at], preferred_element_type=F32)
        push = eta * (keep * grads[:tasks] + grads[tasks:])
        h_out[:, here] = push
        if mine:
            push = push + received[0][:, pl.ds(offset + j * step, step)].astype(F32)
        sent_out[:, here] = push.astype(BF16)


def push(side, resid, scale, design, received, begin, offset, size):
    tasks = scale.shape[0]
    mine = received is not None
    first = isinstance(resid, tuple)
    args = [scale, design, *(resid if first else [resid])] + ([received] if mine else [])
    out = [pltpu.VMEM((tasks, size), F32), pltpu.VMEM((tasks, size), BF16)]
    if first:
        out.append(pltpu.VMEM((2 * tasks, design.shape[0]), BF16))
    return call(
        functools.partial(push_kernel, first, mine, begin, offset, size),
        "push_mine" if mine else "push_other",
        [SMEM] + [VMEM] * len(args),
        tuple(out),
        [VMEM] * len(out),
    )(side, *pin(pltpu.VMEM, *args))


def store_kernel(side, scale, x_ref, u_ref, z_ref, *rest):
    *hs, x_out, stage, sems = rest
    half = x_ref.shape[1] // 2
    keep = 1.0 - scale[:, 1:2]
    copies = []
    done = 0
    for c, h_ref in enumerate(hs):
        size = h_ref.shape[1]
        base = (side[0] if done < half else 1 - side[0]) * half + done % half
        done += size
        for j in range(0, size, NARROW):
            at = columns(base + j, NARROW)
            u, z = u_ref[:, at], z_ref[:, at]
            stage[:, at] = z - u + keep * keep * (x_ref[:, at] - z + u) + h_ref[:, pl.ds(j, NARROW)]
        at = columns(base, size)
        copy = pltpu.make_async_copy(stage.at[:, at], x_out.at[:, at], sems.at[c])
        copy.start()
        copies.append(copy)
    for copy in copies:
        copy.wait()


def store_x(side, scale, x, u, z, mines, others):
    tasks, width = x.shape
    args = [scale, x, u, z, *mines, *others]
    return call(
        store_kernel,
        "store_x",
        [SMEM] + [VMEM] * len(args),
        pltpu.HBM((tasks, width), F32),
        HBM,
        [pltpu.VMEM((tasks, width), F32), pltpu.SemaphoreType.DMA((len(mines) + len(others),))],
    )(side, *pin(pltpu.VMEM, *args))


def final_kernel(blocks_count, pieces, buffered, side, scale, x_ref, u_ref, z_ref, *refs):
    outs = refs[3 * len(pieces) + 2 * buffered :][:2]
    stage, sems = refs[-2:]
    half = x_ref.shape[1] // 2
    pull, limit = scale[:, 1:2], scale[:, 2:3]
    keep = 1.0 - pull
    copies, filled = [], 0
    for k, (mine, begin, offset, size) in enumerate(pieces):
        start, h, pushed = refs[3 * k : 3 * k + 3]
        base = (side[0] if mine else 1 - side[0]) * half + begin
        for j in range(0, size, NARROW):
            cut, here = columns(base + j, NARROW), pl.ds(filled + j, NARROW)
            z = z_ref[:, cut]
            total = keep * keep * start[:, pl.ds(begin + j, NARROW)] + pushed[:, pl.ds(j, NARROW)].astype(F32)
            mean = total * (1.0 / blocks_count) + pull * (1.0 + keep) * z
            new_z = mean - jnp.clip(mean, -limit, limit)
            moved = z + keep * keep * (x_ref[:, cut] - z + u_ref[:, cut]) + h[:, pl.ds(offset + j, NARROW)]
            stage[0, :, here] = new_z
            stage[1, :, here] = moved - new_z
        cut, here = columns(base, size), pl.ds(filled, size)
        for o in range(2):
            copy = pltpu.make_async_copy(stage.at[o, :, here], outs[o].at[:, cut], sems.at[k, o])
            copy.start()
            copies.append(copy)
        filled += size
    for copy in copies:
        copy.wait()


def final(side, scale, x, u, z, pieces, buffers, blocks_count):
    tasks, width = x.shape
    buffered = buffers is not None
    args = pin(pltpu.VMEM, scale, x, u, z, *(v for piece in pieces for v in piece[3:]))
    vmem = len(args)
    places = [(*piece[:3], piece[5].shape[1]) for piece in pieces]
    out = pltpu.HBM((tasks, width), F32)
    aliases = {}
    if buffered:
        aliases = {1 + vmem + o: o for o in range(2)}
        args += pin(pltpu.HBM, *buffers)
    return call(
        functools.partial(final_kernel, blocks_count, places, buffered),
        "final",
        [SMEM] + [VMEM] * vmem + [HBM] * (2 * buffered),
        (out, out),
        [HBM] * 2,
        [pltpu.VMEM((2, tasks, sum(p[3] for p in places)), F32), pltpu.SemaphoreType.DMA((len(pieces), 2))],
        aliases,
    )(side, *args)


def tie(value, *after):
    return lax.optimization_barrier((value, after))[0]


def per_device(design, labels, local_x, dual_u, consensus_z, step_size, rho, penalty):
    tasks, width = consensus_z.shape
    half = width // 2
    blocks_count = lax.axis_size("rows")
    side = (lax.axis_index("rows") & 1).astype(jnp.int32)[None]

    margin1, pulled, design, x0, dual, z, sign, scale, start_mine, start_other = load(
        side, local_x[0], dual_u[0], consensus_z, design, labels, step_size, rho, penalty, blocks_count
    )
    start_mine = start_mine + exchange(start_other, "rows", 1)

    terms, grams = [margin1], []
    for step in range(max(lax.axis_size("feat").bit_length() - 1, 3)):
        more = (1 << step) < lax.axis_size("feat")
        if step > 0 and more:
            terms = [sum(t.astype(F32) for t in terms).astype(BF16)]
        row = gram_row(GRAM_ORDER[step], tie(side, terms[0]), design) if step < 3 else []
        grams.append(row)
        if more:
            got = exchange(terms[0], "feat", 1 << step)
            terms.append(tie(got, row[0], start_mine) if step == 0 else tie(got, row[0]) if step == 1 else got)

    resid1, margin2 = turn(sign, terms, scale, pulled, [g for row in range(3) for g in grams[GRAM_ORDER.index(row)]])
    terms = square_sum(margin2, "feat")
    mask = 2
    while mask < blocks_count:
        start_mine = start_mine + exchange(start_mine, "rows", mask)
        mask *= 2
    terms = tie(terms, start_mine)
    sizes = [half * part // sum(MINE) for part in MINE]
    begins = [sum(sizes[:c]) for c in range(len(sizes))]
    other_sizes = [half * part // sum(OTHER) for part in OTHER]
    other_begins = [sum(other_sizes[:c]) for c in range(len(other_sizes))]
    count = len(sizes)
    others, received = [], []
    resid = (resid1, sign, *terms)
    for begin, size in zip(other_begins, other_sizes):
        value, other, *made = push(side, resid, scale, design, None, begin, 0, size)
        resid = made[0] if made else resid
        others.append(value)
        received.append(exchange(other, "rows", 1))
    mines, sums, places = [], [], []
    token = tie(side, others[-1])
    for begin, size in zip(begins, sizes):
        source = max(k for k, b in enumerate(other_begins) if b <= begin)
        places.append((source, begin - other_begins[source]))
        value, sent = push(token, resid, scale, design, received[source], begin, places[-1][1], size)
        mines.append(value)
        sums.append(doubling(sent, "rows", 2))
        token = tie(side, sent)
    new_x = store_x(side, scale, x0, dual, z, mines, others)

    start_theirs = exchange(tie(start_mine, mines[0]), "rows", 1)

    pieces, backs, results = [], [], None
    for c, (a, b) in enumerate(sums):
        b = tie(b, new_x, results)
        pieces.append((a.astype(F32) + b.astype(F32)).astype(BF16))
        backs.append(exchange(pieces[c], "rows", 1))
        for group in PLAN[c]:
            work = []
            for mine, k in group:
                source, offset = places[k]
                if mine:
                    work.append((True, begins[k], 0, start_mine, mines[k], pieces[k]))
                else:
                    work.append((False, begins[k], offset, start_theirs, others[source], backs[k]))
            results = final(side, scale, x0, dual, z, work, results, blocks_count)
    new_z, new_u = results
    return (new_x[None], new_z, new_u[None])


def solution(mesh):
    in_specs = (
        P("rows", "feat"),
        P(None, "rows"),
        P("rows", None, "feat"),
        P("rows", None, "feat"),
        P(None, "feat"),
        P(),
        P(),
        P(),
    )
    out_specs = (P("rows", None, "feat"), P(None, "feat"), P("rows", None, "feat"))
    return jax.shard_map(
        per_device, mesh=mesh, in_specs=in_specs, out_specs=out_specs, check_vma=False
    )
```
